128 devices in a mesh: region: 64 (over y, x_hi, z, core), coord: 2 (over x_lo).
Axes of the slice: x: 4 (x_hi: 2, x_lo: 2; x = x_hi * 2 + x_lo), y: 4, z: 4, core: 2. Of those that a mesh axis runs over, the one named last changes fastest.
Arguments:
- right_side: float32 [2, 262144], P(None, ('region', 'coord')), may hold values from -6 to 6
- anchor: float32 [262144], P(('region', 'coord')), may hold values from 0.5 to 2
- blocks: float32 [2048, 2, 128, 128], P(('region', 'coord')), may hold values from 2.734375e-05 to 0.02734375
- tile_nbr: int32 [2048, 2], P(('region', 'coord')), may hold values from 0 to 31
- cut_cells: int32 [128, 128, 128], P(('region', 'coord')), may hold values from 0 to 2047
- cut_weight: float32 [128, 128, 128], P(('region', 'coord')), may hold values from 0 to 1, as said below
- pin_cell: int32 [524288], P(('region', 'coord')), may hold values from 0 to 2047
- pin_net: int32 [524288], P(('region', 'coord')), may hold values from 0 to 16383, as said below
- star_weight: float32 [16384], replicated, may hold values from 0.2 to 2
Outputs:
- positions: float32 [2, 262144], P(None, ('region', 'coord'))
- residual: float32 [2, 262144], P(None, ('region', 'coord'))
The draws below stay inside these ranges and needn't reach their ends.
Inputs may be any that keep to these rules, and one draw needn't show every extreme that they name: cut_weight[d, p, s] equals cut_weight[p, d, s], and it is 0 where p equals d. Every net number appears exactly 32 times; net n is owned by partition n // 128, and pin_net[d * 4096 + o * 32 + s] is a net owned by partition o for every partition d, owner o and s below 32.
All inputs are finite; a program needn't handle non-finite values.
Results may differ from the reference program's by a relative error of at most 0.00021.
Values sent between devices are 32-bit elements; how exact they have to be, the bound alone decides.
No kernel may reach another device: no remote copies, remote signals or barrier semaphores. Data moves between devices by JAX's collectives and lax.ppermute only.
A program may use at most 128 MiB of HBM per device.

```python
import math
import jax
import jax.numpy as jnp
from jax import lax

TILE = 128
TILES = 16
NB = 2
CUT = 128
NETS_DEV = 128
FANOUT = 32
ITERS = 3
PARTITIONS = 128
TILES_ALL = 2048
CELLS = 262144
NETS = 16384
PINS_DEV = 4096
PINS = 524288
N_REGION = 64
N_COORD = 2


def draw_right_side(key, part):
    region = jnp.arange(CELLS, dtype=jnp.int32) // (TILES * TILE)
    fraction = region.astype(jnp.float32) / max(PARTITIONS - 1, 1)
    spread = 0.6 * jnp.exp(fraction * jnp.log(3.0))
    values = jax.random.normal(key, (2, CELLS)) * spread
    return jnp.clip(values, -6.0, 6.0)


def draw_cut_weight(key, part):
    dims = (PARTITIONS, PARTITIONS, CUT)
    drawn = jnp.exp(jax.random.uniform(key, dims, minval=jnp.log(0.1), maxval=0.0))
    blended = 0.5 * (drawn + jnp.swapaxes(drawn, 0, 1))
    diagonal_pair = jnp.arange(PARTITIONS)[:, None] == jnp.arange(PARTITIONS)[None, :]
    return jnp.where(diagonal_pair[:, :, None], 0.0, blended)


def draw_pin_net(key, part):
    per_owner = NETS_DEV * FANOUT
    slot_count = per_owner // PARTITIONS
    labels = jnp.arange(per_owner, dtype=jnp.int32) // FANOUT
    owner_keys = jax.random.split(key, PARTITIONS)
    shuffled = jax.vmap(lambda owner_key: jax.random.permutation(owner_key, labels))(owner_keys)
    nets = shuffled + (jnp.arange(PARTITIONS, dtype=jnp.int32) * NETS_DEV)[:, None]
    blocked = nets.reshape(PARTITIONS, PARTITIONS, slot_count)
    return jnp.transpose(blocked, (1, 0, 2)).reshape(-1)


def plant(result, stream_key, smallest, top_value):
    place = [jax.random.randint(jax.random.fold_in(stream_key, axis), (), 0, length) for axis, length in enumerate(result.shape)]
    longest = result.shape.index(max(result.shape))
    next_to = place[:longest] + [(place[longest] + 1) % result.shape[longest]] + place[longest + 1:]
    return result.at[tuple(place)].set(smallest).at[tuple(next_to)].set(top_value)


def block_levels(rng, extent, pieces, smallest, top_value):
    def one(dim, shards_of):
        heights = jax.random.uniform(jax.random.fold_in(jax.random.fold_in(rng, 6), dim), (shards_of,), jnp.float32, smallest / len(pieces), top_value / len(pieces))
        return jnp.repeat(jnp.exp(heights), extent[dim] // shards_of).reshape((-1,) + (1,) * (len(extent) - dim - 1))

    loudness = one(*pieces[0])
    for cut in pieces[1:]:
        loudness = loudness * one(*cut)
    return loudness


def setup_inputs(seed: int = 0) -> dict:
    arg_keys = jax.random.split(jax.random.key(seed), 10)
    return {
        "right_side": draw_right_side(jax.random.fold_in(arg_keys[9], 71), 0),
        "anchor": jnp.clip(0.5 + 1.5 * jax.random.uniform(arg_keys[1], (CELLS,), jnp.float32) ** block_levels(arg_keys[1], (CELLS,), ((0, 128),), -0.2, 0.2), 0.5, 2.0),
        "blocks": jnp.clip(jnp.exp(math.log(0.02734375) - 6.9077552 * jax.random.uniform(arg_keys[2], (TILES_ALL, NB, TILE, TILE), jnp.float32) ** block_levels(arg_keys[2], (TILES_ALL, NB, TILE, TILE), ((0, 128),), -0.2, 0.2)), 2.7343750844011083e-05, 0.02734375),
        "tile_nbr": plant(jax.random.randint(arg_keys[3], (TILES_ALL, NB), 0, N_COORD * TILES), jax.random.fold_in(arg_keys[3], 1), 0, (N_COORD * TILES) - 1).astype(jnp.int32),
        "cut_cells": plant(jax.random.randint(arg_keys[4], (PARTITIONS, PARTITIONS, CUT), 0, TILES * TILE), jax.random.fold_in(arg_keys[4], 1), 0, (TILES * TILE) - 1).astype(jnp.int32),
        "cut_weight": draw_cut_weight(jax.random.fold_in(arg_keys[9], 71), 0),
        "pin_cell": plant(jax.random.randint(arg_keys[6], (PINS,), 0, TILES * TILE), jax.random.fold_in(arg_keys[6], 1), 0, (TILES * TILE) - 1).astype(jnp.int32),
        "pin_net": draw_pin_net(jax.random.fold_in(arg_keys[9], 71), 0),
        "star_weight": jnp.clip(jnp.exp(jax.random.uniform(arg_keys[8], (NETS,), jnp.float32, math.log(0.2), math.log(2.0))), 0.2, 2.0),
    }


exact_prec = lax.Precision.HIGHEST


def region_apply(inputs):
    region_blocks, neighbours, vectors = inputs
    forward = jnp.einsum("tkij,ctkj->cti", region_blocks, vectors[:, neighbours], precision=exact_prec)
    backward = jnp.einsum("tkij,cti->ctkj", region_blocks, vectors, precision=exact_prec)
    flat_back = backward.reshape(vectors.shape[0], -1, vectors.shape[2])
    spread = jnp.zeros_like(vectors).at[:, neighbours.reshape(-1)].add(flat_back)
    return forward + spread


def region_degree(inputs):
    region_blocks, neighbours = inputs
    row_sums = jnp.sum(region_blocks, axis=(1, 3))
    col_sums = jnp.sum(region_blocks, axis=2).reshape(-1, region_blocks.shape[3])
    return row_sums + jnp.zeros_like(row_sums).at[neighbours.reshape(-1)].add(col_sums)


def reference(right_side, anchor, blocks, tile_nbr, cut_cells, cut_weight, pin_cell, pin_net, star_weight):
    region_tiles = N_COORD * TILES
    cells_dev = TILES * TILE
    region_blocks = blocks.reshape(N_REGION, region_tiles, NB, TILE, TILE)
    neighbours = tile_nbr.reshape(N_REGION, region_tiles, NB)
    degree = lax.map(region_degree, (region_blocks, neighbours)).reshape(-1)
    offsets = jnp.arange(PARTITIONS, dtype=jnp.int32) * cells_dev
    own_cells = (cut_cells + offsets[:, None, None]).reshape(-1)
    peer_cells = (jnp.swapaxes(cut_cells, 0, 1) + offsets[None, :, None]).reshape(-1)
    link_weights = cut_weight.reshape(-1)
    pin_owner = jnp.arange(PINS, dtype=jnp.int32) // PINS_DEV
    pin_global = pin_cell + pin_owner * cells_dev
    pin_weight = star_weight[pin_net]
    degree = degree + jnp.zeros((CELLS,), jnp.float32).at[own_cells].add(link_weights)
    degree = degree + jnp.zeros((CELLS,), jnp.float32).at[pin_global].add(pin_weight)
    degree = degree + anchor

    def operate(vectors):
        by_region = jnp.transpose(vectors.reshape(2, N_REGION, region_tiles, TILE), (1, 0, 2, 3))
        local_part = lax.map(region_apply, (region_blocks, neighbours, by_region))
        local_part = jnp.transpose(local_part, (1, 0, 2, 3)).reshape(2, CELLS)
        cut_part = jnp.zeros((2, CELLS), jnp.float32).at[:, own_cells].add(link_weights * vectors[:, peer_cells])
        totals = jnp.zeros((2, NETS), jnp.float32).at[:, pin_net].add(vectors[:, pin_global])
        centre = totals / FANOUT
        star_part = jnp.zeros((2, CELLS), jnp.float32).at[:, pin_global].add(pin_weight * centre[:, pin_net])
        return degree * vectors - local_part - cut_part - star_part

    positions = jnp.zeros_like(right_side)
    residual = right_side
    direction = right_side
    norm_now = jnp.sum(residual * residual, axis=1, keepdims=True)
    for iteration in range(ITERS):
        applied = operate(direction)
        step_size = norm_now / jnp.sum(direction * applied, axis=1, keepdims=True)
        positions = positions + step_size * direction
        residual = residual - step_size * applied
        norm_next = jnp.sum(residual * residual, axis=1, keepdims=True)
        direction = residual + (norm_next / norm_now) * direction
        norm_now = norm_next
    return positions, residual
```

```python
import functools

import jax
import jax.numpy as jnp
from jax import lax
from jax.experimental import pallas as pl
from jax.experimental.pallas import tpu as pltpu
from jax.sharding import PartitionSpec as P

FANOUT = 32
ITERS = 3
AXES = ("region", "coord")
LANES = 128
TILES = 16
F32 = jnp.float32
BF16 = jnp.bfloat16
I32 = jnp.int32
SUM_LANE = 96


def iota(shape, axis):
    return lax.broadcasted_iota(I32, shape, axis)


def split2(x):
    high = x.astype(BF16).astype(F32)
    return [high, (x - high).astype(BF16).astype(F32)]


def split3(x):
    high = x.astype(BF16).astype(F32)
    return [high] + split2(x - high)


def dot_nt(a, b):
    return lax.dot_general(a, b, (((1,), (1,)), ((), ())), preferred_element_type=F32)


def dot_nn(a, b):
    return lax.dot_general(a, b, (((1,), (0,)), ((), ())), preferred_element_type=F32)


def roll(x, shift):
    shift = shift % LANES
    return x if shift == 0 else pltpu.roll(x, shift, 1)


def total(x):
    return jnp.sum(jnp.sum(x, axis=0, keepdims=True), axis=1, keepdims=True)


def lane_value(row, lane):
    return jnp.sum(jnp.where(iota(row.shape, 1) == lane, row, 0.0), axis=1, keepdims=True)


def pick(tables, cells):
    low = cells & (LANES - 1)
    high = cells >> 7
    rows = [jnp.zeros(cells.shape, F32) for _ in tables]
    for tile in range(TILES):
        here = high == tile
        for v, table in enumerate(tables):
            wide = jnp.broadcast_to(table[tile], cells.shape)
            got = jnp.take_along_axis(wide, low, axis=1, mode="promise_in_bounds")
            rows[v] = jnp.where(here, got, rows[v])
    return rows


def one_hot(row, count):
    return jnp.where(iota((count, LANES), 0) == row, 1.0, 0.0).astype(BF16)


def add_rows(row_count, cell_row, value_rows):
    acc = None
    for j in range(0, row_count, 2):
        hots, masked = [], []
        for i in (j, j + 1):
            cells = cell_row(i)
            hots.append(one_hot(cells & (LANES - 1), LANES))
            here = iota((TILES, LANES), 0) == (cells >> 7)
            masked.append(
                jnp.concatenate([jnp.where(here, v, 0.0) for v in value_rows(i)], axis=0).astype(BF16)
            )
        part = dot_nt(jnp.concatenate(masked, axis=1), jnp.concatenate(hots, axis=1))
        acc = part if acc is None else acc + part
    return acc


def fold(acc, vectors, parts):
    size = vectors * TILES
    return sum(acc[i * size : (i + 1) * size] for i in range(parts))


def put_gathered(vectors, sums, cut_cells, pin_cell, pin_net, out_ref):
    lane = iota((32, LANES), 1)
    tail = jnp.zeros((1, LANES), F32)
    for i, s in enumerate(sums):
        tail = jnp.where(iota((1, LANES), 1) == SUM_LANE + i, s, tail)
    gx, gy = pick(vectors, pin_cell[...])
    net = (pin_net[...] & (LANES - 1)).astype(F32)
    for q in range(4):
        row = jnp.where(
            lane < 32,
            roll(gx, -32 * q),
            jnp.where(
                lane < 64,
                roll(gy, 32 - 32 * q),
                jnp.where(lane < 96, roll(net, 64 - 32 * q), tail),
            ),
        )
        out_ref[pl.ds(4 * q + 2, 32, stride=16), :] = row
        out_ref[pl.ds(4 * q + 3, 32, stride=16), :] = jnp.zeros((32, LANES), F32)
    for g in range(16):
        gx, gy = pick(vectors, cut_cells[pl.ds(8 * g, 8), :])
        out_ref[pl.ds(32 * g, 8, stride=4), :] = gx
        out_ref[pl.ds(32 * g + 1, 8, stride=4), :] = gy


def dense(rows, offset):
    lane = iota((32, LANES), 1)
    out = roll(rows[0], -offset)
    for q in range(1, 4):
        out = jnp.where(lane >= 32 * q, roll(rows[q], 32 * q - offset), out)
    return out


def first_kernel(right_ref, cut_cells, pin_cell, pin_net, send_ref, start_ref):
    tables = [
        [right_ref[v : v + 1, LANES * t : LANES * (t + 1)] for t in range(TILES)] for v in range(2)
    ]
    for v in range(2):
        for t in range(TILES):
            start_ref[TILES * v + t : TILES * v + t + 1, :] = tables[v][t]
    r = start_ref[...]
    sums = [total(r[16 * v : 16 * v + 16] * r[16 * v : 16 * v + 16]) for v in range(2)]
    put_gathered(tables, sums, cut_cells, pin_cell, pin_net, send_ref)


def degree_kernel(cut_cells, cut_weight, pin_cell, pin_net, star, anchor, out_ref, rows_ref, pins_ref):
    lane = iota((32, LANES), 1)
    net = pin_net[...] & (LANES - 1)
    for q in range(4):
        got = jnp.take_along_axis(
            star[pl.ds(q, 32, stride=4), :], roll(net, -32 * q), axis=1, mode="promise_in_bounds"
        )
        rows_ref[pl.ds(32 * q, 32), :] = got
    weight = dense([rows_ref[pl.ds(32 * q, 32), :] for q in range(4)], 0)
    for i, part in enumerate(split3(weight)):
        pins_ref[pl.ds(32 * i, 32), :] = part
    acc = add_rows(
        32,
        lambda j: pin_cell[j : j + 1, :],
        lambda j: [pins_ref[32 * i + j : 32 * i + j + 1, :] for i in range(3)],
    )
    acc = acc + add_rows(
        128,
        lambda j: cut_cells[j : j + 1, :],
        lambda j: split3(cut_weight[j : j + 1, :]),
    )
    out_ref[...] = anchor[...] + fold(acc, 1, 3)


def block_kernel(first, place, nbr_row, nbr_col, blocks, own_ref, peer_ref, local_ref, forward_ref, back_ref, near, far, got_f, got_b):
    vectors = 3 if first else 2
    me = place[0]
    pick_rows = jnp.where(iota((32, 32), 1) == nbr_col[...], 1.0, 0.0).astype(BF16)
    spread_rows = jnp.where(iota((32, 32), 0) == nbr_row[...], 1.0, 0.0).astype(BF16)
    own, peer = own_ref[...], peer_ref[...]
    upper = me == 1
    near[...] = jnp.ones(near.shape, F32)
    far[...] = jnp.ones(far.shape, F32)
    for v in range(2):
        o, p = own[16 * v : 16 * v + 16], peer[16 * v : 16 * v + 16]
        whole = jnp.concatenate([jnp.where(upper, p, o), jnp.where(upper, o, p)], axis=0)
        for i, (mine, part) in enumerate(zip(split2(o), split2(whole))):
            near[pl.ds(2 * i + v, 16, stride=8), :] = mine
            picked = dot_nn(pick_rows, part.astype(BF16))
            for k in range(2):
                far[pl.ds(128 * k + 2 * i + v, 16, stride=8), :] = picked[16 * k : 16 * k + 16]
    for t in range(TILES):
        pair = jnp.concatenate([blocks[t, 0], blocks[t, 1]], axis=1)
        high = pair.astype(BF16)
        low = (pair - high.astype(F32)).astype(BF16)
        a = near[8 * t : 8 * t + 8, :].astype(BF16)
        b = jnp.concatenate(
            [far[128 * k + 8 * t : 128 * k + 8 * t + 8, :] for k in range(2)], axis=1
        ).astype(BF16)
        back = dot_nn(a, high) + dot_nn(a, low)
        for k in range(2):
            got_b[128 * k + 8 * t : 128 * k + 8 * t + 8, :] = back[:, LANES * k : LANES * (k + 1)]
        got_f[8 * t : 8 * t + 8, :] = dot_nt(b, high) + dot_nt(b, low)
    for v in range(vectors):
        def take(ref, at):
            if v == 2:
                return ref[pl.ds(at + 4, 16, stride=8), :]
            return ref[pl.ds(at + v, 16, stride=8), :] + ref[pl.ds(at + v + 2, 16, stride=8), :]

        forward = take(got_f, 0)
        backward = jnp.concatenate([take(got_b, 128 * k) for k in range(2)], axis=0)
        spread = sum(dot_nn(spread_rows, part.astype(BF16)) for part in split3(backward))
        lower, higher = spread[:16], spread[16:]
        local_ref[16 * v : 16 * v + 16, :] = forward + jnp.where(upper, higher, lower)
        back_ref[16 * v : 16 * v + 16, :] = jnp.where(upper, lower, higher)
        if v < 2:
            forward_ref[16 * v : 16 * v + 16, :] = forward


def owner_kernel(first, *refs):
    if first:
        (place, sent, got, cut_weight, star, forward_ref, state, parts, local_ref, back_ref,
         out_ref, sums_ref, degree_ref, rows) = refs
        degree = parts[...] + local_ref[32:48, :] + back_ref[32:48, :]
        degree_ref[...] = degree
    else:
        (place, sent, got, cut_weight, star, forward_ref, state, degree_in,
         out_ref, sums_ref, rows) = refs
        degree = degree_in[...]
    pin_rows = [got[pl.ds(4 * q + 2, 32, stride=16), :] for q in range(4)]
    sums = sum(jnp.sum(row, axis=0, keepdims=True) for row in pin_rows)
    sums_ref[...] = jnp.broadcast_to(sums, (8, LANES))
    nets = dense(pin_rows, 64).astype(I32)
    rows[...] = jnp.zeros(rows.shape, F32)
    for v in range(2):
        for i, part in enumerate(split3(dense(pin_rows, 32 * v))):
            rows[pl.ds(2 * i + v, 32, stride=8), :] = part
    acc = None
    for j in range(0, 32, 2):
        hot = jnp.concatenate([one_hot(nets[i : i + 1], LANES) for i in (j, j + 1)], axis=1)
        left = jnp.concatenate([rows[8 * i : 8 * i + 8, :] for i in (j, j + 1)], axis=1)
        part = dot_nt(left.astype(BF16), hot)
        acc = part if acc is None else acc + part
    weight = star[pl.ds(place[1], 1), :] * (1.0 / FANOUT)
    totals = [acc[v : v + 1] + acc[v + 2 : v + 3] + acc[v + 4 : v + 5] for v in range(2)]
    centres = [weight * t for t in totals]
    tail = jnp.zeros((1, LANES), F32)
    for v in range(2):
        r = state[16 * v : 16 * v + 16, :]
        share = r * (degree * r - 2.0 * forward_ref[16 * v : 16 * v + 16, :])
        line = jnp.sum(share, axis=0, keepdims=True) - centres[v] * totals[v]
        cut = cut_weight[...] * (sent[pl.ds(v, 128, stride=4), :] * got[pl.ds(v, 128, stride=4), :])
        line = line - jnp.sum(cut, axis=0, keepdims=True)
        tail = jnp.where(
            iota((1, LANES), 1) == SUM_LANE + v, jnp.sum(line, axis=1, keepdims=True), tail
        )
    lane = iota((8, LANES), 1)
    tables = [jnp.broadcast_to(c, (8, LANES)) for c in centres]
    for g in range(16):
        row = got[pl.ds(32 * g + 2, 8, stride=4), :]
        index = jnp.where(lane < 32, roll(row, -64), roll(row, -32)).astype(I32) & (LANES - 1)
        gx, gy = (
            jnp.take_along_axis(t, index, axis=1, mode="promise_in_bounds") for t in tables
        )
        out_ref[pl.ds(8 * g, 8), :] = jnp.where(
            lane < 32, gx, jnp.where(lane < 64, gy, jnp.where(lane < 96, 0.0, tail))
        )


def cut_kernel(cut_cells, cut_weight, got, local_ref, back_ref, sums_ref, out_ref):
    del sums_ref

    def values(j):
        weight = cut_weight[j : j + 1, :]
        parts = [split2(weight * got[4 * j + v : 4 * j + v + 1, :]) for v in range(2)]
        return [parts[0][0], parts[1][0], parts[0][1], parts[1][1]]

    acc = add_rows(128, lambda j: cut_cells[j : j + 1, :], values)
    out_ref[...] = fold(acc, 2, 2) + local_ref[0:32, :] + back_ref[0:32, :]


def step_kernel(first, last, pin_cell, got, degree_ref, others, sums_ref, *refs):
    refs = list(refs)
    state = refs.pop(0)
    old = None if first else refs.pop(0)
    if last:
        positions_ref, residual_ref, pins = refs
    else:
        cut_cells, pin_net, send_ref, state_ref, old_ref, pins = refs
    pin_rows = [got[pl.ds(q, 32, stride=4), :] for q in range(4)]
    energy = sum(jnp.sum(row, axis=0, keepdims=True) for row in pin_rows)
    for v in range(2):
        for i, part in enumerate(split2(dense(pin_rows, 32 * v))):
            pins[pl.ds(32 * (2 * i + v), 32), :] = part
    acc = add_rows(
        32,
        lambda j: pin_cell[j : j + 1, :],
        lambda j: [pins[32 * i + j : 32 * i + j + 1, :] for i in range(4)],
    )
    removed = fold(acc, 2, 2) + others[...]
    degree = degree_ref[...]
    news, line = [], jnp.zeros((1, LANES), F32)
    lanes = iota((1, LANES), 1)
    sent_sums = [None] * 4
    for v in range(2):
        part = slice(16 * v, 16 * v + 16)
        r = state[part, :]
        z = degree * r - removed[part]
        norm = lane_value(sums_ref[0:1, :], SUM_LANE + v)
        product = lane_value(energy, SUM_LANE + v)
        if first:
            p, q = r, z
        else:
            cross = lane_value(sums_ref[0:1, :], SUM_LANE + 2 + v)
            beta = norm / lane_value(old[0:1, :], v)
            product = product + beta * (2.0 * cross + beta * lane_value(old[0:1, :], 2 + v))
            p = r + beta * state[32 + 16 * v : 48 + 16 * v, :]
            q = z + beta * state[64 + 16 * v : 80 + 16 * v, :]
        step = norm / product
        x = step * p
        if not first:
            x = x + state[96 + 16 * v : 112 + 16 * v, :]
        r = r - step * q
        if last:
            for t in range(TILES):
                positions_ref[v : v + 1, LANES * t : LANES * (t + 1)] = x[t : t + 1]
                residual_ref[v : v + 1, LANES * t : LANES * (t + 1)] = r[t : t + 1]
            continue
        for i, new in enumerate((r, p, q, x)):
            state_ref[32 * i + 16 * v : 32 * i + 16 * v + 16, :] = new
        news.append([r[t : t + 1] for t in range(TILES)])
        sent_sums[v], sent_sums[2 + v] = total(r * r), total(r * q)
        line = jnp.where(lanes == v, norm, jnp.where(lanes == 2 + v, product, line))
    if last:
        return
    old_ref[...] = jnp.broadcast_to(line, (8, LANES))
    put_gathered(news, sent_sums, cut_cells, pin_cell, pin_net, send_ref)


def call(kernel, shapes, scratch, cost, args, smem=0):
    vmem = pl.BlockSpec(memory_space=pltpu.VMEM)
    return pl.pallas_call(
        kernel,
        out_shape=[jax.ShapeDtypeStruct(s, F32) for s in shapes],
        in_specs=[pl.BlockSpec(memory_space=pltpu.SMEM)] * smem + [vmem] * (len(args) - smem),
        out_specs=[vmem] * len(shapes),
        scratch_shapes=[pltpu.VMEM(s, F32) for s in scratch],
        compiler_params=pltpu.CompilerParams(vmem_limit_bytes=32 << 20),
        cost_estimate=pl.CostEstimate(flops=cost, bytes_accessed=1 << 20, transcendentals=0),
    )(*args)


def exchange(rows, height):
    return lax.all_to_all(
        rows.reshape(LANES, height, LANES), AXES, split_axis=0, concat_axis=0, tiled=True
    ).reshape(LANES * height, LANES)


def swap(x):
    return lax.ppermute(x, "coord", [(0, 1), (1, 0)])


def per_device(
    right_side, anchor, blocks, tile_nbr, cut_cells, cut_weight, pin_cell, pin_net, star_weight
):
    cut_cells, cut_weight = cut_cells[0], cut_weight[0]
    pin_cell, pin_net = pin_cell.reshape(32, LANES), pin_net.reshape(32, LANES)
    star, anchor = star_weight.reshape(LANES, LANES), anchor.reshape(TILES, LANES)
    coord = lax.axis_index("coord")
    place = jnp.stack([coord, lax.axis_index("region") * 2 + coord]).astype(I32)
    by_block = tile_nbr.T.reshape(1, 32)
    nbr_row, nbr_col = by_block, by_block.reshape(32, 1)

    send, state = call(
        first_kernel, [(512, LANES), (32, LANES)], [], 1 << 24, (right_side, cut_cells, pin_cell, pin_net)
    )
    parts = call(
        degree_kernel,
        [(16, LANES)],
        [(128, LANES), (96, LANES)],
        1 << 31,
        (cut_cells, cut_weight, pin_cell, pin_net, star, anchor),
    )[0]
    degree = old = None
    for iteration in range(ITERS):
        first, last = iteration == 0, iteration == ITERS - 1
        residual = state[0:32]
        got = exchange(send, 4)
        peer = swap(residual)
        rows = 48 if first else 32
        local_sum, forward, back = call(
            functools.partial(block_kernel, first),
            [(rows, LANES), (32, LANES), (rows, LANES)],
            [(128, LANES), (256, LANES), (128, LANES), (256, LANES)],
            1 << 31,
            (place, nbr_row, nbr_col, blocks, residual, peer),
            smem=1,
        )
        back = swap(back)
        args = (place, send, got, cut_weight, star, forward, state)
        if first:
            out, sums, degree = call(
                functools.partial(owner_kernel, True),
                [(128, LANES), (8, LANES), (16, LANES)],
                [(256, LANES)],
                1 << 26,
                args + (parts, local_sum, back),
                smem=1,
            )
        else:
            out, sums = call(
                functools.partial(owner_kernel, False),
                [(128, LANES), (8, LANES)],
                [(256, LANES)],
                1 << 26,
                args + (degree,),
                smem=1,
            )
        returned = exchange(out, 1)
        others = call(
            cut_kernel, [(32, LANES)], [], 1 << 31, (cut_cells, cut_weight, got, local_sum, back, sums)
        )[0]
        args = (pin_cell, returned, degree, others, sums, state)
        if not first:
            args = args + (old,)
        if last:
            shapes = [(2, TILES * LANES), (2, TILES * LANES)]
        else:
            args = args + (cut_cells, pin_net)
            shapes = [(512, LANES), (128, LANES), (8, LANES)]
        results = call(
            functools.partial(step_kernel, first, last), shapes, [(128, LANES)], 1 << 26, args
        )
        if last:
            return tuple(results)
        send, state, old = results


def solution(mesh):
    return jax.shard_map(
        per_device,
        mesh=mesh,
        in_specs=(
            P(None, AXES),
            P(AXES),
            P(AXES, None, None, None),
            P(AXES, None),
            P(AXES, None, None),
            P(AXES, None, None),
            P(AXES),
            P(AXES),
            P(),
        ),
        out_specs=(P(None, AXES), P(None, AXES)),
        check_vma=False,
    )
```

```python
import functools

import jax
import jax.numpy as jnp
from jax import lax
from jax.experimental import pallas as pl
from jax.experimental.pallas import tpu as pltpu
from jax.sharding import PartitionSpec as P

FANOUT = 32
ITERS = 3
AXES = ("region", "coord")
LANES = 128
TILES = 16
F32 = jnp.float32
BF16 = jnp.bfloat16
I32 = jnp.int32
SUM_LANE = 96


def iota(shape, axis):
    return lax.broadcasted_iota(I32, shape, axis)


def split2(x):
    high = x.astype(BF16).astype(F32)
    return [high, (x - high).astype(BF16).astype(F32)]


def split3(x):
    high = x.astype(BF16).astype(F32)
    return [high] + split2(x - high)


def dot_nt(a, b):
    return lax.dot_general(a, b, (((1,), (1,)), ((), ())), preferred_element_type=F32)


def dot_nn(a, b):
    return lax.dot_general(a, b, (((1,), (0,)), ((), ())), preferred_element_type=F32)


def roll(x, shift):
    shift = shift % LANES
    return x if shift == 0 else pltpu.roll(x, shift, 1)


def total(x):
    return jnp.sum(jnp.sum(x, axis=0, keepdims=True), axis=1, keepdims=True)


def lane_value(row, lane):
    return jnp.sum(jnp.where(iota(row.shape, 1) == lane, row, 0.0), axis=1, keepdims=True)


def pick(tables, cells):
    low = cells & (LANES - 1)
    high = cells >> 7
    rows = [jnp.zeros(cells.shape, F32) for _ in tables]
    for tile in range(TILES):
        here = high == tile
        for v, table in enumerate(tables):
            wide = jnp.broadcast_to(table[tile], cells.shape)
            got = jnp.take_along_axis(wide, low, axis=1, mode="promise_in_bounds")
            rows[v] = jnp.where(here, got, rows[v])
    return rows


def one_hot(row, count):
    return jnp.where(iota((count, LANES), 0) == row, 1.0, 0.0).astype(BF16)


def add_rows(row_count, cell_row, value_rows):
    acc = None
    for j in range(0, row_count, 2):
        hots, masked = [], []
        for i in (j, j + 1):
            cells = cell_row(i)
            hots.append(one_hot(cells & (LANES - 1), LANES))
            here = iota((TILES, LANES), 0) == (cells >> 7)
            masked.append(
                jnp.concatenate([jnp.where(here, v, 0.0) for v in value_rows(i)], axis=0).astype(BF16)
            )
        part = dot_nt(jnp.concatenate(masked, axis=1), jnp.concatenate(hots, axis=1))
        acc = part if acc is None else acc + part
    return acc


def fold(acc, vectors, parts):
    size = vectors * TILES
    return sum(acc[i * size : (i + 1) * size] for i in range(parts))


def put_gathered(vectors, sums, cut_cells, pin_cell, pin_net, out_ref, kept_ref):
    lane = iota((32, LANES), 1)
    tail = jnp.zeros((1, LANES), F32)
    for i, s in enumerate(sums):
        tail = jnp.where(iota((1, LANES), 1) == SUM_LANE + i, s, tail)
    gx, gy = pick(vectors, pin_cell[...])
    net = (pin_net[...] & (LANES - 1)).astype(F32)
    for q in range(4):
        row = jnp.where(
            lane < 32,
            roll(gx, -32 * q),
            jnp.where(
                lane < 64,
                roll(gy, 32 - 32 * q),
                jnp.where(lane < 96, roll(net, 64 - 32 * q), tail),
            ),
        )
        out_ref[pl.ds(4 * q + 2, 32, stride=16), :] = row
        out_ref[pl.ds(4 * q + 3, 32, stride=16), :] = jnp.zeros((32, LANES), F32)
    for g in range(16):
        gx, gy = pick(vectors, cut_cells[pl.ds(8 * g, 8), :])
        out_ref[pl.ds(32 * g, 8, stride=4), :] = gx
        out_ref[pl.ds(32 * g + 1, 8, stride=4), :] = gy
        kept_ref[pl.ds(8 * g, 8), :] = gx
        kept_ref[pl.ds(128 + 8 * g, 8), :] = gy


def dense(rows, offset):
    lane = iota((32, LANES), 1)
    out = roll(rows[0], -offset)
    for q in range(1, 4):
        out = jnp.where(lane >= 32 * q, roll(rows[q], 32 * q - offset), out)
    return out


def first_kernel(right_hbm, cells_hbm, pin_cell_hbm, pin_net_hbm, send_ref, start_ref, kept_ref, right_ref, cut_cells, pin_cell, pin_net, sems):
    copies = [
        pltpu.make_async_copy(source, target, sems.at[i])
        for i, (source, target) in enumerate(
            (
                (right_hbm, right_ref),
                (pin_cell_hbm, pin_cell),
                (pin_net_hbm, pin_net),
                (cells_hbm, cut_cells),
            )
        )
    ]
    for copy in copies:
        copy.start()
    for copy in copies:
        copy.wait()
    tables = [
        [right_ref[v : v + 1, LANES * t : LANES * (t + 1)] for t in range(TILES)] for v in range(2)
    ]
    for v in range(2):
        for t in range(TILES):
            start_ref[TILES * v + t : TILES * v + t + 1, :] = tables[v][t]
    r = start_ref[...]
    sums = [total(r[16 * v : 16 * v + 16] * r[16 * v : 16 * v + 16]) for v in range(2)]
    put_gathered(tables, sums, cut_cells, pin_cell, pin_net, send_ref, kept_ref)


def block_kernel(first, place, own_ref, peer_ref, nbr, blocks, *refs):
    if first:
        (anchor, cut_weight, kept, local_ref, back_ref, share_ref, near, far, got_f, got_b, names, peers,
         *inner, sems) = refs
        copies = [
            pltpu.make_async_copy(source, target, sems.at[TILES + i])
            for i, (source, target) in enumerate(zip((nbr, anchor, cut_weight), inner))
        ]
        tiles = [
            pltpu.make_async_copy(blocks.at[t], inner[3].at[t], sems.at[t]) for t in range(TILES)
        ]
        for copy in copies + tiles:
            copy.start()
        nbr, anchor, cut_weight, blocks = inner
        for v in range(2):
            for t in range(TILES):
                peers[TILES * v + t : TILES * v + t + 1, :] = peer_ref[v : v + 1, LANES * t : LANES * (t + 1)]
        peer = peers[...]
    else:
        degree, local_ref, back_ref, share_ref, near, far, got_f, got_b, names = refs
        peer = peer_ref[...]
    own = own_ref[...]
    upper = place[0] == 1
    if first:
        for copy in copies:
            copy.wait()
    names[...] = jnp.zeros(names.shape, I32)
    for k in range(2):
        names[k : k + 1, 0:TILES] = nbr[k : k + 1, :]
    hot = [jnp.where(iota((128, LANES), 0) == names[k : k + 1, :], 1.0, 0.0) for k in range(2)]
    pick_rows = jnp.concatenate([h.T[:16] for h in hot], axis=0).astype(BF16)
    spread_rows = [h[:32].astype(BF16) for h in hot]
    near[...] = jnp.ones(near.shape, F32)
    far[...] = jnp.ones(far.shape, F32)
    zeros = jnp.zeros((96, LANES), F32)
    wholes = []
    for v in range(2):
        o, p = own[16 * v : 16 * v + 16], peer[16 * v : 16 * v + 16]
        whole = jnp.concatenate([jnp.where(upper, p, o), jnp.where(upper, o, p)], axis=0)
        wholes.append(whole)
        for i, (mine, part) in enumerate(zip(split2(o), split2(whole))):
            near[pl.ds(2 * i + v, 16, stride=8), :] = mine
            picked = dot_nn(pick_rows, jnp.concatenate([part, zeros], axis=0).astype(BF16))
            for k in range(2):
                far[pl.ds(128 * k + 2 * i + v, 16, stride=8), :] = picked[16 * k : 16 * k + 16]
    for t in range(TILES):
        if first:
            tiles[t].wait()
        pair = jnp.concatenate([blocks[t, 0], blocks[t, 1]], axis=1)
        high = pair.astype(BF16)
        low = (pair - high.astype(F32)).astype(BF16)
        a = near[8 * t : 8 * t + 8, :].astype(BF16)
        b = jnp.concatenate(
            [far[128 * k + 8 * t : 128 * k + 8 * t + 8, :] for k in range(2)], axis=1
        ).astype(BF16)
        back = dot_nn(a, high) + dot_nn(a, low)
        for k in range(2):
            got_b[128 * k + 8 * t : 128 * k + 8 * t + 8, :] = back[:, LANES * k : LANES * (k + 1)]
        got_f[8 * t : 8 * t + 8, :] = dot_nt(b, high) + dot_nt(b, low)
    filler = jnp.zeros((112, LANES), F32)
    ahead, whole_spread = [], []
    for v in range(3 if first else 2):
        def take(ref, at):
            if v == 2:
                return ref[pl.ds(at + 4, 16, stride=8), :]
            return ref[pl.ds(at + v, 16, stride=8), :] + ref[pl.ds(at + v + 2, 16, stride=8), :]

        forward = take(got_f, 0)
        spread = sum(
            dot_nn(spread_rows[k], jnp.concatenate([part, filler], axis=0).astype(BF16))
            for k in range(2)
            for part in split3(take(got_b, 128 * k))
        )
        ahead.append(forward)
        whole_spread.append(spread)
        lower, higher = spread[:16], spread[16:]
        local_ref[16 * v : 16 * v + 16, :] = forward + jnp.where(upper, higher, lower)
        back_ref[16 * v : 16 * v + 16, :] = jnp.where(upper, lower, higher)
    for v in range(2):
        r = own[16 * v : 16 * v + 16]
        if first:
            square = r * (r * (anchor[...] + ahead[2]) - 2.0 * ahead[v])
            line = jnp.sum(square, axis=0, keepdims=True)
            line = line + jnp.sum(wholes[v] * wholes[v] * whole_spread[2], axis=0, keepdims=True)
            cut = kept[128 * v : 128 * v + 128, :]
            line = line + jnp.sum(cut_weight[...] * cut * cut, axis=0, keepdims=True)
        else:
            line = jnp.sum(r * (r * degree[...] - 2.0 * ahead[v]), axis=0, keepdims=True)
        share_ref[v : v + 1, :] = line
    share_ref[2:8, :] = jnp.zeros((6, LANES), F32)


def owner_kernel(first, place, got, kept, cut_weight, star, share_ref, out_ref, sums_ref, rows):
    height = 16 if first else 8
    pin_rows = [got[pl.ds(4 * q + 2, 32, stride=16), :] for q in range(4)]
    sums = sum(jnp.sum(row, axis=0, keepdims=True) for row in pin_rows)
    sums_ref[...] = jnp.broadcast_to(sums, (8, LANES))
    nets = dense(pin_rows, 64).astype(I32)
    rows[...] = jnp.zeros(rows.shape, F32)
    for v in range(2):
        pins = dense(pin_rows, 32 * v)
        for i, part in enumerate(split3(pins)):
            rows[pl.ds(2 * i + v, 32, stride=height), :] = part
        if first:
            for i, part in enumerate(split3(pins * pins)):
                rows[pl.ds(8 + 2 * i + v, 32, stride=height), :] = part
    acc = None
    for j in range(0, 32, 2):
        hot = jnp.concatenate([one_hot(nets[i : i + 1], LANES) for i in (j, j + 1)], axis=1)
        left = jnp.concatenate(
            [rows[height * i : height * i + height, :] for i in (j, j + 1)], axis=1
        )
        part = dot_nt(left.astype(BF16), hot)
        acc = part if acc is None else acc + part
    weight = star[pl.ds(place[1], 1), :]
    totals = [acc[v : v + 1] + acc[v + 2 : v + 3] + acc[v + 4 : v + 5] for v in range(2)]
    centres = [weight * (1.0 / FANOUT) * t for t in totals]
    tail = jnp.zeros((1, LANES), F32)
    for v in range(2):
        line = share_ref[v : v + 1, :] - centres[v] * totals[v]
        if first:
            squares = acc[8 + v : 9 + v] + acc[10 + v : 11 + v] + acc[12 + v : 13 + v]
            line = line + weight * squares
        cut = cut_weight[...] * (kept[128 * v : 128 * v + 128, :] * got[pl.ds(v, 128, stride=4), :])
        line = line - jnp.sum(cut, axis=0, keepdims=True)
        tail = jnp.where(
            iota((1, LANES), 1) == SUM_LANE + v, jnp.sum(line, axis=1, keepdims=True), tail
        )
    lane = iota((8, LANES), 1)
    tables = [jnp.broadcast_to(c, (8, LANES)) for c in centres]
    for g in range(16):
        row = got[pl.ds(32 * g + 2, 8, stride=4), :]
        index = jnp.where(lane < 32, roll(row, -64), roll(row, -32)).astype(I32) & (LANES - 1)
        gx, gy = (
            jnp.take_along_axis(t, index, axis=1, mode="promise_in_bounds") for t in tables
        )
        out_ref[pl.ds(8 * g, 8), :] = jnp.where(
            lane < 32, gx, jnp.where(lane < 64, gy, jnp.where(lane < 96, 0.0, tail))
        )


def cut_kernel(first, cut_cells, cut_weight, got, local_ref, back_ref, sums_ref, *refs):
    del sums_ref

    def values(j):
        weight = cut_weight[j : j + 1, :]
        parts = [split2(weight * got[4 * j + v : 4 * j + v + 1, :]) for v in range(2)]
        moved = [parts[0][0], parts[1][0], parts[0][1], parts[1][1]]
        return moved + split3(weight) if first else moved

    acc = add_rows(128, lambda j: cut_cells[j : j + 1, :], values)
    if not first:
        (out_ref,) = refs
        out_ref[...] = fold(acc, 2, 2) + local_ref[...] + back_ref[...]
        return
    pin_cell, pin_net, star, anchor, out_ref, degree_ref, rows_ref, pins_ref = refs
    out_ref[...] = fold(acc[:64], 2, 2) + local_ref[0:32, :] + back_ref[0:32, :]
    net = pin_net[...] & (LANES - 1)
    for q in range(4):
        rows_ref[pl.ds(32 * q, 32), :] = jnp.take_along_axis(
            star[pl.ds(q, 32, stride=4), :], roll(net, -32 * q), axis=1, mode="promise_in_bounds"
        )
    weight = dense([rows_ref[pl.ds(32 * q, 32), :] for q in range(4)], 0)
    for i, part in enumerate(split3(weight)):
        pins_ref[pl.ds(32 * i, 32), :] = part
    pinned = add_rows(
        32,
        lambda j: pin_cell[j : j + 1, :],
        lambda j: [pins_ref[32 * i + j : 32 * i + j + 1, :] for i in range(3)],
    )
    degree_ref[...] = (
        anchor[...] + fold(acc[64:], 1, 3) + fold(pinned, 1, 3) + local_ref[32:48, :] + back_ref[32:48, :]
    )


def step_kernel(first, last, pin_cell, got, degree_ref, others, sums_ref, start_ref, *refs):
    refs = list(refs)
    state, old = (None, None) if first else (refs.pop(0), refs.pop(0))
    if last:
        positions_ref, residual_ref, pins = refs
    else:
        cut_cells, pin_net, send_ref, residual_ref, state_ref, old_ref, kept_ref, pins = refs
    pin_rows = [got[pl.ds(q, 32, stride=4), :] for q in range(4)]
    energy = sum(jnp.sum(row, axis=0, keepdims=True) for row in pin_rows)
    for v in range(2):
        for i, part in enumerate(split2(dense(pin_rows, 32 * v))):
            pins[pl.ds(32 * (2 * i + v), 32), :] = part
    acc = add_rows(
        32,
        lambda j: pin_cell[j : j + 1, :],
        lambda j: [pins[32 * i + j : 32 * i + j + 1, :] for i in range(4)],
    )
    removed = fold(acc, 2, 2) + others[...]
    degree = degree_ref[...]
    news, line = [], jnp.zeros((1, LANES), F32)
    lanes = iota((1, LANES), 1)
    sent_sums = [None] * 4
    for v in range(2):
        part = slice(16 * v, 16 * v + 16)
        r = start_ref[part, :]
        z = degree * r - removed[part]
        norm = lane_value(sums_ref[0:1, :], SUM_LANE + v)
        product = lane_value(energy, SUM_LANE + v)
        if first:
            p, q = r, z
        else:
            cross = lane_value(sums_ref[0:1, :], SUM_LANE + 2 + v)
            beta = norm / lane_value(old[0:1, :], v)
            product = product + beta * (2.0 * cross + beta * lane_value(old[0:1, :], 2 + v))
            p = r + beta * state[part, :]
            q = z + beta * state[32 + 16 * v : 48 + 16 * v, :]
        step = norm / product
        x = step * p
        if not first:
            x = x + state[64 + 16 * v : 80 + 16 * v, :]
        r = r - step * q
        if last:
            for t in range(TILES):
                positions_ref[v : v + 1, LANES * t : LANES * (t + 1)] = x[t : t + 1]
                residual_ref[v : v + 1, LANES * t : LANES * (t + 1)] = r[t : t + 1]
            continue
        residual_ref[part, :] = r
        for i, new in enumerate((p, q, x)):
            state_ref[32 * i + 16 * v : 32 * i + 16 * v + 16, :] = new
        news.append([r[t : t + 1] for t in range(TILES)])
        sent_sums[v], sent_sums[2 + v] = total(r * r), total(r * q)
        line = jnp.where(lanes == v, norm, jnp.where(lanes == 2 + v, product, line))
    if last:
        return
    old_ref[...] = jnp.broadcast_to(line, (8, LANES))
    put_gathered(news, sent_sums, cut_cells, pin_cell, pin_net, send_ref, kept_ref)


VMEM, SMEM, HBM = (pl.BlockSpec(memory_space=m) for m in (pltpu.VMEM, pltpu.SMEM, pltpu.HBM))


def call(kernel, shapes, scratch, cost, args, spaces=()):
    return pl.pallas_call(
        kernel,
        out_shape=[jax.ShapeDtypeStruct(s, F32) for s in shapes],
        in_specs=list(spaces) + [VMEM] * (len(args) - len(spaces)),
        out_specs=[VMEM] * len(shapes),
        scratch_shapes=[pltpu.VMEM(s, F32) if isinstance(s, tuple) else s for s in scratch],
        compiler_params=pltpu.CompilerParams(vmem_limit_bytes=32 << 20),
        cost_estimate=pl.CostEstimate(flops=cost, bytes_accessed=1 << 20, transcendentals=0),
    )(*args)


def stay(x):
    return pltpu.with_memory_space_constraint(x, pltpu.HBM)


def exchange(rows, height):
    return lax.all_to_all(
        rows.reshape(LANES, height, LANES), AXES, split_axis=0, concat_axis=0, tiled=True
    ).reshape(LANES * height, LANES)


def swap(x):
    return lax.ppermute(x, "coord", [(0, 1), (1, 0)])


def per_device(
    right_side, anchor, blocks, tile_nbr, cut_cells, cut_weight, pin_cell, pin_net, star_weight
):
    cut_cells, cut_weight = cut_cells[0], cut_weight[0]
    pin_cell, pin_net = pin_cell.reshape(32, LANES), pin_net.reshape(32, LANES)
    star, anchor = star_weight.reshape(LANES, LANES), anchor.reshape(TILES, LANES)
    coord = lax.axis_index("coord")
    place = jnp.stack([coord, lax.axis_index("region") * 2 + coord]).astype(I32)
    nbr = tile_nbr.T
    peer = swap(right_side)
    send, residual, kept = call(
        first_kernel,
        [(512, LANES), (32, LANES), (256, LANES)],
        [
            (2, TILES * LANES),
            pltpu.VMEM((128, LANES), I32),
            pltpu.VMEM((32, LANES), I32),
            pltpu.VMEM((32, LANES), I32),
            pltpu.SemaphoreType.DMA((4,)),
        ],
        1 << 24,
        tuple(stay(x) for x in (right_side, cut_cells, pin_cell, pin_net)),
        [HBM] * 4,
    )
    own_scratch = [
        (32, LANES),
        pltpu.VMEM((2, TILES), I32),
        (TILES, LANES),
        (LANES, LANES),
        (TILES, 2, LANES, LANES),
        pltpu.SemaphoreType.DMA((TILES + 3,)),
    ]
    for iteration in range(ITERS):
        first, last = iteration == 0, iteration == ITERS - 1
        got = exchange(send, 4)
        if not first:
            peer = swap(residual)
        rows = 48 if first else 32
        scratch = [(128, LANES), (256, LANES), (128, LANES), (256, LANES), pltpu.VMEM((8, LANES), I32)]
        local_sum, back, share = call(
            functools.partial(block_kernel, first),
            [(rows, LANES), (rows, LANES), (8, LANES)],
            scratch + own_scratch if first else scratch,
            1 << 31,
            (place, residual, peer)
            + (tuple(stay(x) for x in (nbr, blocks, anchor, cut_weight)) + (kept,) if first else (nbr, blocks, degree)),
            [SMEM, VMEM, VMEM] + [HBM] * 4 if first else [SMEM],
        )
        back = swap(back)
        out, sums = call(
            functools.partial(owner_kernel, first),
            [(128, LANES), (8, LANES)],
            [(512 if first else 256, LANES)],
            1 << 26,
            (place, got, kept, cut_weight, star, share),
            [SMEM],
        )
        returned = exchange(out, 1)
        args = (cut_cells, cut_weight, got, local_sum, back, sums)
        if first:
            others, degree = call(
                functools.partial(cut_kernel, True),
                [(32, LANES), (16, LANES)],
                [(128, LANES), (96, LANES)],
                1 << 31,
                args + (pin_cell, pin_net, star, anchor),
            )
        else:
            others = call(functools.partial(cut_kernel, False), [(32, LANES)], [], 1 << 31, args)[0]
        args = (pin_cell, returned, degree, others, sums, residual)
        if not first:
            args = args + (state, old)
        if last:
            shapes = [(2, TILES * LANES), (2, TILES * LANES)]
        else:
            args = args + (cut_cells, pin_net)
            shapes = [(512, LANES), (32, LANES), (96, LANES), (8, LANES), (256, LANES)]
        results = call(
            functools.partial(step_kernel, first, last), shapes, [(128, LANES)], 1 << 26, args
        )
        if last:
            return tuple(results)
        send, residual, state, old, kept = results


def solution(mesh):
    return jax.shard_map(
        per_device,
        mesh=mesh,
        in_specs=(
            P(None, AXES),
            P(AXES),
            P(AXES, None, None, None),
            P(AXES, None),
            P(AXES, None, None),
            P(AXES, None, None),
            P(AXES),
            P(AXES),
            P(),
        ),
        out_specs=(P(None, AXES), P(None, AXES)),
        check_vma=False,
    )
```

```python
import functools

import jax
import jax.numpy as jnp
from jax import lax
from jax.experimental import pallas as pl
from jax.experimental.pallas import tpu as pltpu
from jax.sharding import PartitionSpec as P

FANOUT = 32
ITERS = 3
AXES = ("region", "coord")
LANES = 128
TILES = 16
F32 = jnp.float32
BF16 = jnp.bfloat16
I32 = jnp.int32
SUM_LANE = 96


def iota(shape, axis):
    return lax.broadcasted_iota(I32, shape, axis)


def split2(x):
    high = x.astype(BF16).astype(F32)
    return [high, (x - high).astype(BF16).astype(F32)]


def split3(x):
    high = x.astype(BF16).astype(F32)
    return [high] + split2(x - high)


def dot_nt(a, b):
    return lax.dot_general(a, b, (((1,), (1,)), ((), ())), preferred_element_type=F32)


def dot_nn(a, b):
    return lax.dot_general(a, b, (((1,), (0,)), ((), ())), preferred_element_type=F32)


def roll(x, shift):
    shift = shift % LANES
    return x if shift == 0 else pltpu.roll(x, shift, 1)


def total(x):
    return jnp.sum(jnp.sum(x, axis=0, keepdims=True), axis=1, keepdims=True)


def lane_value(row, lane):
    return jnp.sum(jnp.where(iota(row.shape, 1) == lane, row, 0.0), axis=1, keepdims=True)


def pick(tables, cells):
    low = cells & (LANES - 1)
    high = cells >> 7
    rows = [jnp.zeros(cells.shape, F32) for _ in tables]
    for tile in range(TILES):
        here = high == tile
        for v, table in enumerate(tables):
            wide = jnp.broadcast_to(table[tile], cells.shape)
            got = jnp.take_along_axis(wide, low, axis=1, mode="promise_in_bounds")
            rows[v] = jnp.where(here, got, rows[v])
    return rows


def one_hot(row, count):
    return jnp.where(iota((count, LANES), 0) == row, 1.0, 0.0).astype(BF16)


def add_rows(row_count, cell_row, value_rows):
    acc = None
    for j in range(0, row_count, 2):
        hots, masked = [], []
        for i in (j, j + 1):
            cells = cell_row(i)
            hots.append(one_hot(cells & (LANES - 1), LANES))
            here = iota((TILES, LANES), 0) == (cells >> 7)
            masked.append(
                jnp.concatenate([jnp.where(here, v, 0.0) for v in value_rows(i)], axis=0).astype(BF16)
            )
        part = dot_nt(jnp.concatenate(masked, axis=1), jnp.concatenate(hots, axis=1))
        acc = part if acc is None else acc + part
    return acc


def fold(acc, vectors, parts):
    size = vectors * TILES
    return sum(acc[i * size : (i + 1) * size] for i in range(parts))


def put_gathered(vectors, sums, cut_cells, pin_cell, pin_net, out_ref, kept_ref):
    lane = iota((32, LANES), 1)
    tail = jnp.zeros((1, LANES), F32)
    for i, s in enumerate(sums):
        tail = jnp.where(iota((1, LANES), 1) == SUM_LANE + i, s, tail)
    gx, gy = pick(vectors, pin_cell[...])
    net = (pin_net[...] & (LANES - 1)).astype(F32)
    for q in range(4):
        row = jnp.where(
            lane < 32,
            roll(gx, -32 * q),
            jnp.where(
                lane < 64,
                roll(gy, 32 - 32 * q),
                jnp.where(lane < 96, roll(net, 64 - 32 * q), tail),
            ),
        )
        out_ref[pl.ds(4 * q + 2, 32, stride=16), :] = row
        out_ref[pl.ds(4 * q + 3, 32, stride=16), :] = jnp.zeros((32, LANES), F32)
    for g in range(16):
        gx, gy = pick(vectors, cut_cells[pl.ds(8 * g, 8), :])
        out_ref[pl.ds(32 * g, 8, stride=4), :] = gx
        out_ref[pl.ds(32 * g + 1, 8, stride=4), :] = gy
        kept_ref[pl.ds(8 * g, 8), :] = gx
        kept_ref[pl.ds(128 + 8 * g, 8), :] = gy


def dense(rows, offset):
    lane = iota((32, LANES), 1)
    out = roll(rows[0], -offset)
    for q in range(1, 4):
        out = jnp.where(lane >= 32 * q, roll(rows[q], 32 * q - offset), out)
    return out


def first_kernel(right_hbm, cells_hbm, pin_cell_hbm, pin_net_hbm, blocks_hbm, weight_hbm, anchor_hbm,
                 send_ref, start_ref, kept_ref, blocks_ref, weight_ref, anchor_ref,
                 right_ref, cut_cells, pin_cell, pin_net, sems):
    copies = [
        pltpu.make_async_copy(source, target, sems.at[i])
        for i, (source, target) in enumerate(
            (
                (right_hbm, right_ref),
                (pin_cell_hbm, pin_cell),
                (pin_net_hbm, pin_net),
                (cells_hbm, cut_cells),
                (weight_hbm, weight_ref),
                (anchor_hbm, anchor_ref),
                (blocks_hbm, blocks_ref),
            )
        )
    ]
    for copy in copies:
        copy.start()
    for copy in copies[:4]:
        copy.wait()
    tables = [
        [right_ref[v : v + 1, LANES * t : LANES * (t + 1)] for t in range(TILES)] for v in range(2)
    ]
    for v in range(2):
        for t in range(TILES):
            start_ref[TILES * v + t : TILES * v + t + 1, :] = tables[v][t]
    r = start_ref[...]
    sums = [total(r[16 * v : 16 * v + 16] * r[16 * v : 16 * v + 16]) for v in range(2)]
    put_gathered(tables, sums, cut_cells, pin_cell, pin_net, send_ref, kept_ref)
    for copy in copies[4:]:
        copy.wait()


def block_kernel(first, place, own_ref, peer_ref, nbr, blocks, *refs):
    if first:
        anchor, cut_weight, kept, local_ref, back_ref, share_ref, near, far, got_f, got_b, names, peers = refs
        for v in range(2):
            for t in range(TILES):
                peers[TILES * v + t : TILES * v + t + 1, :] = peer_ref[v : v + 1, LANES * t : LANES * (t + 1)]
        peer = peers[...]
    else:
        degree, local_ref, back_ref, share_ref, near, far, got_f, got_b, names = refs
        peer = peer_ref[...]
    own = own_ref[...]
    upper = place[0] == 1
    names[...] = jnp.zeros(names.shape, I32)
    for k in range(2):
        names[k : k + 1, 0:TILES] = nbr[k : k + 1, :]
    hot = [jnp.where(iota((128, LANES), 0) == names[k : k + 1, :], 1.0, 0.0) for k in range(2)]
    pick_rows = jnp.concatenate([h.T[:16] for h in hot], axis=0).astype(BF16)
    spread_rows = [h[:32].astype(BF16) for h in hot]
    near[...] = jnp.ones(near.shape, F32)
    far[...] = jnp.ones(far.shape, F32)
    zeros = jnp.zeros((96, LANES), F32)
    wholes = []
    for v in range(2):
        o, p = own[16 * v : 16 * v + 16], peer[16 * v : 16 * v + 16]
        whole = jnp.concatenate([jnp.where(upper, p, o), jnp.where(upper, o, p)], axis=0)
        wholes.append(whole)
        for i, (mine, part) in enumerate(zip(split2(o), split2(whole))):
            near[pl.ds(2 * i + v, 16, stride=8), :] = mine
            picked = dot_nn(pick_rows, jnp.concatenate([part, zeros], axis=0).astype(BF16))
            for k in range(2):
                far[pl.ds(128 * k + 2 * i + v, 16, stride=8), :] = picked[16 * k : 16 * k + 16]
    for t in range(TILES):
        pair = jnp.concatenate([blocks[t, 0], blocks[t, 1]], axis=1)
        high = pair.astype(BF16)
        low = (pair - high.astype(F32)).astype(BF16)
        a = near[8 * t : 8 * t + 8, :].astype(BF16)
        b = jnp.concatenate(
            [far[128 * k + 8 * t : 128 * k + 8 * t + 8, :] for k in range(2)], axis=1
        ).astype(BF16)
        back = dot_nn(a, high) + dot_nn(a, low)
        for k in range(2):
            got_b[128 * k + 8 * t : 128 * k + 8 * t + 8, :] = back[:, LANES * k : LANES * (k + 1)]
        got_f[8 * t : 8 * t + 8, :] = dot_nt(b, high) + dot_nt(b, low)
    filler = jnp.zeros((112, LANES), F32)
    ahead, whole_spread = [], []
    for v in range(3 if first else 2):
        def take(ref, at):
            if v == 2:
                return ref[pl.ds(at + 4, 16, stride=8), :]
            return ref[pl.ds(at + v, 16, stride=8), :] + ref[pl.ds(at + v + 2, 16, stride=8), :]

        forward = take(got_f, 0)
        spread = sum(
            dot_nn(spread_rows[k], jnp.concatenate([part, filler], axis=0).astype(BF16))
            for k in range(2)
            for part in split3(take(got_b, 128 * k))
        )
        ahead.append(forward)
        whole_spread.append(spread)
        lower, higher = spread[:16], spread[16:]
        local_ref[16 * v : 16 * v + 16, :] = forward + jnp.where(upper, higher, lower)
        back_ref[16 * v : 16 * v + 16, :] = jnp.where(upper, lower, higher)
    for v in range(2):
        r = own[16 * v : 16 * v + 16]
        if first:
            square = r * (r * (anchor[...] + ahead[2]) - 2.0 * ahead[v])
            line = jnp.sum(square, axis=0, keepdims=True)
            line = line + jnp.sum(wholes[v] * wholes[v] * whole_spread[2], axis=0, keepdims=True)
            cut = kept[128 * v : 128 * v + 128, :]
            line = line + jnp.sum(cut_weight[...] * cut * cut, axis=0, keepdims=True)
        else:
            line = jnp.sum(r * (r * degree[...] - 2.0 * ahead[v]), axis=0, keepdims=True)
        share_ref[v : v + 1, :] = line
    share_ref[2:8, :] = jnp.zeros((6, LANES), F32)


def owner_kernel(first, place, got, kept, cut_weight, star, share_ref, out_ref, sums_ref, rows):
    height = 16 if first else 8
    pin_rows = [got[pl.ds(4 * q + 2, 32, stride=16), :] for q in range(4)]
    sums = sum(jnp.sum(row, axis=0, keepdims=True) for row in pin_rows)
    sums_ref[...] = jnp.broadcast_to(sums, (8, LANES))
    nets = dense(pin_rows, 64).astype(I32)
    rows[...] = jnp.zeros(rows.shape, F32)
    for v in range(2):
        pins = dense(pin_rows, 32 * v)
        for i, part in enumerate(split3(pins)):
            rows[pl.ds(2 * i + v, 32, stride=height), :] = part
        if first:
            for i, part in enumerate(split3(pins * pins)):
                rows[pl.ds(8 + 2 * i + v, 32, stride=height), :] = part
    acc = None
    for j in range(0, 32, 2):
        hot = jnp.concatenate([one_hot(nets[i : i + 1], LANES) for i in (j, j + 1)], axis=1)
        left = jnp.concatenate(
            [rows[height * i : height * i + height, :] for i in (j, j + 1)], axis=1
        )
        part = dot_nt(left.astype(BF16), hot)
        acc = part if acc is None else acc + part
    weight = star[pl.ds(place[1], 1), :]
    totals = [acc[v : v + 1] + acc[v + 2 : v + 3] + acc[v + 4 : v + 5] for v in range(2)]
    centres = [weight * (1.0 / FANOUT) * t for t in totals]
    tail = jnp.zeros((1, LANES), F32)
    for v in range(2):
        line = share_ref[v : v + 1, :] - centres[v] * totals[v]
        if first:
            squares = acc[8 + v : 9 + v] + acc[10 + v : 11 + v] + acc[12 + v : 13 + v]
            line = line + weight * squares
        cut = cut_weight[...] * (kept[128 * v : 128 * v + 128, :] * got[pl.ds(v, 128, stride=4), :])
        line = line - jnp.sum(cut, axis=0, keepdims=True)
        tail = jnp.where(
            iota((1, LANES), 1) == SUM_LANE + v, jnp.sum(line, axis=1, keepdims=True), tail
        )
    lane = iota((8, LANES), 1)
    tables = [jnp.broadcast_to(c, (8, LANES)) for c in centres]
    for g in range(16):
        row = got[pl.ds(32 * g + 2, 8, stride=4), :]
        index = jnp.where(lane < 32, roll(row, -64), roll(row, -32)).astype(I32) & (LANES - 1)
        gx, gy = (
            jnp.take_along_axis(t, index, axis=1, mode="promise_in_bounds") for t in tables
        )
        out_ref[pl.ds(8 * g, 8), :] = jnp.where(
            lane < 32, gx, jnp.where(lane < 64, gy, jnp.where(lane < 96, 0.0, tail))
        )


def cut_kernel(first, cut_cells, cut_weight, got, local_ref, back_ref, sums_ref, *refs):
    del sums_ref

    def values(j):
        weight = cut_weight[j : j + 1, :]
        parts = [split2(weight * got[4 * j + v : 4 * j + v + 1, :]) for v in range(2)]
        moved = [parts[0][0], parts[1][0], parts[0][1], parts[1][1]]
        return moved + split3(weight) if first else moved

    acc = add_rows(128, lambda j: cut_cells[j : j + 1, :], values)
    if not first:
        (out_ref,) = refs
        out_ref[...] = fold(acc, 2, 2) + local_ref[...] + back_ref[...]
        return
    pin_cell, pin_net, star, anchor, out_ref, degree_ref, rows_ref, pins_ref = refs
    out_ref[...] = fold(acc[:64], 2, 2) + local_ref[0:32, :] + back_ref[0:32, :]
    net = pin_net[...] & (LANES - 1)
    for q in range(4):
        rows_ref[pl.ds(32 * q, 32), :] = jnp.take_along_axis(
            star[pl.ds(q, 32, stride=4), :], roll(net, -32 * q), axis=1, mode="promise_in_bounds"
        )
    weight = dense([rows_ref[pl.ds(32 * q, 32), :] for q in range(4)], 0)
    for i, part in enumerate(split3(weight)):
        pins_ref[pl.ds(32 * i, 32), :] = part
    pinned = add_rows(
        32,
        lambda j: pin_cell[j : j + 1, :],
        lambda j: [pins_ref[32 * i + j : 32 * i + j + 1, :] for i in range(3)],
    )
    degree_ref[...] = (
        anchor[...] + fold(acc[64:], 1, 3) + fold(pinned, 1, 3) + local_ref[32:48, :] + back_ref[32:48, :]
    )


def step_kernel(first, last, pin_cell, got, degree_ref, others, sums_ref, start_ref, *refs):
    refs = list(refs)
    state, old = (None, None) if first else (refs.pop(0), refs.pop(0))
    if last:
        positions_ref, residual_ref, pins = refs
    else:
        cut_cells, pin_net, send_ref, residual_ref, state_ref, old_ref, kept_ref, pins = refs
    pin_rows = [got[pl.ds(q, 32, stride=4), :] for q in range(4)]
    energy = sum(jnp.sum(row, axis=0, keepdims=True) for row in pin_rows)
    for v in range(2):
        for i, part in enumerate(split2(dense(pin_rows, 32 * v))):
            pins[pl.ds(32 * (2 * i + v), 32), :] = part
    acc = add_rows(
        32,
        lambda j: pin_cell[j : j + 1, :],
        lambda j: [pins[32 * i + j : 32 * i + j + 1, :] for i in range(4)],
    )
    removed = fold(acc, 2, 2) + others[...]
    degree = degree_ref[...]
    news, line = [], jnp.zeros((1, LANES), F32)
    lanes = iota((1, LANES), 1)
    sent_sums = [None] * 4
    for v in range(2):
        part = slice(16 * v, 16 * v + 16)
        r = start_ref[part, :]
        z = degree * r - removed[part]
        norm = lane_value(sums_ref[0:1, :], SUM_LANE + v)
        product = lane_value(energy, SUM_LANE + v)
        if first:
            p, q = r, z
        else:
            cross = lane_value(sums_ref[0:1, :], SUM_LANE + 2 + v)
            beta = norm / lane_value(old[0:1, :], v)
            product = product + beta * (2.0 * cross + beta * lane_value(old[0:1, :], 2 + v))
            p = r + beta * state[part, :]
            q = z + beta * state[32 + 16 * v : 48 + 16 * v, :]
        step = norm / product
        x = step * p
        if not first:
            x = x + state[64 + 16 * v : 80 + 16 * v, :]
        r = r - step * q
        if last:
            for t in range(TILES):
                positions_ref[v : v + 1, LANES * t : LANES * (t + 1)] = x[t : t + 1]
                residual_ref[v : v + 1, LANES * t : LANES * (t + 1)] = r[t : t + 1]
            continue
        residual_ref[part, :] = r
        for i, new in enumerate((p, q, x)):
            state_ref[32 * i + 16 * v : 32 * i + 16 * v + 16, :] = new
        news.append([r[t : t + 1] for t in range(TILES)])
        sent_sums[v], sent_sums[2 + v] = total(r * r), total(r * q)
        line = jnp.where(lanes == v, norm, jnp.where(lanes == 2 + v, product, line))
    if last:
        return
    old_ref[...] = jnp.broadcast_to(line, (8, LANES))
    put_gathered(news, sent_sums, cut_cells, pin_cell, pin_net, send_ref, kept_ref)


VMEM, SMEM, HBM = (pl.BlockSpec(memory_space=m) for m in (pltpu.VMEM, pltpu.SMEM, pltpu.HBM))


def call(kernel, shapes, scratch, cost, args, spaces=()):
    return pl.pallas_call(
        kernel,
        out_shape=[jax.ShapeDtypeStruct(s, F32) for s in shapes],
        in_specs=list(spaces) + [VMEM] * (len(args) - len(spaces)),
        out_specs=[VMEM] * len(shapes),
        scratch_shapes=[pltpu.VMEM(s, F32) if isinstance(s, tuple) else s for s in scratch],
        compiler_params=pltpu.CompilerParams(vmem_limit_bytes=32 << 20),
        cost_estimate=pl.CostEstimate(flops=cost, bytes_accessed=1 << 20, transcendentals=0),
    )(*args)


def stay(x):
    return pltpu.with_memory_space_constraint(x, pltpu.HBM)


def exchange(rows, height):
    return lax.all_to_all(
        rows.reshape(LANES, height, LANES), AXES, split_axis=0, concat_axis=0, tiled=True
    ).reshape(LANES * height, LANES)


def swap(x):
    return lax.ppermute(x, "coord", [(0, 1), (1, 0)])


def per_device(
    right_side, anchor, blocks, tile_nbr, cut_cells, cut_weight, pin_cell, pin_net, star_weight
):
    cut_cells, cut_weight = cut_cells[0], cut_weight[0]
    pin_cell, pin_net = pin_cell.reshape(32, LANES), pin_net.reshape(32, LANES)
    star, anchor = star_weight.reshape(LANES, LANES), anchor.reshape(TILES, LANES)
    coord = lax.axis_index("coord")
    place = jnp.stack([coord, lax.axis_index("region") * 2 + coord]).astype(I32)
    nbr = tile_nbr.T
    peer = swap(right_side)
    send, residual, kept, blocks, cut_weight, anchor = call(
        first_kernel,
        [(512, LANES), (32, LANES), (256, LANES), blocks.shape, (LANES, LANES), (TILES, LANES)],
        [
            (2, TILES * LANES),
            pltpu.VMEM((128, LANES), I32),
            pltpu.VMEM((32, LANES), I32),
            pltpu.VMEM((32, LANES), I32),
            pltpu.SemaphoreType.DMA((7,)),
        ],
        1 << 24,
        tuple(stay(x) for x in (right_side, cut_cells, pin_cell, pin_net, blocks, cut_weight, anchor)),
        [HBM] * 7,
    )
    for iteration in range(ITERS):
        first, last = iteration == 0, iteration == ITERS - 1
        got = exchange(send, 4)
        if not first:
            peer = swap(residual)
        rows = 48 if first else 32
        scratch = [(128, LANES), (256, LANES), (128, LANES), (256, LANES), pltpu.VMEM((8, LANES), I32)]
        local_sum, back, share = call(
            functools.partial(block_kernel, first),
            [(rows, LANES), (rows, LANES), (8, LANES)],
            scratch + [(32, LANES)] if first else scratch,
            1 << 32,
            (place, residual, peer, nbr, blocks) + ((anchor, cut_weight, kept) if first else (degree,)),
            [SMEM],
        )
        back = swap(back)
        out, sums = call(
            functools.partial(owner_kernel, first),
            [(128, LANES), (8, LANES)],
            [(512 if first else 256, LANES)],
            1 << 26,
            (place, got, kept, cut_weight, star, share),
            [SMEM],
        )
        returned = exchange(out, 1)
        args = (cut_cells, cut_weight, got, local_sum, back, sums)
        if first:
            others, degree = call(
                functools.partial(cut_kernel, True),
                [(32, LANES), (16, LANES)],
                [(128, LANES), (96, LANES)],
                1 << 31,
                args + (pin_cell, pin_net, star, anchor),
            )
        else:
            others = call(functools.partial(cut_kernel, False), [(32, LANES)], [], 1 << 31, args)[0]
        args = (pin_cell, returned, degree, others, sums, residual)
        if not first:
            args = args + (state, old)
        if last:
            shapes = [(2, TILES * LANES), (2, TILES * LANES)]
        else:
            args = args + (cut_cells, pin_net)
            shapes = [(512, LANES), (32, LANES), (96, LANES), (8, LANES), (256, LANES)]
        results = call(
            functools.partial(step_kernel, first, last), shapes, [(128, LANES)], 1 << 26, args
        )
        if last:
            return tuple(results)
        send, residual, state, old, kept = results


def solution(mesh):
    return jax.shard_map(
        per_device,
        mesh=mesh,
        in_specs=(
            P(None, AXES),
            P(AXES),
            P(AXES, None, None, None),
            P(AXES, None),
            P(AXES, None, None),
            P(AXES, None, None),
            P(AXES),
            P(AXES),
            P(),
        ),
        out_specs=(P(None, AXES), P(None, AXES)),
        check_vma=False,
    )
```

```python
import functools

import jax
import jax.numpy as jnp
from jax import lax
from jax.experimental import pallas as pl
from jax.experimental.pallas import tpu as pltpu
from jax.sharding import PartitionSpec as P

FANOUT = 32
ITERS = 3
AXES = ("region", "coord")
LANES = 128
TILES = 16
F32 = jnp.float32
BF16 = jnp.bfloat16
I32 = jnp.int32
SUM_LANE = 96


def iota(shape, axis):
    return lax.broadcasted_iota(I32, shape, axis)


def split2(x):
    high = x.astype(BF16).astype(F32)
    return [high, (x - high).astype(BF16).astype(F32)]


def split3(x):
    high = x.astype(BF16).astype(F32)
    return [high] + split2(x - high)


def dot_nt(a, b):
    return lax.dot_general(a, b, (((1,), (1,)), ((), ())), preferred_element_type=F32)


def dot_nn(a, b):
    return lax.dot_general(a, b, (((1,), (0,)), ((), ())), preferred_element_type=F32)


def roll(x, shift):
    shift = shift % LANES
    return x if shift == 0 else pltpu.roll(x, shift, 1)


def total(x):
    return jnp.sum(jnp.sum(x, axis=0, keepdims=True), axis=1, keepdims=True)


def lane_value(row, lane):
    return jnp.sum(jnp.where(iota(row.shape, 1) == lane, row, 0.0), axis=1, keepdims=True)


def pick(tables, cells):
    low = cells & (LANES - 1)
    high = cells >> 7
    rows = [jnp.zeros(cells.shape, F32) for _ in tables]
    for tile in range(TILES):
        here = high == tile
        for v, table in enumerate(tables):
            wide = jnp.broadcast_to(table[tile], cells.shape)
            got = jnp.take_along_axis(wide, low, axis=1, mode="promise_in_bounds")
            rows[v] = jnp.where(here, got, rows[v])
    return rows


def one_hot(row, count):
    return jnp.where(iota((count, LANES), 0) == row, 1.0, 0.0).astype(BF16)


def add_rows(row_count, cell_row, value_rows):
    acc = None
    for j in range(0, row_count, 2):
        hots, masked = [], []
        for i in (j, j + 1):
            cells = cell_row(i)
            hots.append(one_hot(cells & (LANES - 1), LANES))
            here = iota((TILES, LANES), 0) == (cells >> 7)
            masked.append(
                jnp.concatenate([jnp.where(here, v, 0.0) for v in value_rows(i)], axis=0).astype(BF16)
            )
        part = dot_nt(jnp.concatenate(masked, axis=1), jnp.concatenate(hots, axis=1))
        acc = part if acc is None else acc + part
    return acc


def fold(acc, vectors, parts):
    size = vectors * TILES
    return sum(acc[i * size : (i + 1) * size] for i in range(parts))


def put_gathered(vectors, sums, cut_cells, pin_cell, pin_net, out_ref, kept_ref):
    lane = iota((32, LANES), 1)
    tail = jnp.zeros((1, LANES), F32)
    for i, s in enumerate(sums):
        tail = jnp.where(iota((1, LANES), 1) == SUM_LANE + i, s, tail)
    groups = [pick(vectors, pin_cell[8 * h : 8 * h + 8, :]) for h in range(4)]
    gx, gy = (jnp.concatenate([g[v] for g in groups], axis=0) for v in range(2))
    net = (pin_net[...] & (LANES - 1)).astype(F32)
    for q in range(4):
        row = jnp.where(
            lane < 32,
            roll(gx, -32 * q),
            jnp.where(
                lane < 64,
                roll(gy, 32 - 32 * q),
                jnp.where(lane < 96, roll(net, 64 - 32 * q), tail),
            ),
        )
        out_ref[pl.ds(3 * q + 2, 32, stride=12), :] = row
    for g in range(16):
        gx, gy = pick(vectors, cut_cells[pl.ds(8 * g, 8), :])
        out_ref[pl.ds(24 * g, 8, stride=3), :] = gx
        out_ref[pl.ds(24 * g + 1, 8, stride=3), :] = gy
        kept_ref[pl.ds(8 * g, 8), :] = gx
        kept_ref[pl.ds(128 + 8 * g, 8), :] = gy


def dense(rows, offset):
    lane = iota((32, LANES), 1)
    out = roll(rows[0], -offset)
    for q in range(1, 4):
        out = jnp.where(lane >= 32 * q, roll(rows[q], 32 * q - offset), out)
    return out


def first_kernel(right_hbm, cells_hbm, pin_cell_hbm, pin_net_hbm, blocks_hbm, weight_hbm, anchor_hbm,
                 send_ref, start_ref, kept_ref, blocks_ref, weight_ref, anchor_ref,
                 right_ref, cut_cells, pin_cell, pin_net, sems):
    copies = [
        pltpu.make_async_copy(source, target, sems.at[i])
        for i, (source, target) in enumerate(
            (
                (right_hbm, right_ref),
                (pin_cell_hbm, pin_cell),
                (pin_net_hbm, pin_net),
                (cells_hbm, cut_cells),
                (weight_hbm, weight_ref),
                (anchor_hbm, anchor_ref),
                (blocks_hbm, blocks_ref),
            )
        )
    ]
    for copy in copies:
        copy.start()
    for copy in copies[:4]:
        copy.wait()
    tables = [
        [right_ref[v : v + 1, LANES * t : LANES * (t + 1)] for t in range(TILES)] for v in range(2)
    ]
    for v in range(2):
        for t in range(TILES):
            start_ref[TILES * v + t : TILES * v + t + 1, :] = tables[v][t]
    r = start_ref[...]
    sums = [total(r[16 * v : 16 * v + 16] * r[16 * v : 16 * v + 16]) for v in range(2)]
    put_gathered(tables, sums, cut_cells, pin_cell, pin_net, send_ref, kept_ref)
    for copy in copies[4:]:
        copy.wait()


def block_kernel(first, place, own_ref, peer_ref, nbr, blocks, *refs):
    if first:
        (anchor, cut_weight, kept, star, local_ref, back_ref, share_ref, net_weight_ref,
         near, far, got_f, got_b, names, peers) = refs
        net_weight_ref[...] = jnp.broadcast_to(star[pl.ds(place[1], 1), :], (8, LANES))
        for v in range(2):
            for t in range(TILES):
                peers[TILES * v + t : TILES * v + t + 1, :] = peer_ref[v : v + 1, LANES * t : LANES * (t + 1)]
        peer = peers[...]
    else:
        degree, local_ref, back_ref, share_ref, near, far, got_f, got_b, names = refs
        peer = peer_ref[...]
    own = own_ref[...]
    upper = place[0] == 1
    names[...] = jnp.zeros(names.shape, I32)
    for k in range(2):
        names[k : k + 1, 0:TILES] = nbr[k : k + 1, :]
    hot = [jnp.where(iota((128, LANES), 0) == names[k : k + 1, :], 1.0, 0.0) for k in range(2)]
    pick_rows = jnp.concatenate([h.T[:16] for h in hot], axis=0).astype(BF16)
    spread_rows = [h[:32].astype(BF16) for h in hot]
    near[...] = jnp.ones(near.shape, F32)
    far[...] = jnp.ones(far.shape, F32)
    zeros = jnp.zeros((96, LANES), F32)
    wholes = []
    for v in range(2):
        o, p = own[16 * v : 16 * v + 16], peer[16 * v : 16 * v + 16]
        whole = jnp.concatenate([jnp.where(upper, p, o), jnp.where(upper, o, p)], axis=0)
        wholes.append(whole)
        for i, (mine, part) in enumerate(zip(split2(o), split2(whole))):
            near[pl.ds(2 * i + v, 16, stride=8), :] = mine
            picked = dot_nn(pick_rows, jnp.concatenate([part, zeros], axis=0).astype(BF16))
            for k in range(2):
                far[pl.ds(128 * k + 2 * i + v, 16, stride=8), :] = picked[16 * k : 16 * k + 16]
    for t in range(TILES):
        pair = jnp.concatenate([blocks[t, 0], blocks[t, 1]], axis=1)
        high = pair.astype(BF16)
        low = (pair - high.astype(F32)).astype(BF16)
        a = near[8 * t : 8 * t + 8, :].astype(BF16)
        b = jnp.concatenate(
            [far[128 * k + 8 * t : 128 * k + 8 * t + 8, :] for k in range(2)], axis=1
        ).astype(BF16)
        back = dot_nn(a, high) + dot_nn(a, low)
        for k in range(2):
            got_b[128 * k + 8 * t : 128 * k + 8 * t + 8, :] = back[:, LANES * k : LANES * (k + 1)]
        got_f[8 * t : 8 * t + 8, :] = dot_nt(b, high) + dot_nt(b, low)
    filler = jnp.zeros((112, LANES), F32)
    ahead, whole_spread = [], []
    for v in range(3 if first else 2):
        def take(ref, at):
            if v == 2:
                return ref[pl.ds(at + 4, 16, stride=8), :]
            return ref[pl.ds(at + v, 16, stride=8), :] + ref[pl.ds(at + v + 2, 16, stride=8), :]

        forward = take(got_f, 0)
        spread = sum(
            dot_nn(spread_rows[k], jnp.concatenate([part, filler], axis=0).astype(BF16))
            for k in range(2)
            for part in split3(take(got_b, 128 * k))
        )
        ahead.append(forward)
        whole_spread.append(spread)
        lower, higher = spread[:16], spread[16:]
        local_ref[16 * v : 16 * v + 16, :] = forward + jnp.where(upper, higher, lower)
        back_ref[16 * v : 16 * v + 16, :] = jnp.where(upper, lower, higher)
    for v in range(2):
        r = own[16 * v : 16 * v + 16]
        if first:
            square = r * (r * (anchor[...] + ahead[2]) - 2.0 * ahead[v])
            line = jnp.sum(square, axis=0, keepdims=True)
            line = line + jnp.sum(wholes[v] * wholes[v] * whole_spread[2], axis=0, keepdims=True)
            cut = kept[128 * v : 128 * v + 128, :]
            line = line + jnp.sum(cut_weight[...] * cut * cut, axis=0, keepdims=True)
        else:
            line = jnp.sum(r * (r * degree[...] - 2.0 * ahead[v]), axis=0, keepdims=True)
        share_ref[v : v + 1, :] = line
    share_ref[2:8, :] = jnp.zeros((6, LANES), F32)


def owner_kernel(first, got, kept, cut_weight, net_weight, share_ref, out_ref, sums_ref, rows):
    height = 16 if first else 8
    pin_rows = [got[pl.ds(3 * q + 2, 32, stride=12), :] for q in range(4)]
    sums = sum(jnp.sum(row, axis=0, keepdims=True) for row in pin_rows)
    sums_ref[...] = jnp.broadcast_to(sums, (8, LANES))
    nets = dense(pin_rows, 64).astype(I32)
    rows[...] = jnp.zeros(rows.shape, F32)
    for v in range(2):
        pins = dense(pin_rows, 32 * v)
        for i, part in enumerate(split3(pins)):
            rows[pl.ds(2 * i + v, 32, stride=height), :] = part
        if first:
            for i, part in enumerate(split3(pins * pins)):
                rows[pl.ds(8 + 2 * i + v, 32, stride=height), :] = part
    acc = None
    for j in range(0, 32, 2):
        hot = jnp.concatenate([one_hot(nets[i : i + 1], LANES) for i in (j, j + 1)], axis=1)
        left = jnp.concatenate(
            [rows[height * i : height * i + height, :] for i in (j, j + 1)], axis=1
        )
        part = dot_nt(left.astype(BF16), hot)
        acc = part if acc is None else acc + part
    weight = net_weight[0:1, :]
    totals = [acc[v : v + 1] + acc[v + 2 : v + 3] + acc[v + 4 : v + 5] for v in range(2)]
    centres = [weight * (1.0 / FANOUT) * t for t in totals]
    tail = jnp.zeros((1, LANES), F32)
    for v in range(2):
        line = share_ref[v : v + 1, :] - centres[v] * totals[v]
        if first:
            squares = acc[8 + v : 9 + v] + acc[10 + v : 11 + v] + acc[12 + v : 13 + v]
            line = line + weight * squares
        cut = cut_weight[...] * (kept[128 * v : 128 * v + 128, :] * got[pl.ds(v, 128, stride=3), :])
        line = line - jnp.sum(cut, axis=0, keepdims=True)
        tail = jnp.where(
            iota((1, LANES), 1) == SUM_LANE + v, jnp.sum(line, axis=1, keepdims=True), tail
        )
    lane = iota((8, LANES), 1)
    tables = [jnp.broadcast_to(c, (8, LANES)) for c in centres]
    for g in range(16):
        row = got[pl.ds(24 * g + 2, 8, stride=3), :]
        index = jnp.where(lane < 32, roll(row, -64), roll(row, -32)).astype(I32) & (LANES - 1)
        gx, gy = (
            jnp.take_along_axis(t, index, axis=1, mode="promise_in_bounds") for t in tables
        )
        out_ref[pl.ds(8 * g, 8), :] = jnp.where(
            lane < 32, gx, jnp.where(lane < 64, gy, jnp.where(lane < 96, 0.0, tail))
        )


def cut_kernel(first, cut_cells, cut_weight, got, local_ref, back_ref, sums_ref, *refs):
    del sums_ref

    def values(j):
        weight = cut_weight[j : j + 1, :]
        parts = [split2(weight * got[3 * j + v : 3 * j + v + 1, :]) for v in range(2)]
        moved = [parts[0][0], parts[1][0], parts[0][1], parts[1][1]]
        return moved + split3(weight) if first else moved

    acc = add_rows(128, lambda j: cut_cells[j : j + 1, :], values)
    if not first:
        (out_ref,) = refs
        out_ref[...] = fold(acc, 2, 2) + local_ref[...] + back_ref[...]
        return
    pin_cell, pin_net, star, anchor, out_ref, degree_ref, rows_ref, pins_ref = refs
    out_ref[...] = fold(acc[:64], 2, 2) + local_ref[0:32, :] + back_ref[0:32, :]
    net = pin_net[...] & (LANES - 1)
    for q in range(4):
        rows_ref[pl.ds(32 * q, 32), :] = jnp.take_along_axis(
            star[pl.ds(q, 32, stride=4), :], roll(net, -32 * q), axis=1, mode="promise_in_bounds"
        )
    weight = dense([rows_ref[pl.ds(32 * q, 32), :] for q in range(4)], 0)
    for i, part in enumerate(split3(weight)):
        pins_ref[pl.ds(32 * i, 32), :] = part
    pinned = add_rows(
        32,
        lambda j: pin_cell[j : j + 1, :],
        lambda j: [pins_ref[32 * i + j : 32 * i + j + 1, :] for i in range(3)],
    )
    degree_ref[...] = (
        anchor[...] + fold(acc[64:], 1, 3) + fold(pinned, 1, 3) + local_ref[32:48, :] + back_ref[32:48, :]
    )


def step_kernel(first, last, pin_cell, got, degree_ref, others, sums_ref, start_ref, *refs):
    refs = list(refs)
    state, old = (None, None) if first else (refs.pop(0), refs.pop(0))
    if last:
        positions_ref, residual_ref, pins = refs
    else:
        cut_cells, pin_net, send_ref, residual_ref, state_ref, old_ref, kept_ref, pins = refs
    pin_rows = [got[pl.ds(q, 32, stride=4), :] for q in range(4)]
    energy = sum(jnp.sum(row, axis=0, keepdims=True) for row in pin_rows)
    for v in range(2):
        for i, part in enumerate(split2(dense(pin_rows, 32 * v))):
            pins[pl.ds(32 * (2 * i + v), 32), :] = part
    acc = add_rows(
        32,
        lambda j: pin_cell[j : j + 1, :],
        lambda j: [pins[32 * i + j : 32 * i + j + 1, :] for i in range(4)],
    )
    removed = fold(acc, 2, 2) + others[...]
    degree = degree_ref[...]
    news, line = [], jnp.zeros((1, LANES), F32)
    lanes = iota((1, LANES), 1)
    sent_sums = [None] * 4
    for v in range(2):
        part = slice(16 * v, 16 * v + 16)
        r = start_ref[part, :]
        z = degree * r - removed[part]
        norm = lane_value(sums_ref[0:1, :], SUM_LANE + v)
        product = lane_value(energy, SUM_LANE + v)
        if first:
            p, q = r, z
        else:
            cross = lane_value(sums_ref[0:1, :], SUM_LANE + 2 + v)
            beta = norm / lane_value(old[0:1, :], v)
            product = product + beta * (2.0 * cross + beta * lane_value(old[0:1, :], 2 + v))
            p = r + beta * state[part, :]
            q = z + beta * state[32 + 16 * v : 48 + 16 * v, :]
        step = norm / product
        x = step * p
        if not first:
            x = x + state[64 + 16 * v : 80 + 16 * v, :]
        r = r - step * q
        if last:
            for t in range(TILES):
                positions_ref[v : v + 1, LANES * t : LANES * (t + 1)] = x[t : t + 1]
                residual_ref[v : v + 1, LANES * t : LANES * (t + 1)] = r[t : t + 1]
            continue
        residual_ref[part, :] = r
        for i, new in enumerate((p, q, x)):
            state_ref[32 * i + 16 * v : 32 * i + 16 * v + 16, :] = new
        news.append([r[t : t + 1] for t in range(TILES)])
        sent_sums[v], sent_sums[2 + v] = total(r * r), total(r * q)
        line = jnp.where(lanes == v, norm, jnp.where(lanes == 2 + v, product, line))
    if last:
        return
    old_ref[...] = jnp.broadcast_to(line, (8, LANES))
    put_gathered(news, sent_sums, cut_cells, pin_cell, pin_net, send_ref, kept_ref)


VMEM, SMEM, HBM = (pl.BlockSpec(memory_space=m) for m in (pltpu.VMEM, pltpu.SMEM, pltpu.HBM))


def call(kernel, shapes, scratch, cost, args, spaces=()):
    return pl.pallas_call(
        kernel,
        out_shape=[jax.ShapeDtypeStruct(s, F32) for s in shapes],
        in_specs=list(spaces) + [VMEM] * (len(args) - len(spaces)),
        out_specs=[VMEM] * len(shapes),
        scratch_shapes=[pltpu.VMEM(s, F32) if isinstance(s, tuple) else s for s in scratch],
        compiler_params=pltpu.CompilerParams(vmem_limit_bytes=32 << 20),
        cost_estimate=pl.CostEstimate(flops=cost, bytes_accessed=1 << 20, transcendentals=0),
    )(*args)


def stay(x):
    return pltpu.with_memory_space_constraint(x, pltpu.HBM)


def exchange(rows, height):
    return lax.all_to_all(
        rows.reshape(LANES, 1, height * LANES), AXES, split_axis=0, concat_axis=0, tiled=True
    ).reshape(LANES * height, LANES)


def swap(x):
    return lax.ppermute(x, "coord", [(0, 1), (1, 0)])


def per_device(
    right_side, anchor, blocks, tile_nbr, cut_cells, cut_weight, pin_cell, pin_net, star_weight
):
    cut_cells, cut_weight = cut_cells[0], cut_weight[0]
    pin_cell, pin_net = pin_cell.reshape(32, LANES), pin_net.reshape(32, LANES)
    star, anchor = star_weight.reshape(LANES, LANES), anchor.reshape(TILES, LANES)
    coord = lax.axis_index("coord")
    place = jnp.stack([coord, lax.axis_index("region") * 2 + coord]).astype(I32)
    nbr = tile_nbr.T
    peer = swap(right_side)
    send, residual, kept, blocks, cut_weight, anchor = call(
        first_kernel,
        [(384, LANES), (32, LANES), (256, LANES), blocks.shape, (LANES, LANES), (TILES, LANES)],
        [
            (2, TILES * LANES),
            pltpu.VMEM((128, LANES), I32),
            pltpu.VMEM((32, LANES), I32),
            pltpu.VMEM((32, LANES), I32),
            pltpu.SemaphoreType.DMA((7,)),
        ],
        1 << 24,
        tuple(stay(x) for x in (right_side, cut_cells, pin_cell, pin_net, blocks, cut_weight, anchor)),
        [HBM] * 7,
    )
    for iteration in range(ITERS):
        first, last = iteration == 0, iteration == ITERS - 1
        got = exchange(send, 3)
        if not first:
            peer = swap(residual)
        rows = 48 if first else 32
        scratch = [(128, LANES), (256, LANES), (128, LANES), (256, LANES), pltpu.VMEM((8, LANES), I32)]
        local_sum, back, share, *more = call(
            functools.partial(block_kernel, first),
            [(rows, LANES), (rows, LANES), (8, LANES)] + [(8, LANES)] * first,
            scratch + [(32, LANES)] if first else scratch,
            1 << 32,
            (place, residual, peer, nbr, blocks) + ((anchor, cut_weight, kept, star) if first else (degree,)),
            [SMEM],
        )
        back = swap(back)
        if first:
            net_weight = more[0]
        out, sums = call(
            functools.partial(owner_kernel, first),
            [(128, LANES), (8, LANES)],
            [(512 if first else 256, LANES)],
            1 << 26,
            (got, kept, cut_weight, net_weight, share),
        )
        returned = exchange(out, 1)
        args = (cut_cells, cut_weight, got, local_sum, back, sums)
        if first:
            others, degree = call(
                functools.partial(cut_kernel, True),
                [(32, LANES), (16, LANES)],
                [(128, LANES), (96, LANES)],
                1 << 31,
                args + (pin_cell, pin_net, star, anchor),
            )
        else:
            others = call(functools.partial(cut_kernel, False), [(32, LANES)], [], 1 << 31, args)[0]
        args = (pin_cell, returned, degree, others, sums, residual)
        if not first:
            args = args + (state, old)
        if last:
            shapes = [(2, TILES * LANES), (2, TILES * LANES)]
        else:
            args = args + (cut_cells, pin_net)
            shapes = [(384, LANES), (32, LANES), (96, LANES), (8, LANES), (256, LANES)]
        results = call(
            functools.partial(step_kernel, first, last), shapes, [(128, LANES)], 1 << 26, args
        )
        if last:
            return tuple(results)
        send, residual, state, old, kept = results


def solution(mesh):
    return jax.shard_map(
        per_device,
        mesh=mesh,
        in_specs=(
            P(None, AXES),
            P(AXES),
            P(AXES, None, None, None),
            P(AXES, None),
            P(AXES, None, None),
            P(AXES, None, None),
            P(AXES),
            P(AXES),
            P(),
        ),
        out_specs=(P(None, AXES), P(None, AXES)),
        check_vma=False,
    )
```

```python
import functools

import jax
import jax.numpy as jnp
from jax import lax
from jax.experimental import pallas as pl
from jax.experimental.pallas import tpu as pltpu
from jax.sharding import PartitionSpec as P

FANOUT = 32
BACKWARD_COST = 1 << 30
FORWARD_COST = 1 << 30
ITERS = 3
AXES = ("region", "coord")
LANES = 128
TILES = 16
F32 = jnp.float32
BF16 = jnp.bfloat16
I32 = jnp.int32
SUM_LANE = 96


def iota(shape, axis):
    return lax.broadcasted_iota(I32, shape, axis)


def split2(x):
    high = x.astype(BF16).astype(F32)
    return [high, (x - high).astype(BF16).astype(F32)]


def split3(x):
    high = x.astype(BF16).astype(F32)
    return [high] + split2(x - high)


def dot_nt(a, b):
    return lax.dot_general(a, b, (((1,), (1,)), ((), ())), preferred_element_type=F32)


def dot_nn(a, b):
    return lax.dot_general(a, b, (((1,), (0,)), ((), ())), preferred_element_type=F32)


def roll(x, shift):
    shift = shift % LANES
    return x if shift == 0 else pltpu.roll(x, shift, 1)


def total(x):
    return jnp.sum(jnp.sum(x, axis=0, keepdims=True), axis=1, keepdims=True)


def lane_value(row, lane):
    return jnp.sum(jnp.where(iota(row.shape, 1) == lane, row, 0.0), axis=1, keepdims=True)


def pick(tables, cells):
    low = cells & (LANES - 1)
    high = cells >> 7
    rows = [jnp.zeros(cells.shape, F32) for _ in tables]
    for tile in range(TILES):
        here = high == tile
        for v, table in enumerate(tables):
            wide = jnp.broadcast_to(table[tile], cells.shape)
            got = jnp.take_along_axis(wide, low, axis=1, mode="promise_in_bounds")
            rows[v] = jnp.where(here, got, rows[v])
    return rows


def one_hot(row, count):
    return jnp.where(iota((count, LANES), 0) == row, 1.0, 0.0).astype(BF16)


def add_rows(row_count, cell_row, value_rows):
    acc = None
    for j in range(0, row_count, 2):
        hots, masked = [], []
        for i in (j, j + 1):
            cells = cell_row(i)
            hots.append(one_hot(cells & (LANES - 1), LANES))
            here = iota((TILES, LANES), 0) == (cells >> 7)
            masked.append(
                jnp.concatenate([jnp.where(here, v, 0.0) for v in value_rows(i)], axis=0).astype(BF16)
            )
        part = dot_nt(jnp.concatenate(masked, axis=1), jnp.concatenate(hots, axis=1))
        acc = part if acc is None else acc + part
    return acc


def fold(acc, vectors, parts):
    size = vectors * TILES
    return sum(acc[i * size : (i + 1) * size] for i in range(parts))


def put_gathered(vectors, sums, cut_cells, pin_cell, pin_net, out_ref, kept_ref):
    lane = iota((32, LANES), 1)
    tail = jnp.zeros((1, LANES), F32)
    for i, s in enumerate(sums):
        tail = jnp.where(iota((1, LANES), 1) == SUM_LANE + i, s, tail)
    groups = [pick(vectors, pin_cell[8 * h : 8 * h + 8, :]) for h in range(4)]
    gx, gy = (jnp.concatenate([g[v] for g in groups], axis=0) for v in range(2))
    net = (pin_net[...] & (LANES - 1)).astype(F32)
    for q in range(4):
        row = jnp.where(
            lane < 32,
            roll(gx, -32 * q),
            jnp.where(
                lane < 64,
                roll(gy, 32 - 32 * q),
                jnp.where(lane < 96, roll(net, 64 - 32 * q), tail),
            ),
        )
        out_ref[pl.ds(3 * q + 2, 32, stride=12), :] = row
    for g in range(16):
        gx, gy = pick(vectors, cut_cells[pl.ds(8 * g, 8), :])
        out_ref[pl.ds(24 * g, 8, stride=3), :] = gx
        out_ref[pl.ds(24 * g + 1, 8, stride=3), :] = gy
        kept_ref[pl.ds(8 * g, 8), :] = gx
        kept_ref[pl.ds(128 + 8 * g, 8), :] = gy


def dense(rows, offset):
    lane = iota((32, LANES), 1)
    out = roll(rows[0], -offset)
    for q in range(1, 4):
        out = jnp.where(lane >= 32 * q, roll(rows[q], 32 * q - offset), out)
    return out


def first_kernel(right_hbm, cells_hbm, pin_cell_hbm, pin_net_hbm, blocks_hbm, weight_hbm, anchor_hbm,
                 send_ref, start_ref, kept_ref, blocks_ref, weight_ref, anchor_ref,
                 right_ref, cut_cells, pin_cell, pin_net, sems):
    copies = [
        pltpu.make_async_copy(source, target, sems.at[i])
        for i, (source, target) in enumerate(
            (
                (right_hbm, right_ref),
                (pin_cell_hbm, pin_cell),
                (pin_net_hbm, pin_net),
                (cells_hbm, cut_cells),
                (weight_hbm, weight_ref),
                (anchor_hbm, anchor_ref),
                (blocks_hbm, blocks_ref),
            )
        )
    ]
    for copy in copies:
        copy.start()
    for copy in copies[:4]:
        copy.wait()
    tables = [
        [right_ref[v : v + 1, LANES * t : LANES * (t + 1)] for t in range(TILES)] for v in range(2)
    ]
    for v in range(2):
        for t in range(TILES):
            start_ref[TILES * v + t : TILES * v + t + 1, :] = tables[v][t]
    r = start_ref[...]
    sums = [total(r[16 * v : 16 * v + 16] * r[16 * v : 16 * v + 16]) for v in range(2)]
    put_gathered(tables, sums, cut_cells, pin_cell, pin_net, send_ref, kept_ref)
    for copy in copies[4:]:
        copy.wait()


def tile_names(nbr, names):
    names[...] = jnp.zeros(names.shape, I32)
    for k in range(2):
        names[k : k + 1, 0:TILES] = nbr[k : k + 1, :]
    return [jnp.where(iota((LANES, LANES), 0) == names[k : k + 1, :], 1.0, 0.0) for k in range(2)]


def block_parts(blocks, t):
    pair = jnp.concatenate([blocks[t, 0], blocks[t, 1]], axis=1)
    high = pair.astype(BF16)
    return high, (pair - high.astype(F32)).astype(BF16)


def tile_rows(ref, at, v):
    if v == 2:
        return ref[pl.ds(at + 4, 16, stride=8), :]
    return ref[pl.ds(at + v, 16, stride=8), :] + ref[pl.ds(at + v + 2, 16, stride=8), :]


def backward_kernel(first, own_ref, side, nbr, blocks, *refs):
    if first:
        place, star, local_ref, back_ref, ones_ref, net_weight_ref, near, got, names = refs
        net_weight_ref[...] = jnp.broadcast_to(star[pl.ds(place[1], 1), :], (8, LANES))
    else:
        local_ref, back_ref, near, got, names = refs
    spread_rows = [h[:32].astype(BF16) for h in tile_names(nbr, names)]
    near[...] = jnp.ones(near.shape, F32)
    for v in range(2):
        for i, part in enumerate(split2(own_ref[16 * v : 16 * v + 16, :])):
            near[pl.ds(2 * i + v, 16, stride=8), :] = part
    for t in range(TILES):
        a = near[8 * t : 8 * t + 8, :].astype(BF16)
        high, low = block_parts(blocks, t)
        back = dot_nn(a, high) + dot_nn(a, low)
        for k in range(2):
            got[128 * k + 8 * t : 128 * k + 8 * t + 8, :] = back[:, LANES * k : LANES * (k + 1)]
    filler = jnp.zeros((112, LANES), F32)
    upper = side[0:1, :] > 0.5
    for v in range(3 if first else 2):
        spread = sum(
            dot_nn(spread_rows[k], jnp.concatenate([part, filler], axis=0).astype(BF16))
            for k in range(2)
            for part in split3(tile_rows(got, 128 * k, v))
        )
        lower, higher = spread[:16], spread[16:]
        local_ref[16 * v : 16 * v + 16, :] = jnp.where(upper, higher, lower)
        back_ref[16 * v : 16 * v + 16, :] = jnp.where(upper, lower, higher)
        if v == 2:
            ones_ref[...] = spread


def forward_kernel(first, own_ref, peer_ref, side, nbr, blocks, before_ref, *refs):
    if first:
        ones_ref, anchor, cut_weight, kept, local_ref, share_ref, far, got, names, peers = refs
        for v in range(2):
            for t in range(TILES):
                peers[TILES * v + t : TILES * v + t + 1, :] = peer_ref[v : v + 1, LANES * t : LANES * (t + 1)]
        peer_ref = peers
    else:
        degree, local_ref, share_ref, far, got, names = refs
    upper = side[0:1, :] > 0.5
    pick_rows = jnp.concatenate([h.T[:16] for h in tile_names(nbr, names)], axis=0).astype(BF16)
    far[...] = jnp.ones(far.shape, F32)
    zeros = jnp.zeros((96, LANES), F32)
    wholes = []
    for v in range(2):
        o, p = own_ref[16 * v : 16 * v + 16, :], peer_ref[16 * v : 16 * v + 16, :]
        whole = jnp.concatenate([jnp.where(upper, p, o), jnp.where(upper, o, p)], axis=0)
        wholes.append(whole)
        for i, part in enumerate(split2(whole)):
            picked = dot_nn(pick_rows, jnp.concatenate([part, zeros], axis=0).astype(BF16))
            for k in range(2):
                far[pl.ds(128 * k + 2 * i + v, 16, stride=8), :] = picked[16 * k : 16 * k + 16]
    for t in range(TILES):
        b = jnp.concatenate(
            [far[128 * k + 8 * t : 128 * k + 8 * t + 8, :] for k in range(2)], axis=1
        ).astype(BF16)
        high, low = block_parts(blocks, t)
        got[8 * t : 8 * t + 8, :] = dot_nt(b, high) + dot_nt(b, low)
    ahead = [tile_rows(got, 0, v) for v in range(3 if first else 2)]
    for v, forward in enumerate(ahead):
        local_ref[16 * v : 16 * v + 16, :] = before_ref[16 * v : 16 * v + 16, :] + forward
    for v in range(2):
        r = own_ref[16 * v : 16 * v + 16, :]
        if first:
            square = r * (r * (anchor[...] + ahead[2]) - 2.0 * ahead[v])
            line = jnp.sum(square, axis=0, keepdims=True)
            line = line + jnp.sum(wholes[v] * wholes[v] * ones_ref[...], axis=0, keepdims=True)
            cut = kept[128 * v : 128 * v + 128, :]
            line = line + jnp.sum(cut_weight[...] * cut * cut, axis=0, keepdims=True)
        else:
            line = jnp.sum(r * (r * degree[...] - 2.0 * ahead[v]), axis=0, keepdims=True)
        share_ref[v : v + 1, :] = line
    share_ref[2:8, :] = jnp.zeros((6, LANES), F32)


def owner_kernel(first, got, kept, cut_weight, net_weight, share_ref, out_ref, sums_ref, rows):
    height = 16 if first else 8
    pin_rows = [got[pl.ds(3 * q + 2, 32, stride=12), :] for q in range(4)]
    sums = sum(jnp.sum(row, axis=0, keepdims=True) for row in pin_rows)
    sums_ref[...] = jnp.broadcast_to(sums, (8, LANES))
    nets = dense(pin_rows, 64).astype(I32)
    rows[...] = jnp.zeros(rows.shape, F32)
    for v in range(2):
        pins = dense(pin_rows, 32 * v)
        for i, part in enumerate(split3(pins)):
            rows[pl.ds(2 * i + v, 32, stride=height), :] = part
        if first:
            for i, part in enumerate(split3(pins * pins)):
                rows[pl.ds(8 + 2 * i + v, 32, stride=height), :] = part
    acc = None
    for j in range(0, 32, 2):
        hot = jnp.concatenate([one_hot(nets[i : i + 1], LANES) for i in (j, j + 1)], axis=1)
        left = jnp.concatenate(
            [rows[height * i : height * i + height, :] for i in (j, j + 1)], axis=1
        )
        part = dot_nt(left.astype(BF16), hot)
        acc = part if acc is None else acc + part
    weight = net_weight[0:1, :]
    totals = [acc[v : v + 1] + acc[v + 2 : v + 3] + acc[v + 4 : v + 5] for v in range(2)]
    centres = [weight * (1.0 / FANOUT) * t for t in totals]
    tail = jnp.zeros((1, LANES), F32)
    for v in range(2):
        line = share_ref[v : v + 1, :] - centres[v] * totals[v]
        if first:
            squares = acc[8 + v : 9 + v] + acc[10 + v : 11 + v] + acc[12 + v : 13 + v]
            line = line + weight * squares
        cut = cut_weight[...] * (kept[128 * v : 128 * v + 128, :] * got[pl.ds(v, 128, stride=3), :])
        line = line - jnp.sum(cut, axis=0, keepdims=True)
        tail = jnp.where(
            iota((1, LANES), 1) == SUM_LANE + v, jnp.sum(line, axis=1, keepdims=True), tail
        )
    lane = iota((8, LANES), 1)
    tables = [jnp.broadcast_to(c, (8, LANES)) for c in centres]
    for g in range(16):
        row = got[pl.ds(24 * g + 2, 8, stride=3), :]
        index = jnp.where(lane < 32, roll(row, -64), roll(row, -32)).astype(I32) & (LANES - 1)
        gx, gy = (
            jnp.take_along_axis(t, index, axis=1, mode="promise_in_bounds") for t in tables
        )
        out_ref[pl.ds(8 * g, 8), :] = jnp.where(
            lane < 32, gx, jnp.where(lane < 64, gy, jnp.where(lane < 96, 0.0, tail))
        )


def cut_kernel(first, cut_cells, cut_weight, got, local_ref, sums_ref, *refs):
    del sums_ref

    def values(j):
        weight = cut_weight[j : j + 1, :]
        parts = [split2(weight * got[3 * j + v : 3 * j + v + 1, :]) for v in range(2)]
        moved = [parts[0][0], parts[1][0], parts[0][1], parts[1][1]]
        return moved + split3(weight) if first else moved

    acc = add_rows(128, lambda j: cut_cells[j : j + 1, :], values)
    if not first:
        (out_ref,) = refs
        out_ref[...] = fold(acc, 2, 2) + local_ref[...]
        return
    pin_cell, pin_net, star, anchor, out_ref, degree_ref, rows_ref, pins_ref = refs
    out_ref[...] = fold(acc[:64], 2, 2) + local_ref[0:32, :]
    net = pin_net[...] & (LANES - 1)
    for q in range(4):
        rows_ref[pl.ds(32 * q, 32), :] = jnp.take_along_axis(
            star[pl.ds(q, 32, stride=4), :], roll(net, -32 * q), axis=1, mode="promise_in_bounds"
        )
    weight = dense([rows_ref[pl.ds(32 * q, 32), :] for q in range(4)], 0)
    for i, part in enumerate(split3(weight)):
        pins_ref[pl.ds(32 * i, 32), :] = part
    pinned = add_rows(
        32,
        lambda j: pin_cell[j : j + 1, :],
        lambda j: [pins_ref[32 * i + j : 32 * i + j + 1, :] for i in range(3)],
    )
    degree_ref[...] = (
        anchor[...] + fold(acc[64:], 1, 3) + fold(pinned, 1, 3) + local_ref[32:48, :]
    )


def step_kernel(first, last, pin_cell, got, degree_in, others, back_ref, sums_ref, start_ref, *refs):
    refs = list(refs)
    state, old = (None, None) if first else (refs.pop(0), refs.pop(0))
    if last:
        positions_ref, residual_ref, pins = refs
    elif first:
        cut_cells, pin_net, send_ref, residual_ref, state_ref, old_ref, kept_ref, degree_ref, pins = refs
    else:
        cut_cells, pin_net, send_ref, residual_ref, state_ref, old_ref, kept_ref, pins = refs
    pin_rows = [got[pl.ds(q, 32, stride=4), :] for q in range(4)]
    energy = sum(jnp.sum(row, axis=0, keepdims=True) for row in pin_rows)
    for v in range(2):
        for i, part in enumerate(split2(dense(pin_rows, 32 * v))):
            pins[pl.ds(32 * (2 * i + v), 32), :] = part
    acc = add_rows(
        32,
        lambda j: pin_cell[j : j + 1, :],
        lambda j: [pins[32 * i + j : 32 * i + j + 1, :] for i in range(4)],
    )
    removed = fold(acc, 2, 2) + others[...] + back_ref[0:32, :]
    degree = degree_in[...]
    if first:
        degree = degree + back_ref[32:48, :]
        degree_ref[...] = degree
    news, line = [], jnp.zeros((1, LANES), F32)
    lanes = iota((1, LANES), 1)
    sent_sums = [None] * 4
    for v in range(2):
        part = slice(16 * v, 16 * v + 16)
        r = start_ref[part, :]
        z = degree * r - removed[part]
        norm = lane_value(sums_ref[0:1, :], SUM_LANE + v)
        product = lane_value(energy, SUM_LANE + v)
        if first:
            p, q = r, z
        else:
            cross = lane_value(sums_ref[0:1, :], SUM_LANE + 2 + v)
            beta = norm / lane_value(old[0:1, :], v)
            product = product + beta * (2.0 * cross + beta * lane_value(old[0:1, :], 2 + v))
            p = r + beta * state[part, :]
            q = z + beta * state[32 + 16 * v : 48 + 16 * v, :]
        step = norm / product
        x = step * p
        if not first:
            x = x + state[64 + 16 * v : 80 + 16 * v, :]
        r = r - step * q
        if last:
            for t in range(TILES):
                positions_ref[v : v + 1, LANES * t : LANES * (t + 1)] = x[t : t + 1]
                residual_ref[v : v + 1, LANES * t : LANES * (t + 1)] = r[t : t + 1]
            continue
        residual_ref[part, :] = r
        for i, new in enumerate((p, q, x)):
            state_ref[32 * i + 16 * v : 32 * i + 16 * v + 16, :] = new
        news.append([r[t : t + 1] for t in range(TILES)])
        sent_sums[v], sent_sums[2 + v] = total(r * r), total(r * q)
        line = jnp.where(lanes == v, norm, jnp.where(lanes == 2 + v, product, line))
    if last:
        return
    old_ref[...] = jnp.broadcast_to(line, (8, LANES))
    put_gathered(news, sent_sums, cut_cells, pin_cell, pin_net, send_ref, kept_ref)


VMEM, SMEM, HBM = (pl.BlockSpec(memory_space=m) for m in (pltpu.VMEM, pltpu.SMEM, pltpu.HBM))


def call(kernel, shapes, scratch, cost, args, spaces=()):
    return pl.pallas_call(
        kernel,
        out_shape=[jax.ShapeDtypeStruct(s, F32) for s in shapes],
        in_specs=list(spaces) + [VMEM] * (len(args) - len(spaces)),
        out_specs=[VMEM] * len(shapes),
        scratch_shapes=[pltpu.VMEM(s, F32) if isinstance(s, tuple) else s for s in scratch],
        compiler_params=pltpu.CompilerParams(vmem_limit_bytes=32 << 20),
        cost_estimate=pl.CostEstimate(flops=cost, bytes_accessed=1 << 20, transcendentals=0),
    )(*args)


def stay(x):
    return pltpu.with_memory_space_constraint(x, pltpu.HBM)


def exchange(rows, height):
    return lax.all_to_all(
        rows.reshape(LANES, 1, height * LANES), AXES, split_axis=0, concat_axis=0, tiled=True
    ).reshape(LANES * height, LANES)


def swap(x):
    return lax.ppermute(x, "coord", [(0, 1), (1, 0)])


def per_device(
    right_side, anchor, blocks, tile_nbr, cut_cells, cut_weight, pin_cell, pin_net, star_weight
):
    cut_cells, cut_weight = cut_cells[0], cut_weight[0]
    pin_cell, pin_net = pin_cell.reshape(32, LANES), pin_net.reshape(32, LANES)
    star, anchor = star_weight.reshape(LANES, LANES), anchor.reshape(TILES, LANES)
    coord = lax.axis_index("coord")
    place = jnp.stack([coord, lax.axis_index("region") * 2 + coord]).astype(I32)
    side = jnp.full((8, LANES), coord).astype(F32)
    nbr = tile_nbr.T
    peer = swap(right_side)
    send, residual, kept, blocks, cut_weight, anchor = call(
        first_kernel,
        [(384, LANES), (32, LANES), (256, LANES), blocks.shape, (LANES, LANES), (TILES, LANES)],
        [
            (2, TILES * LANES),
            pltpu.VMEM((128, LANES), I32),
            pltpu.VMEM((32, LANES), I32),
            pltpu.VMEM((32, LANES), I32),
            pltpu.SemaphoreType.DMA((7,)),
        ],
        1 << 24,
        tuple(stay(x) for x in (right_side, cut_cells, pin_cell, pin_net, blocks, cut_weight, anchor)),
        [HBM] * 7,
    )
    for iteration in range(ITERS):
        first, last = iteration == 0, iteration == ITERS - 1
        got = exchange(send, 3)
        if not first:
            peer = swap(residual)
        rows = 48 if first else 32
        scratch = [(256, LANES), (128, LANES), pltpu.VMEM((8, LANES), I32)]
        local_sum, back, *more = call(
            functools.partial(backward_kernel, first),
            [(rows, LANES), (rows, LANES)] + [(32, LANES), (8, LANES)] * first,
            [(128, LANES), (256, LANES), pltpu.VMEM((8, LANES), I32)],
            BACKWARD_COST,
            (residual, side, nbr, blocks) + ((place, star) if first else ()),
            [VMEM] * 4 + [SMEM] * first,
        )
        if first:
            ones, net_weight = more
        local_sum, share = call(
            functools.partial(forward_kernel, first),
            [(rows, LANES), (8, LANES)],
            scratch + [(32, LANES)] * first,
            FORWARD_COST,
            (residual, peer, side, nbr, blocks, local_sum)
            + ((ones, anchor, cut_weight, kept) if first else (degree,)),
        )
        out, sums = call(
            functools.partial(owner_kernel, first),
            [(128, LANES), (8, LANES)],
            [(512 if first else 256, LANES)],
            1 << 26,
            (got, kept, cut_weight, net_weight, share),
        )
        returned = exchange(out, 1)
        back, sums = lax.optimization_barrier((back, sums))
        back = swap(back)
        args = (cut_cells, cut_weight, got, local_sum, sums)
        if first:
            others, degree = call(
                functools.partial(cut_kernel, True),
                [(32, LANES), (16, LANES)],
                [(128, LANES), (96, LANES)],
                1 << 31,
                args + (pin_cell, pin_net, star, anchor),
            )
        else:
            others = call(functools.partial(cut_kernel, False), [(32, LANES)], [], 1 << 31, args)[0]
        args = (pin_cell, returned, degree, others, back, sums, residual)
        if not first:
            args = args + (state, old)
        if last:
            shapes = [(2, TILES * LANES), (2, TILES * LANES)]
        else:
            args = args + (cut_cells, pin_net)
            shapes = [(384, LANES), (32, LANES), (96, LANES), (8, LANES), (256, LANES)]
            shapes = shapes + [(16, LANES)] * first
        results = call(
            functools.partial(step_kernel, first, last), shapes, [(128, LANES)], 1 << 26, args
        )
        if last:
            return tuple(results)
        send, residual, state, old, kept, *more = results
        if first:
            degree = more[0]


def solution(mesh):
    return jax.shard_map(
        per_device,
        mesh=mesh,
        in_specs=(
            P(None, AXES),
            P(AXES),
            P(AXES, None, None, None),
            P(AXES, None),
            P(AXES, None, None),
            P(AXES, None, None),
            P(AXES),
            P(AXES),
            P(),
        ),
        out_specs=(P(None, AXES), P(None, AXES)),
        check_vma=False,
    )
```

```python
import functools

import jax
import jax.numpy as jnp
from jax import lax
from jax.experimental import pallas as pl
from jax.experimental.pallas import tpu as pltpu
from jax.sharding import PartitionSpec as P

FANOUT = 32
BACKWARD_COST = 1 << 30
FORWARD_COST = 1 << 30
ITERS = 3
AXES = ("region", "coord")
LANES = 128
TILES = 16
F32 = jnp.float32
BF16 = jnp.bfloat16
I32 = jnp.int32
SUM_LANE = 96


def iota(shape, axis):
    return lax.broadcasted_iota(I32, shape, axis)


def split2(x):
    high = x.astype(BF16).astype(F32)
    return [high, (x - high).astype(BF16).astype(F32)]


def split3(x):
    high = x.astype(BF16).astype(F32)
    return [high] + split2(x - high)


def dot_nt(a, b):
    return lax.dot_general(a, b, (((1,), (1,)), ((), ())), preferred_element_type=F32)


def dot_nn(a, b):
    return lax.dot_general(a, b, (((1,), (0,)), ((), ())), preferred_element_type=F32)


def roll(x, shift):
    shift = shift % LANES
    return x if shift == 0 else pltpu.roll(x, shift, 1)


def total(x):
    return jnp.sum(jnp.sum(x, axis=0, keepdims=True), axis=1, keepdims=True)


def lane_value(row, lane):
    return jnp.sum(jnp.where(iota(row.shape, 1) == lane, row, 0.0), axis=1, keepdims=True)


def pick(tables, cells):
    low = cells & (LANES - 1)
    high = cells >> 7
    rows = [jnp.zeros(cells.shape, F32) for _ in tables]
    for tile in range(TILES):
        here = high == tile
        for v, table in enumerate(tables):
            wide = jnp.broadcast_to(table[tile], cells.shape)
            got = jnp.take_along_axis(wide, low, axis=1, mode="promise_in_bounds")
            rows[v] = jnp.where(here, got, rows[v])
    return rows


def one_hot(row, count):
    return jnp.where(iota((count, LANES), 0) == row, 1.0, 0.0).astype(BF16)


def add_rows(row_count, cell_row, value_rows):
    acc = None
    for j in range(0, row_count, 2):
        hots, masked = [], []
        for i in (j, j + 1):
            cells = cell_row(i)
            hots.append(one_hot(cells & (LANES - 1), LANES))
            here = iota((TILES, LANES), 0) == (cells >> 7)
            masked.append(
                jnp.concatenate([jnp.where(here, v, 0.0) for v in value_rows(i)], axis=0).astype(BF16)
            )
        part = dot_nt(jnp.concatenate(masked, axis=1), jnp.concatenate(hots, axis=1))
        acc = part if acc is None else acc + part
    return acc


def fold(acc, vectors, parts):
    size = vectors * TILES
    return sum(acc[i * size : (i + 1) * size] for i in range(parts))


def put_gathered(vectors, sums, cut_cells, pin_cell, pin_net, out_ref, kept_ref):
    lane = iota((32, LANES), 1)
    tail = jnp.zeros((1, LANES), F32)
    for i, s in enumerate(sums):
        tail = jnp.where(iota((1, LANES), 1) == SUM_LANE + i, s, tail)
    groups = [pick(vectors, pin_cell[8 * h : 8 * h + 8, :]) for h in range(4)]
    gx, gy = (jnp.concatenate([g[v] for g in groups], axis=0) for v in range(2))
    net = (pin_net[...] & (LANES - 1)).astype(F32)
    for q in range(4):
        row = jnp.where(
            lane < 32,
            roll(gx, -32 * q),
            jnp.where(
                lane < 64,
                roll(gy, 32 - 32 * q),
                jnp.where(lane < 96, roll(net, 64 - 32 * q), tail),
            ),
        )
        out_ref[pl.ds(3 * q + 2, 32, stride=12), :] = row
    for g in range(16):
        gx, gy = pick(vectors, cut_cells[pl.ds(8 * g, 8), :])
        out_ref[pl.ds(24 * g, 8, stride=3), :] = gx
        out_ref[pl.ds(24 * g + 1, 8, stride=3), :] = gy
        kept_ref[pl.ds(8 * g, 8), :] = gx
        kept_ref[pl.ds(128 + 8 * g, 8), :] = gy


def dense(rows, offset):
    lane = iota((32, LANES), 1)
    out = roll(rows[0], -offset)
    for q in range(1, 4):
        out = jnp.where(lane >= 32 * q, roll(rows[q], 32 * q - offset), out)
    return out


def first_kernel(right_hbm, cells_hbm, pin_cell_hbm, pin_net_hbm, blocks_hbm, weight_hbm, anchor_hbm,
                 send_ref, start_ref, kept_ref, blocks_ref, weight_ref, anchor_ref,
                 right_ref, cut_cells, pin_cell, pin_net, sems):
    copies = [
        pltpu.make_async_copy(source, target, sems.at[i])
        for i, (source, target) in enumerate(
            (
                (right_hbm, right_ref),
                (pin_cell_hbm, pin_cell),
                (pin_net_hbm, pin_net),
                (cells_hbm, cut_cells),
                (weight_hbm, weight_ref),
                (anchor_hbm, anchor_ref),
                (blocks_hbm, blocks_ref),
            )
        )
    ]
    for copy in copies:
        copy.start()
    for copy in copies[:4]:
        copy.wait()
    tables = [
        [right_ref[v : v + 1, LANES * t : LANES * (t + 1)] for t in range(TILES)] for v in range(2)
    ]
    for v in range(2):
        for t in range(TILES):
            start_ref[TILES * v + t : TILES * v + t + 1, :] = tables[v][t]
    r = start_ref[...]
    sums = [total(r[16 * v : 16 * v + 16] * r[16 * v : 16 * v + 16]) for v in range(2)]
    put_gathered(tables, sums, cut_cells, pin_cell, pin_net, send_ref, kept_ref)
    for copy in copies[4:]:
        copy.wait()


def tile_names(nbr, names):
    names[...] = jnp.zeros(names.shape, I32)
    for k in range(2):
        names[k : k + 1, 0:TILES] = nbr[k : k + 1, :]
    return [jnp.where(iota((LANES, LANES), 0) == names[k : k + 1, :], 1.0, 0.0) for k in range(2)]


def block_parts(blocks, t):
    pair = jnp.concatenate([blocks[t, 0], blocks[t, 1]], axis=1)
    high = pair.astype(BF16)
    return high, (pair - high.astype(F32)).astype(BF16)


def tile_rows(ref, at, v):
    if v == 2:
        return ref[pl.ds(at + 4, 16, stride=8), :]
    return ref[pl.ds(at + v, 16, stride=8), :] + ref[pl.ds(at + v + 2, 16, stride=8), :]


def backward_kernel(first, own_ref, side, nbr, blocks, *refs):
    if first:
        place, star, local_ref, back_ref, ones_ref, net_weight_ref, near, got, names = refs
        net_weight_ref[...] = jnp.broadcast_to(star[pl.ds(place[1], 1), :], (8, LANES))
    else:
        local_ref, back_ref, near, got, names = refs
    spread_rows = [h[:32].astype(BF16) for h in tile_names(nbr, names)]
    near[...] = jnp.ones(near.shape, F32)
    for v in range(2):
        for i, part in enumerate(split2(own_ref[16 * v : 16 * v + 16, :])):
            near[pl.ds(2 * i + v, 16, stride=8), :] = part
    for t in range(TILES):
        a = near[8 * t : 8 * t + 8, :].astype(BF16)
        high, low = block_parts(blocks, t)
        back = dot_nn(a, high) + dot_nn(a, low)
        for k in range(2):
            got[128 * k + 8 * t : 128 * k + 8 * t + 8, :] = back[:, LANES * k : LANES * (k + 1)]
    filler = jnp.zeros((112, LANES), F32)
    upper = side[0:1, :] > 0.5
    for v in range(3 if first else 2):
        spread = sum(
            dot_nn(spread_rows[k], jnp.concatenate([part, filler], axis=0).astype(BF16))
            for k in range(2)
            for part in split3(tile_rows(got, 128 * k, v))
        )
        lower, higher = spread[:16], spread[16:]
        local_ref[16 * v : 16 * v + 16, :] = jnp.where(upper, higher, lower)
        back_ref[16 * v : 16 * v + 16, :] = jnp.where(upper, lower, higher)
        if v == 2:
            ones_ref[...] = spread


def forward_kernel(first, own_ref, peer_ref, side, nbr, blocks, before_ref, *refs):
    if first:
        ones_ref, anchor, cut_weight, kept, local_ref, share_ref, far, got, names = refs
    else:
        degree, local_ref, share_ref, far, got, names = refs
    upper = side[0:1, :] > 0.5
    pick_rows = jnp.concatenate([h.T[:16] for h in tile_names(nbr, names)], axis=0).astype(BF16)
    far[...] = jnp.ones(far.shape, F32)
    zeros = jnp.zeros((96, LANES), F32)
    wholes = []
    for v in range(2):
        o, p = own_ref[16 * v : 16 * v + 16, :], peer_ref[16 * v : 16 * v + 16, :]
        whole = jnp.concatenate([jnp.where(upper, p, o), jnp.where(upper, o, p)], axis=0)
        wholes.append(whole)
        for i, part in enumerate(split2(whole)):
            picked = dot_nn(pick_rows, jnp.concatenate([part, zeros], axis=0).astype(BF16))
            for k in range(2):
                far[pl.ds(128 * k + 2 * i + v, 16, stride=8), :] = picked[16 * k : 16 * k + 16]
    for t in range(TILES):
        b = jnp.concatenate(
            [far[128 * k + 8 * t : 128 * k + 8 * t + 8, :] for k in range(2)], axis=1
        ).astype(BF16)
        high, low = block_parts(blocks, t)
        got[8 * t : 8 * t + 8, :] = dot_nt(b, high) + dot_nt(b, low)
    ahead = [tile_rows(got, 0, v) for v in range(3 if first else 2)]
    for v, forward in enumerate(ahead):
        local_ref[16 * v : 16 * v + 16, :] = before_ref[16 * v : 16 * v + 16, :] + forward
    for v in range(2):
        r = own_ref[16 * v : 16 * v + 16, :]
        if first:
            square = r * (r * (anchor[...] + ahead[2]) - 2.0 * ahead[v])
            line = jnp.sum(square, axis=0, keepdims=True)
            line = line + jnp.sum(wholes[v] * wholes[v] * ones_ref[...], axis=0, keepdims=True)
            cut = kept[128 * v : 128 * v + 128, :]
            line = line + jnp.sum(cut_weight[...] * cut * cut, axis=0, keepdims=True)
        else:
            line = jnp.sum(r * (r * degree[...] - 2.0 * ahead[v]), axis=0, keepdims=True)
        share_ref[v : v + 1, :] = line
    share_ref[2:8, :] = jnp.zeros((6, LANES), F32)


def owner_kernel(first, got, kept, cut_weight, net_weight, share_ref, out_ref, sums_ref, rows):
    height = 16 if first else 8
    pin_rows = [got[pl.ds(3 * q + 2, 32, stride=12), :] for q in range(4)]
    sums = sum(jnp.sum(row, axis=0, keepdims=True) for row in pin_rows)
    sums_ref[...] = jnp.broadcast_to(sums, (8, LANES))
    nets = dense(pin_rows, 64).astype(I32)
    rows[...] = jnp.zeros(rows.shape, F32)
    for v in range(2):
        pins = dense(pin_rows, 32 * v)
        for i, part in enumerate(split3(pins)):
            rows[pl.ds(2 * i + v, 32, stride=height), :] = part
        if first:
            for i, part in enumerate(split3(pins * pins)):
                rows[pl.ds(8 + 2 * i + v, 32, stride=height), :] = part
    acc = None
    for j in range(0, 32, 2):
        hot = jnp.concatenate([one_hot(nets[i : i + 1], LANES) for i in (j, j + 1)], axis=1)
        left = jnp.concatenate(
            [rows[height * i : height * i + height, :] for i in (j, j + 1)], axis=1
        )
        part = dot_nt(left.astype(BF16), hot)
        acc = part if acc is None else acc + part
    weight = net_weight[0:1, :]
    totals = [acc[v : v + 1] + acc[v + 2 : v + 3] + acc[v + 4 : v + 5] for v in range(2)]
    centres = [weight * (1.0 / FANOUT) * t for t in totals]
    tail = jnp.zeros((1, LANES), F32)
    for v in range(2):
        line = share_ref[v : v + 1, :] - centres[v] * totals[v]
        if first:
            squares = acc[8 + v : 9 + v] + acc[10 + v : 11 + v] + acc[12 + v : 13 + v]
            line = line + weight * squares
        cut = cut_weight[...] * (kept[128 * v : 128 * v + 128, :] * got[pl.ds(v, 128, stride=3), :])
        line = line - jnp.sum(cut, axis=0, keepdims=True)
        tail = jnp.where(
            iota((1, LANES), 1) == SUM_LANE + v, jnp.sum(line, axis=1, keepdims=True), tail
        )
    lane = iota((8, LANES), 1)
    tables = [jnp.broadcast_to(c, (8, LANES)) for c in centres]
    for g in range(16):
        row = got[pl.ds(24 * g + 2, 8, stride=3), :]
        index = jnp.where(lane < 32, roll(row, -64), roll(row, -32)).astype(I32) & (LANES - 1)
        gx, gy = (
            jnp.take_along_axis(t, index, axis=1, mode="promise_in_bounds") for t in tables
        )
        out_ref[pl.ds(8 * g, 8), :] = jnp.where(
            lane < 32, gx, jnp.where(lane < 64, gy, jnp.where(lane < 96, 0.0, tail))
        )


def cut_kernel(first, cut_cells, cut_weight, got, local_ref, sums_ref, *refs):
    del sums_ref

    def values(j):
        weight = cut_weight[j : j + 1, :]
        parts = [split2(weight * got[3 * j + v : 3 * j + v + 1, :]) for v in range(2)]
        moved = [parts[0][0], parts[1][0], parts[0][1], parts[1][1]]
        return moved + split3(weight) if first else moved

    acc = add_rows(128, lambda j: cut_cells[j : j + 1, :], values)
    if not first:
        (out_ref,) = refs
        out_ref[...] = fold(acc, 2, 2) + local_ref[...]
        return
    pin_cell, pin_net, star, anchor, out_ref, degree_ref, rows_ref, pins_ref = refs
    out_ref[...] = fold(acc[:64], 2, 2) + local_ref[0:32, :]
    net = pin_net[...] & (LANES - 1)
    for q in range(4):
        rows_ref[pl.ds(32 * q, 32), :] = jnp.take_along_axis(
            star[pl.ds(q, 32, stride=4), :], roll(net, -32 * q), axis=1, mode="promise_in_bounds"
        )
    weight = dense([rows_ref[pl.ds(32 * q, 32), :] for q in range(4)], 0)
    for i, part in enumerate(split3(weight)):
        pins_ref[pl.ds(32 * i, 32), :] = part
    pinned = add_rows(
        32,
        lambda j: pin_cell[j : j + 1, :],
        lambda j: [pins_ref[32 * i + j : 32 * i + j + 1, :] for i in range(3)],
    )
    degree_ref[...] = (
        anchor[...] + fold(acc[64:], 1, 3) + fold(pinned, 1, 3) + local_ref[32:48, :]
    )


def step_kernel(first, last, pin_cell, got, degree_in, others, back_ref, sums_ref, start_ref, *refs):
    refs = list(refs)
    state, old = (None, None) if first else (refs.pop(0), refs.pop(0))
    if last:
        positions_ref, residual_ref, pins = refs
    elif first:
        cut_cells, pin_net, send_ref, residual_ref, state_ref, old_ref, kept_ref, degree_ref, pins = refs
    else:
        cut_cells, pin_net, send_ref, residual_ref, state_ref, old_ref, kept_ref, pins = refs
    pin_rows = [got[pl.ds(q, 32, stride=4), :] for q in range(4)]
    energy = sum(jnp.sum(row, axis=0, keepdims=True) for row in pin_rows)
    for v in range(2):
        for i, part in enumerate(split2(dense(pin_rows, 32 * v))):
            pins[pl.ds(32 * (2 * i + v), 32), :] = part
    acc = add_rows(
        32,
        lambda j: pin_cell[j : j + 1, :],
        lambda j: [pins[32 * i + j : 32 * i + j + 1, :] for i in range(4)],
    )
    removed = fold(acc, 2, 2) + others[...] + back_ref[0:32, :]
    degree = degree_in[...]
    if first:
        degree = degree + back_ref[32:48, :]
        degree_ref[...] = degree
    news, line = [], jnp.zeros((1, LANES), F32)
    lanes = iota((1, LANES), 1)
    sent_sums = [None] * 4
    for v in range(2):
        part = slice(16 * v, 16 * v + 16)
        r = start_ref[part, :]
        z = degree * r - removed[part]
        norm = lane_value(sums_ref[0:1, :], SUM_LANE + v)
        product = lane_value(energy, SUM_LANE + v)
        if first:
            p, q = r, z
        else:
            cross = lane_value(sums_ref[0:1, :], SUM_LANE + 2 + v)
            beta = norm / lane_value(old[0:1, :], v)
            product = product + beta * (2.0 * cross + beta * lane_value(old[0:1, :], 2 + v))
            p = r + beta * state[part, :]
            q = z + beta * state[32 + 16 * v : 48 + 16 * v, :]
        step = norm / product
        x = step * p
        if not first:
            x = x + state[64 + 16 * v : 80 + 16 * v, :]
        r = r - step * q
        if last:
            for t in range(TILES):
                positions_ref[v : v + 1, LANES * t : LANES * (t + 1)] = x[t : t + 1]
                residual_ref[v : v + 1, LANES * t : LANES * (t + 1)] = r[t : t + 1]
            continue
        residual_ref[part, :] = r
        for i, new in enumerate((p, q, x)):
            state_ref[32 * i + 16 * v : 32 * i + 16 * v + 16, :] = new
        news.append([r[t : t + 1] for t in range(TILES)])
        sent_sums[v], sent_sums[2 + v] = total(r * r), total(r * q)
        line = jnp.where(lanes == v, norm, jnp.where(lanes == 2 + v, product, line))
    if last:
        return
    old_ref[...] = jnp.broadcast_to(line, (8, LANES))
    put_gathered(news, sent_sums, cut_cells, pin_cell, pin_net, send_ref, kept_ref)


VMEM, SMEM, HBM = (pl.BlockSpec(memory_space=m) for m in (pltpu.VMEM, pltpu.SMEM, pltpu.HBM))


def call(kernel, shapes, scratch, cost, args, spaces=()):
    return pl.pallas_call(
        kernel,
        out_shape=[jax.ShapeDtypeStruct(s, F32) for s in shapes],
        in_specs=list(spaces) + [VMEM] * (len(args) - len(spaces)),
        out_specs=[VMEM] * len(shapes),
        scratch_shapes=[pltpu.VMEM(s, F32) if isinstance(s, tuple) else s for s in scratch],
        compiler_params=pltpu.CompilerParams(vmem_limit_bytes=32 << 20),
        cost_estimate=pl.CostEstimate(flops=cost, bytes_accessed=1 << 20, transcendentals=0),
    )(*args)


def stay(x):
    return pltpu.with_memory_space_constraint(x, pltpu.HBM)


def exchange(rows, height):
    return lax.all_to_all(
        rows.reshape(LANES, 1, height * LANES), AXES, split_axis=0, concat_axis=0, tiled=True
    ).reshape(LANES * height, LANES)


def swap(x):
    return lax.ppermute(x, "coord", [(0, 1), (1, 0)])


def per_device(
    right_side, anchor, blocks, tile_nbr, cut_cells, cut_weight, pin_cell, pin_net, star_weight
):
    cut_cells, cut_weight = cut_cells[0], cut_weight[0]
    pin_cell, pin_net = pin_cell.reshape(32, LANES), pin_net.reshape(32, LANES)
    star, anchor = star_weight.reshape(LANES, LANES), anchor.reshape(TILES, LANES)
    coord = lax.axis_index("coord")
    place = jnp.stack([coord, lax.axis_index("region") * 2 + coord]).astype(I32)
    side = jnp.full((8, LANES), coord).astype(F32)
    nbr = tile_nbr.T
    send, residual, kept, blocks, cut_weight, anchor = call(
        first_kernel,
        [(384, LANES), (32, LANES), (256, LANES), blocks.shape, (LANES, LANES), (TILES, LANES)],
        [
            (2, TILES * LANES),
            pltpu.VMEM((128, LANES), I32),
            pltpu.VMEM((32, LANES), I32),
            pltpu.VMEM((32, LANES), I32),
            pltpu.SemaphoreType.DMA((7,)),
        ],
        1 << 24,
        tuple(stay(x) for x in (right_side, cut_cells, pin_cell, pin_net, blocks, cut_weight, anchor)),
        [HBM] * 7,
    )
    for iteration in range(ITERS):
        first, last = iteration == 0, iteration == ITERS - 1
        got = exchange(send, 3)
        peer = swap(residual)
        rows = 48 if first else 32
        scratch = [(256, LANES), (128, LANES), pltpu.VMEM((8, LANES), I32)]
        local_sum, back, *more = call(
            functools.partial(backward_kernel, first),
            [(rows, LANES), (rows, LANES)] + [(32, LANES), (8, LANES)] * first,
            [(128, LANES), (256, LANES), pltpu.VMEM((8, LANES), I32)],
            BACKWARD_COST,
            (residual, side, nbr, blocks) + ((place, star) if first else ()),
            [VMEM] * 4 + [SMEM] * first,
        )
        if first:
            ones, net_weight = more
        local_sum, share = call(
            functools.partial(forward_kernel, first),
            [(rows, LANES), (8, LANES)],
            scratch,
            FORWARD_COST,
            (residual, peer, side, nbr, blocks, local_sum)
            + ((ones, anchor, cut_weight, kept) if first else (degree,)),
        )
        out, sums = call(
            functools.partial(owner_kernel, first),
            [(128, LANES), (8, LANES)],
            [(512 if first else 256, LANES)],
            1 << 26,
            (got, kept, cut_weight, net_weight, share),
        )
        returned = exchange(out, 1)
        back, sums = lax.optimization_barrier((back, sums))
        back = swap(back)
        args = (cut_cells, cut_weight, got, local_sum, sums)
        if first:
            others, degree = call(
                functools.partial(cut_kernel, True),
                [(32, LANES), (16, LANES)],
                [(128, LANES), (96, LANES)],
                1 << 31,
                args + (pin_cell, pin_net, star, anchor),
            )
        else:
            others = call(functools.partial(cut_kernel, False), [(32, LANES)], [], 1 << 31, args)[0]
        args = (pin_cell, returned, degree, others, back, sums, residual)
        if not first:
            args = args + (state, old)
        if last:
            shapes = [(2, TILES * LANES), (2, TILES * LANES)]
        else:
            args = args + (cut_cells, pin_net)
            shapes = [(384, LANES), (32, LANES), (96, LANES), (8, LANES), (256, LANES)]
            shapes = shapes + [(16, LANES)] * first
        results = call(
            functools.partial(step_kernel, first, last), shapes, [(128, LANES)], 1 << 26, args
        )
        if last:
            return tuple(results)
        send, residual, state, old, kept, *more = results
        if first:
            degree = more[0]


def solution(mesh):
    return jax.shard_map(
        per_device,
        mesh=mesh,
        in_specs=(
            P(None, AXES),
            P(AXES),
            P(AXES, None, None, None),
            P(AXES, None),
            P(AXES, None, None),
            P(AXES, None, None),
            P(AXES),
            P(AXES),
            P(),
        ),
        out_specs=(P(None, AXES), P(None, AXES)),
        check_vma=False,
    )
```

```python
import functools

import jax
import jax.numpy as jnp
from jax import lax
from jax.experimental import pallas as pl
from jax.experimental.pallas import tpu as pltpu
from jax.sharding import PartitionSpec as P

FANOUT = 32
BACKWARD_COST = 1 << 30
FORWARD_COST = 1 << 30
ITERS = 3
AXES = ("region", "coord")
LANES = 128
TILES = 16
F32 = jnp.float32
BF16 = jnp.bfloat16
I32 = jnp.int32
SUM_LANE = 96


def iota(shape, axis):
    return lax.broadcasted_iota(I32, shape, axis)


def split2(x):
    high = x.astype(BF16).astype(F32)
    return [high, (x - high).astype(BF16).astype(F32)]


def split3(x):
    high = x.astype(BF16).astype(F32)
    return [high] + split2(x - high)


def dot_nt(a, b):
    return lax.dot_general(a, b, (((1,), (1,)), ((), ())), preferred_element_type=F32)


def dot_nn(a, b):
    return lax.dot_general(a, b, (((1,), (0,)), ((), ())), preferred_element_type=F32)


def roll(x, shift):
    shift = shift % LANES
    return x if shift == 0 else pltpu.roll(x, shift, 1)


def total(x):
    return jnp.sum(jnp.sum(x, axis=0, keepdims=True), axis=1, keepdims=True)


def lane_value(row, lane):
    return jnp.sum(jnp.where(iota(row.shape, 1) == lane, row, 0.0), axis=1, keepdims=True)


def pick(tables, cells):
    low = cells & (LANES - 1)
    high = cells >> 7
    rows = [jnp.zeros(cells.shape, F32) for _ in tables]
    for tile in range(TILES):
        here = high == tile
        for v, table in enumerate(tables):
            wide = jnp.broadcast_to(table[tile], cells.shape)
            got = jnp.take_along_axis(wide, low, axis=1, mode="promise_in_bounds")
            rows[v] = jnp.where(here, got, rows[v])
    return rows


def one_hot(row, count):
    return jnp.where(iota((count, LANES), 0) == row, 1.0, 0.0).astype(BF16)


def add_rows(row_count, cell_row, value_rows):
    acc = None
    for j in range(0, row_count, 2):
        hots, masked = [], []
        for i in (j, j + 1):
            cells = cell_row(i)
            hots.append(one_hot(cells & (LANES - 1), LANES))
            here = iota((TILES, LANES), 0) == (cells >> 7)
            masked.append(
                jnp.concatenate([jnp.where(here, v, 0.0) for v in value_rows(i)], axis=0).astype(BF16)
            )
        part = dot_nt(jnp.concatenate(masked, axis=1), jnp.concatenate(hots, axis=1))
        acc = part if acc is None else acc + part
    return acc


def fold(acc, vectors, parts):
    size = vectors * TILES
    return sum(acc[i * size : (i + 1) * size] for i in range(parts))


def put_gathered(vectors, sums, cut_cells, pin_cell, pin_net, out_ref, kept_ref):
    lane = iota((32, LANES), 1)
    tail = jnp.zeros((1, LANES), F32)
    for i, s in enumerate(sums):
        tail = jnp.where(iota((1, LANES), 1) == SUM_LANE + i, s, tail)
    groups = [pick(vectors, pin_cell[8 * h : 8 * h + 8, :]) for h in range(4)]
    gx, gy = (jnp.concatenate([g[v] for g in groups], axis=0) for v in range(2))
    net = (pin_net[...] & (LANES - 1)).astype(F32)
    for q in range(4):
        row = jnp.where(
            lane < 32,
            roll(gx, -32 * q),
            jnp.where(
                lane < 64,
                roll(gy, 32 - 32 * q),
                jnp.where(lane < 96, roll(net, 64 - 32 * q), tail),
            ),
        )
        out_ref[pl.ds(3 * q + 2, 32, stride=12), :] = row
    for g in range(16):
        gx, gy = pick(vectors, cut_cells[pl.ds(8 * g, 8), :])
        out_ref[pl.ds(24 * g, 8, stride=3), :] = gx
        out_ref[pl.ds(24 * g + 1, 8, stride=3), :] = gy
        kept_ref[pl.ds(8 * g, 8), :] = gx
        kept_ref[pl.ds(128 + 8 * g, 8), :] = gy


def dense(rows, offset):
    lane = iota((32, LANES), 1)
    out = roll(rows[0], -offset)
    for q in range(1, 4):
        out = jnp.where(lane >= 32 * q, roll(rows[q], 32 * q - offset), out)
    return out


def first_kernel(right_hbm, cells_hbm, pin_cell_hbm, pin_net_hbm, weight_hbm, anchor_hbm, star_hbm, nbr_hbm,
                 send_ref, start_ref, kept_ref, weight_ref, anchor_ref, star_ref, nbr_ref,
                 right_ref, cut_cells, pin_cell, pin_net, sems):
    copies = [
        pltpu.make_async_copy(source, target, sems.at[i])
        for i, (source, target) in enumerate(
            (
                (right_hbm, right_ref),
                (pin_cell_hbm, pin_cell),
                (pin_net_hbm, pin_net),
                (cells_hbm, cut_cells),
                (weight_hbm, weight_ref),
                (anchor_hbm, anchor_ref),
                (star_hbm, star_ref),
                (nbr_hbm, nbr_ref),
            )
        )
    ]
    for copy in copies:
        copy.start()
    for copy in copies[:4]:
        copy.wait()
    tables = [
        [right_ref[v : v + 1, LANES * t : LANES * (t + 1)] for t in range(TILES)] for v in range(2)
    ]
    for v in range(2):
        for t in range(TILES):
            start_ref[TILES * v + t : TILES * v + t + 1, :] = tables[v][t]
    r = start_ref[...]
    sums = [total(r[16 * v : 16 * v + 16] * r[16 * v : 16 * v + 16]) for v in range(2)]
    put_gathered(tables, sums, cut_cells, pin_cell, pin_net, send_ref, kept_ref)
    for copy in copies[4:]:
        copy.wait()


def tile_names(nbr, names):
    names[...] = jnp.zeros(names.shape, I32)
    for k in range(2):
        names[k : k + 1, 0:TILES] = nbr[k : k + 1, :]
    return [jnp.where(iota((LANES, LANES), 0) == names[k : k + 1, :], 1.0, 0.0) for k in range(2)]


def block_parts(blocks, t):
    pair = jnp.concatenate([blocks[t, 0], blocks[t, 1]], axis=1)
    high = pair.astype(BF16)
    return high, (pair - high.astype(F32)).astype(BF16)


def tile_rows(ref, at, v):
    if v == 2:
        return ref[pl.ds(at + 4, 16, stride=8), :]
    return ref[pl.ds(at + v, 16, stride=8), :] + ref[pl.ds(at + v + 2, 16, stride=8), :]


def backward_kernel(first, own_ref, side, nbr, blocks, *refs):
    if first:
        place, star, local_ref, back_ref, ones_ref, net_weight_ref, near, got, names = refs
        net_weight_ref[...] = jnp.broadcast_to(star[pl.ds(place[1], 1), :], (8, LANES))
    else:
        local_ref, back_ref, near, got, names = refs
    spread_rows = [h[:32].astype(BF16) for h in tile_names(nbr, names)]
    near[...] = jnp.ones(near.shape, F32)
    for v in range(2):
        for i, part in enumerate(split2(own_ref[16 * v : 16 * v + 16, :])):
            near[pl.ds(2 * i + v, 16, stride=8), :] = part
    for t in range(TILES):
        a = near[8 * t : 8 * t + 8, :].astype(BF16)
        high, low = block_parts(blocks, t)
        back = dot_nn(a, high) + dot_nn(a, low)
        for k in range(2):
            got[128 * k + 8 * t : 128 * k + 8 * t + 8, :] = back[:, LANES * k : LANES * (k + 1)]
    filler = jnp.zeros((112, LANES), F32)
    upper = side[0:1, :] > 0.5
    for v in range(3 if first else 2):
        spread = sum(
            dot_nn(spread_rows[k], jnp.concatenate([part, filler], axis=0).astype(BF16))
            for k in range(2)
            for part in split3(tile_rows(got, 128 * k, v))
        )
        lower, higher = spread[:16], spread[16:]
        local_ref[16 * v : 16 * v + 16, :] = jnp.where(upper, higher, lower)
        back_ref[16 * v : 16 * v + 16, :] = jnp.where(upper, lower, higher)
        if v == 2:
            ones_ref[...] = spread


def forward_kernel(first, own_ref, peer_ref, side, nbr, blocks, before_ref, *refs):
    if first:
        ones_ref, anchor, cut_weight, kept, local_ref, share_ref, far, got, names = refs
    else:
        degree, local_ref, share_ref, far, got, names = refs
    upper = side[0:1, :] > 0.5
    pick_rows = jnp.concatenate([h.T[:16] for h in tile_names(nbr, names)], axis=0).astype(BF16)
    far[...] = jnp.ones(far.shape, F32)
    zeros = jnp.zeros((96, LANES), F32)
    wholes = []
    for v in range(2):
        o, p = own_ref[16 * v : 16 * v + 16, :], peer_ref[16 * v : 16 * v + 16, :]
        whole = jnp.concatenate([jnp.where(upper, p, o), jnp.where(upper, o, p)], axis=0)
        wholes.append(whole)
        for i, part in enumerate(split2(whole)):
            picked = dot_nn(pick_rows, jnp.concatenate([part, zeros], axis=0).astype(BF16))
            for k in range(2):
                far[pl.ds(128 * k + 2 * i + v, 16, stride=8), :] = picked[16 * k : 16 * k + 16]
    for t in range(TILES):
        b = jnp.concatenate(
            [far[128 * k + 8 * t : 128 * k + 8 * t + 8, :] for k in range(2)], axis=1
        ).astype(BF16)
        high, low = block_parts(blocks, t)
        got[8 * t : 8 * t + 8, :] = dot_nt(b, high) + dot_nt(b, low)
    ahead = [tile_rows(got, 0, v) for v in range(3 if first else 2)]
    for v, forward in enumerate(ahead):
        local_ref[16 * v : 16 * v + 16, :] = before_ref[16 * v : 16 * v + 16, :] + forward
    for v in range(2):
        r = own_ref[16 * v : 16 * v + 16, :]
        if first:
            square = r * (r * (anchor[...] + ahead[2]) - 2.0 * ahead[v])
            line = jnp.sum(square, axis=0, keepdims=True)
            line = line + jnp.sum(wholes[v] * wholes[v] * ones_ref[...], axis=0, keepdims=True)
            cut = kept[128 * v : 128 * v + 128, :]
            line = line + jnp.sum(cut_weight[...] * cut * cut, axis=0, keepdims=True)
        else:
            line = jnp.sum(r * (r * degree[...] - 2.0 * ahead[v]), axis=0, keepdims=True)
        share_ref[v : v + 1, :] = line
    share_ref[2:8, :] = jnp.zeros((6, LANES), F32)


def owner_kernel(first, got, kept, cut_weight, net_weight, share_ref, out_ref, sums_ref, rows):
    height = 16 if first else 8
    pin_rows = [got[pl.ds(3 * q + 2, 32, stride=12), :] for q in range(4)]
    sums = sum(jnp.sum(row, axis=0, keepdims=True) for row in pin_rows)
    sums_ref[...] = jnp.broadcast_to(sums, (8, LANES))
    nets = dense(pin_rows, 64).astype(I32)
    rows[...] = jnp.zeros(rows.shape, F32)
    for v in range(2):
        pins = dense(pin_rows, 32 * v)
        for i, part in enumerate(split3(pins)):
            rows[pl.ds(2 * i + v, 32, stride=height), :] = part
        if first:
            for i, part in enumerate(split3(pins * pins)):
                rows[pl.ds(8 + 2 * i + v, 32, stride=height), :] = part
    acc = None
    for j in range(0, 32, 2):
        hot = jnp.concatenate([one_hot(nets[i : i + 1], LANES) for i in (j, j + 1)], axis=1)
        left = jnp.concatenate(
            [rows[height * i : height * i + height, :] for i in (j, j + 1)], axis=1
        )
        part = dot_nt(left.astype(BF16), hot)
        acc = part if acc is None else acc + part
    weight = net_weight[0:1, :]
    totals = [acc[v : v + 1] + acc[v + 2 : v + 3] + acc[v + 4 : v + 5] for v in range(2)]
    centres = [weight * (1.0 / FANOUT) * t for t in totals]
    tail = jnp.zeros((1, LANES), F32)
    for v in range(2):
        line = share_ref[v : v + 1, :] - centres[v] * totals[v]
        if first:
            squares = acc[8 + v : 9 + v] + acc[10 + v : 11 + v] + acc[12 + v : 13 + v]
            line = line + weight * squares
        cut = cut_weight[...] * (kept[128 * v : 128 * v + 128, :] * got[pl.ds(v, 128, stride=3), :])
        line = line - jnp.sum(cut, axis=0, keepdims=True)
        tail = jnp.where(
            iota((1, LANES), 1) == SUM_LANE + v, jnp.sum(line, axis=1, keepdims=True), tail
        )
    lane = iota((8, LANES), 1)
    tables = [jnp.broadcast_to(c, (8, LANES)) for c in centres]
    for g in range(16):
        row = got[pl.ds(24 * g + 2, 8, stride=3), :]
        index = jnp.where(lane < 32, roll(row, -64), roll(row, -32)).astype(I32) & (LANES - 1)
        gx, gy = (
            jnp.take_along_axis(t, index, axis=1, mode="promise_in_bounds") for t in tables
        )
        out_ref[pl.ds(8 * g, 8), :] = jnp.where(
            lane < 32, gx, jnp.where(lane < 64, gy, jnp.where(lane < 96, 0.0, tail))
        )


def put_hots(hot_ref, numbers):
    columns = jnp.concatenate([numbers, numbers, numbers, numbers], axis=0).astype(F32).T
    for j in range(32):
        wide = jnp.broadcast_to(columns[:, j : j + 1], (LANES, LANES)).astype(I32)
        hot = jnp.where(iota((LANES, LANES), 1) == wide, 1.0, 0.0)
        hot_ref[LANES * j : LANES * (j + 1), :] = hot.astype(BF16)


def cut_kernel(first, cut_cells, cut_weight, got, local_ref, sums_ref, pin_cell, *refs):
    del sums_ref

    def values(j):
        weight = cut_weight[j : j + 1, :]
        parts = [split2(weight * got[3 * j + v : 3 * j + v + 1, :]) for v in range(2)]
        moved = [parts[0][0], parts[1][0], parts[0][1], parts[1][1]]
        return moved + split3(weight) if first else moved

    acc = add_rows(128, lambda j: cut_cells[j : j + 1, :], values)
    if not first:
        out_ref, cell_hot = refs
        put_hots(cell_hot, pin_cell[...] & (LANES - 1))
        out_ref[...] = fold(acc, 2, 2) + local_ref[...]
        return
    pin_net, star, anchor, out_ref, cell_hot, degree_ref, rows_ref, pins_ref = refs
    put_hots(cell_hot, pin_cell[...] & (LANES - 1))
    out_ref[...] = fold(acc[:64], 2, 2) + local_ref[0:32, :]
    net = pin_net[...] & (LANES - 1)
    for q in range(4):
        rows_ref[pl.ds(32 * q, 32), :] = jnp.take_along_axis(
            star[pl.ds(q, 32, stride=4), :], roll(net, -32 * q), axis=1, mode="promise_in_bounds"
        )
    weight = dense([rows_ref[pl.ds(32 * q, 32), :] for q in range(4)], 0)
    for i, part in enumerate(split3(weight)):
        pins_ref[pl.ds(32 * i, 32), :] = part
    pinned = add_rows(
        32,
        lambda j: pin_cell[j : j + 1, :],
        lambda j: [pins_ref[32 * i + j : 32 * i + j + 1, :] for i in range(3)],
    )
    degree_ref[...] = (
        anchor[...] + fold(acc[64:], 1, 3) + fold(pinned, 1, 3) + local_ref[32:48, :]
    )


def step_kernel(first, last, pin_cell, cell_hot, got, degree_in, others, back_ref, sums_ref, start_ref, *refs):
    refs = list(refs)
    state, old = (None, None) if first else (refs.pop(0), refs.pop(0))
    if last:
        positions_ref, residual_ref, pins = refs
    elif first:
        cut_cells, pin_net, send_ref, residual_ref, state_ref, old_ref, kept_ref, degree_ref, pins = refs
    else:
        cut_cells, pin_net, send_ref, residual_ref, state_ref, old_ref, kept_ref, pins = refs
    pin_rows = [got[pl.ds(q, 32, stride=4), :] for q in range(4)]
    energy = sum(jnp.sum(row, axis=0, keepdims=True) for row in pin_rows)
    for v in range(2):
        for i, part in enumerate(split2(dense(pin_rows, 32 * v))):
            pins[pl.ds(32 * (2 * i + v), 32), :] = part
    acc = None
    for j in range(0, 32, 2):
        masked = []
        for k in (j, j + 1):
            here = iota((TILES, LANES), 0) == (pin_cell[k : k + 1, :] >> 7)
            values = [pins[32 * i + k : 32 * i + k + 1, :] for i in range(4)]
            masked.append(jnp.concatenate([jnp.where(here, v, 0.0) for v in values], axis=0).astype(BF16))
        part = dot_nn(jnp.concatenate(masked, axis=1), cell_hot[LANES * j : LANES * (j + 2), :])
        acc = part if acc is None else acc + part
    removed = fold(acc, 2, 2) + others[...] + back_ref[0:32, :]
    degree = degree_in[...]
    if first:
        degree = degree + back_ref[32:48, :]
        degree_ref[...] = degree
    news, line = [], jnp.zeros((1, LANES), F32)
    lanes = iota((1, LANES), 1)
    sent_sums = [None] * 4
    for v in range(2):
        part = slice(16 * v, 16 * v + 16)
        r = start_ref[part, :]
        z = degree * r - removed[part]
        norm = lane_value(sums_ref[0:1, :], SUM_LANE + v)
        product = lane_value(energy, SUM_LANE + v)
        if first:
            p, q = r, z
        else:
            cross = lane_value(sums_ref[0:1, :], SUM_LANE + 2 + v)
            beta = norm / lane_value(old[0:1, :], v)
            product = product + beta * (2.0 * cross + beta * lane_value(old[0:1, :], 2 + v))
            p = r + beta * state[part, :]
            q = z + beta * state[32 + 16 * v : 48 + 16 * v, :]
        step = norm / product
        x = step * p
        if not first:
            x = x + state[64 + 16 * v : 80 + 16 * v, :]
        r = r - step * q
        if last:
            for t in range(TILES):
                positions_ref[v : v + 1, LANES * t : LANES * (t + 1)] = x[t : t + 1]
                residual_ref[v : v + 1, LANES * t : LANES * (t + 1)] = r[t : t + 1]
            continue
        residual_ref[part, :] = r
        for i, new in enumerate((p, q, x)):
            state_ref[32 * i + 16 * v : 32 * i + 16 * v + 16, :] = new
        news.append([r[t : t + 1] for t in range(TILES)])
        sent_sums[v], sent_sums[2 + v] = total(r * r), total(r * q)
        line = jnp.where(lanes == v, norm, jnp.where(lanes == 2 + v, product, line))
    if last:
        return
    old_ref[...] = jnp.broadcast_to(line, (8, LANES))
    put_gathered(news, sent_sums, cut_cells, pin_cell, pin_net, send_ref, kept_ref)


VMEM, SMEM, HBM = (pl.BlockSpec(memory_space=m) for m in (pltpu.VMEM, pltpu.SMEM, pltpu.HBM))


def call(kernel, shapes, scratch, cost, args, spaces=()):
    return pl.pallas_call(
        kernel,
        out_shape=[jax.ShapeDtypeStruct(s, F32) if isinstance(s, tuple) else s for s in shapes],
        in_specs=list(spaces) + [VMEM] * (len(args) - len(spaces)),
        out_specs=[VMEM] * len(shapes),
        scratch_shapes=[pltpu.VMEM(s, F32) if isinstance(s, tuple) else s for s in scratch],
        compiler_params=pltpu.CompilerParams(vmem_limit_bytes=32 << 20),
        cost_estimate=pl.CostEstimate(flops=cost, bytes_accessed=1 << 20, transcendentals=0),
    )(*args)


def stay(x):
    return pltpu.with_memory_space_constraint(x, pltpu.HBM)


def exchange(rows, height):
    return lax.all_to_all(
        rows.reshape(LANES, 1, height * LANES), AXES, split_axis=0, concat_axis=0, tiled=True
    ).reshape(LANES * height, LANES)


def swap(x):
    return lax.ppermute(x, "coord", [(0, 1), (1, 0)])


def per_device(
    right_side, anchor, blocks, tile_nbr, cut_cells, cut_weight, pin_cell, pin_net, star_weight
):
    cut_cells, cut_weight = cut_cells[0], cut_weight[0]
    pin_cell, pin_net = pin_cell.reshape(32, LANES), pin_net.reshape(32, LANES)
    star, anchor = star_weight.reshape(LANES, LANES), anchor.reshape(TILES, LANES)
    coord = lax.axis_index("coord")
    place = jnp.stack([coord, lax.axis_index("region") * 2 + coord]).astype(I32)
    side = jnp.full((8, LANES), coord).astype(F32)
    nbr = tile_nbr.T
    send, residual, kept, cut_weight, anchor, star, nbr = call(
        first_kernel,
        [(384, LANES), (32, LANES), (256, LANES), (LANES, LANES), (TILES, LANES), (LANES, LANES),
         jax.ShapeDtypeStruct(nbr.shape, I32)],
        [
            (2, TILES * LANES),
            pltpu.VMEM((128, LANES), I32),
            pltpu.VMEM((32, LANES), I32),
            pltpu.VMEM((32, LANES), I32),
            pltpu.SemaphoreType.DMA((8,)),
        ],
        1 << 24,
        tuple(stay(x) for x in (right_side, cut_cells, pin_cell, pin_net, cut_weight, anchor, star, nbr)),
        [HBM] * 8,
    )
    hots = jax.ShapeDtypeStruct((32 * LANES, LANES), BF16)
    for iteration in range(ITERS):
        first, last = iteration == 0, iteration == ITERS - 1
        got = exchange(send, 3)
        peer = swap(residual)
        rows = 48 if first else 32
        scratch = [(256, LANES), (128, LANES), pltpu.VMEM((8, LANES), I32)]
        local_sum, back, *more = call(
            functools.partial(backward_kernel, first),
            [(rows, LANES), (rows, LANES)] + [(32, LANES), (8, LANES)] * first,
            [(128, LANES), (256, LANES), pltpu.VMEM((8, LANES), I32)],
            BACKWARD_COST,
            (residual, side, nbr, blocks) + ((place, star) if first else ()),
            [VMEM] * 4 + [SMEM] * first,
        )
        if first:
            ones, net_weight = more
        local_sum, share = call(
            functools.partial(forward_kernel, first),
            [(rows, LANES), (8, LANES)],
            scratch,
            FORWARD_COST,
            (residual, peer, side, nbr, blocks, local_sum)
            + ((ones, anchor, cut_weight, kept) if first else (degree,)),
        )
        out, sums = call(
            functools.partial(owner_kernel, first),
            [(128, LANES), (8, LANES)],
            [(512 if first else 256, LANES)],
            1 << 26,
            (got, kept, cut_weight, net_weight, share),
        )
        returned = exchange(out, 1)
        back, sums = lax.optimization_barrier((back, sums))
        back = swap(back)
        args = (cut_cells, cut_weight, got, local_sum, sums, pin_cell)
        if first:
            others, cell_hot, degree = call(
                functools.partial(cut_kernel, True),
                [(32, LANES), hots, (16, LANES)],
                [(128, LANES), (96, LANES)],
                1 << 31,
                args + (pin_net, star, anchor),
            )
        else:
            others, cell_hot = call(
                functools.partial(cut_kernel, False), [(32, LANES), hots], [], 1 << 31, args
            )
        args = (pin_cell, cell_hot, returned, degree, others, back, sums, residual)
        if not first:
            args = args + (state, old)
        if last:
            shapes = [(2, TILES * LANES), (2, TILES * LANES)]
        else:
            args = args + (cut_cells, pin_net)
            shapes = [(384, LANES), (32, LANES), (96, LANES), (8, LANES), (256, LANES)]
            shapes = shapes + [(16, LANES)] * first
        results = call(
            functools.partial(step_kernel, first, last), shapes, [(128, LANES)], 1 << 26, args
        )
        if last:
            return tuple(results)
        send, residual, state, old, kept, *more = results
        if first:
            degree = more[0]


def solution(mesh):
    return jax.shard_map(
        per_device,
        mesh=mesh,
        in_specs=(
            P(None, AXES),
            P(AXES),
            P(AXES, None, None, None),
            P(AXES, None),
            P(AXES, None, None),
            P(AXES, None, None),
            P(AXES),
            P(AXES),
            P(),
        ),
        out_specs=(P(None, AXES), P(None, AXES)),
        check_vma=False,
    )
```

```python
import functools

import jax
import jax.numpy as jnp
from jax import lax
from jax.experimental import pallas as pl
from jax.experimental.pallas import tpu as pltpu
from jax.sharding import PartitionSpec as P

FANOUT = 32
BACKWARD_COST = 1 << 30
FORWARD_COST = 1 << 30
ITERS = 3
AXES = ("region", "coord")
LANES = 128
TILES = 16
F32 = jnp.float32
BF16 = jnp.bfloat16
I32 = jnp.int32
SUM_LANE = 96


def iota(shape, axis):
    return lax.broadcasted_iota(I32, shape, axis)


def split2(x):
    high = x.astype(BF16).astype(F32)
    return [high, (x - high).astype(BF16).astype(F32)]


def split3(x):
    high = x.astype(BF16).astype(F32)
    return [high] + split2(x - high)


def dot_nt(a, b):
    return lax.dot_general(a, b, (((1,), (1,)), ((), ())), preferred_element_type=F32)


def dot_nn(a, b):
    return lax.dot_general(a, b, (((1,), (0,)), ((), ())), preferred_element_type=F32)


def roll(x, shift):
    shift = shift % LANES
    return x if shift == 0 else pltpu.roll(x, shift, 1)


def total(x):
    return jnp.sum(jnp.sum(x, axis=0, keepdims=True), axis=1, keepdims=True)


def lane_value(row, lane):
    return jnp.sum(jnp.where(iota(row.shape, 1) == lane, row, 0.0), axis=1, keepdims=True)


def pick(tables, cells):
    low = cells & (LANES - 1)
    high = cells >> 7
    rows = [jnp.zeros(cells.shape, F32) for _ in tables]
    for tile in range(TILES):
        here = high == tile
        for v, table in enumerate(tables):
            wide = jnp.broadcast_to(table[tile], cells.shape)
            got = jnp.take_along_axis(wide, low, axis=1, mode="promise_in_bounds")
            rows[v] = jnp.where(here, got, rows[v])
    return rows


def one_hot(row, count):
    return jnp.where(iota((count, LANES), 0) == row, 1.0, 0.0).astype(BF16)


def add_rows(row_count, cell_row, value_rows):
    acc = None
    for j in range(0, row_count, 2):
        hots, masked = [], []
        for i in (j, j + 1):
            cells = cell_row(i)
            hots.append(one_hot(cells & (LANES - 1), LANES))
            here = iota((TILES, LANES), 0) == (cells >> 7)
            masked.append(
                jnp.concatenate([jnp.where(here, v, 0.0) for v in value_rows(i)], axis=0).astype(BF16)
            )
        part = dot_nt(jnp.concatenate(masked, axis=1), jnp.concatenate(hots, axis=1))
        acc = part if acc is None else acc + part
    return acc


def fold(acc, vectors, parts):
    size = vectors * TILES
    return sum(acc[i * size : (i + 1) * size] for i in range(parts))


def put_gathered(vectors, sums, cut_cells, pin_cell, pin_net, out_ref, kept_ref):
    lane = iota((32, LANES), 1)
    tail = jnp.zeros((1, LANES), F32)
    for i, s in enumerate(sums):
        tail = jnp.where(iota((1, LANES), 1) == SUM_LANE + i, s, tail)
    groups = [pick(vectors, pin_cell[8 * h : 8 * h + 8, :]) for h in range(4)]
    gx, gy = (jnp.concatenate([g[v] for g in groups], axis=0) for v in range(2))
    net = (pin_net[...] & (LANES - 1)).astype(F32)
    for q in range(4):
        row = jnp.where(
            lane < 32,
            roll(gx, -32 * q),
            jnp.where(
                lane < 64,
                roll(gy, 32 - 32 * q),
                jnp.where(lane < 96, roll(net, 64 - 32 * q), tail),
            ),
        )
        out_ref[pl.ds(3 * q + 2, 32, stride=12), :] = row
    for g in range(16):
        gx, gy = pick(vectors, cut_cells[pl.ds(8 * g, 8), :])
        out_ref[pl.ds(24 * g, 8, stride=3), :] = gx
        out_ref[pl.ds(24 * g + 1, 8, stride=3), :] = gy
        kept_ref[pl.ds(8 * g, 8), :] = gx
        kept_ref[pl.ds(128 + 8 * g, 8), :] = gy


def dense(rows, offset):
    lane = iota((32, LANES), 1)
    out = roll(rows[0], -offset)
    for q in range(1, 4):
        out = jnp.where(lane >= 32 * q, roll(rows[q], 32 * q - offset), out)
    return out


def first_kernel(right_hbm, cells_hbm, pin_cell_hbm, pin_net_hbm, weight_hbm, anchor_hbm, star_hbm, nbr_hbm,
                 send_ref, start_ref, kept_ref, weight_ref, anchor_ref, star_ref, nbr_ref,
                 right_ref, cut_cells, pin_cell, pin_net, sems):
    copies = [
        pltpu.make_async_copy(source, target, sems.at[i])
        for i, (source, target) in enumerate(
            (
                (right_hbm, right_ref),
                (pin_cell_hbm, pin_cell),
                (pin_net_hbm, pin_net),
                (cells_hbm, cut_cells),
                (weight_hbm, weight_ref),
                (anchor_hbm, anchor_ref),
                (star_hbm, star_ref),
                (nbr_hbm, nbr_ref),
            )
        )
    ]
    for copy in copies:
        copy.start()
    for copy in copies[:4]:
        copy.wait()
    tables = [
        [right_ref[v : v + 1, LANES * t : LANES * (t + 1)] for t in range(TILES)] for v in range(2)
    ]
    for v in range(2):
        for t in range(TILES):
            start_ref[TILES * v + t : TILES * v + t + 1, :] = tables[v][t]
    r = start_ref[...]
    sums = [total(r[16 * v : 16 * v + 16] * r[16 * v : 16 * v + 16]) for v in range(2)]
    put_gathered(tables, sums, cut_cells, pin_cell, pin_net, send_ref, kept_ref)
    for copy in copies[4:]:
        copy.wait()


def tile_names(nbr, names):
    names[...] = jnp.zeros(names.shape, I32)
    for k in range(2):
        names[k : k + 1, 0:TILES] = nbr[k : k + 1, :]
    return [jnp.where(iota((LANES, LANES), 0) == names[k : k + 1, :], 1.0, 0.0) for k in range(2)]


def block_parts(blocks, t):
    pair = jnp.concatenate([blocks[t, 0], blocks[t, 1]], axis=1)
    high = pair.astype(BF16)
    return high, (pair - high.astype(F32)).astype(BF16)


def tile_rows(ref, at, v):
    if v == 2:
        return ref[pl.ds(at + 4, 16, stride=8), :]
    return ref[pl.ds(at + v, 16, stride=8), :] + ref[pl.ds(at + v + 2, 16, stride=8), :]


def backward_kernel(first, own_ref, side, nbr, blocks, *refs):
    if first:
        place, star, local_ref, back_ref, ones_ref, net_weight_ref, near, got, names = refs
        net_weight_ref[...] = jnp.broadcast_to(star[pl.ds(place[1], 1), :], (8, LANES))
    else:
        local_ref, back_ref, near, got, names = refs
    spread_rows = [h[:32].astype(BF16) for h in tile_names(nbr, names)]
    near[...] = jnp.ones(near.shape, F32)
    for v in range(2):
        for i, part in enumerate(split2(own_ref[16 * v : 16 * v + 16, :])):
            near[pl.ds(2 * i + v, 16, stride=8), :] = part
    for t in range(TILES):
        a = near[8 * t : 8 * t + 8, :].astype(BF16)
        high, low = block_parts(blocks, t)
        back = dot_nn(a, high) + dot_nn(a, low)
        for k in range(2):
            got[128 * k + 8 * t : 128 * k + 8 * t + 8, :] = back[:, LANES * k : LANES * (k + 1)]
    filler = jnp.zeros((112, LANES), F32)
    upper = side[0:1, :] > 0.5
    for v in range(3 if first else 2):
        spread = sum(
            dot_nn(spread_rows[k], jnp.concatenate([part, filler], axis=0).astype(BF16))
            for k in range(2)
            for part in split3(tile_rows(got, 128 * k, v))
        )
        lower, higher = spread[:16], spread[16:]
        local_ref[16 * v : 16 * v + 16, :] = jnp.where(upper, higher, lower)
        back_ref[16 * v : 16 * v + 16, :] = jnp.where(upper, lower, higher)
        if v == 2:
            ones_ref[...] = spread


def forward_kernel(first, own_ref, peer_ref, side, nbr, blocks, before_ref, *refs):
    if first:
        ones_ref, anchor, cut_weight, kept, local_ref, share_ref, far, got, names = refs
    else:
        degree, local_ref, share_ref, far, got, names = refs
    upper = side[0:1, :] > 0.5
    pick_rows = jnp.concatenate([h.T[:16] for h in tile_names(nbr, names)], axis=0).astype(BF16)
    far[...] = jnp.ones(far.shape, F32)
    zeros = jnp.zeros((96, LANES), F32)
    wholes = []
    for v in range(2):
        o, p = own_ref[16 * v : 16 * v + 16, :], peer_ref[16 * v : 16 * v + 16, :]
        whole = jnp.concatenate([jnp.where(upper, p, o), jnp.where(upper, o, p)], axis=0)
        wholes.append(whole)
        for i, part in enumerate(split2(whole)):
            picked = dot_nn(pick_rows, jnp.concatenate([part, zeros], axis=0).astype(BF16))
            for k in range(2):
                far[pl.ds(128 * k + 2 * i + v, 16, stride=8), :] = picked[16 * k : 16 * k + 16]
    for t in range(TILES):
        b = jnp.concatenate(
            [far[128 * k + 8 * t : 128 * k + 8 * t + 8, :] for k in range(2)], axis=1
        ).astype(BF16)
        high, low = block_parts(blocks, t)
        got[8 * t : 8 * t + 8, :] = dot_nt(b, high) + dot_nt(b, low)
    ahead = [tile_rows(got, 0, v) for v in range(3 if first else 2)]
    for v, forward in enumerate(ahead):
        local_ref[16 * v : 16 * v + 16, :] = before_ref[16 * v : 16 * v + 16, :] + forward
    for v in range(2):
        r = own_ref[16 * v : 16 * v + 16, :]
        if first:
            square = r * (r * (anchor[...] + ahead[2]) - 2.0 * ahead[v])
            line = jnp.sum(square, axis=0, keepdims=True)
            line = line + jnp.sum(wholes[v] * wholes[v] * ones_ref[...], axis=0, keepdims=True)
            cut = kept[128 * v : 128 * v + 128, :]
            line = line + jnp.sum(cut_weight[...] * cut * cut, axis=0, keepdims=True)
        else:
            line = jnp.sum(r * (r * degree[...] - 2.0 * ahead[v]), axis=0, keepdims=True)
        share_ref[v : v + 1, :] = line
    share_ref[2:8, :] = jnp.zeros((6, LANES), F32)


def owner_kernel(first, got, kept, cut_weight, net_weight, share_ref, *refs):
    if first:
        out_ref, sums_ref, nets_ref, rows = refs
    else:
        net_hot, out_ref, sums_ref, rows = refs
    height = 16 if first else 8
    pin_rows = [got[pl.ds(3 * q + 2, 32, stride=12), :] for q in range(4)]
    sums = sum(jnp.sum(row, axis=0, keepdims=True) for row in pin_rows)
    sums_ref[...] = jnp.broadcast_to(sums, (8, LANES))
    if first:
        nets_ref[...] = dense(pin_rows, 64)
        nets = nets_ref[...].astype(I32)
    rows[...] = jnp.zeros(rows.shape, F32)
    for v in range(2):
        pins = dense(pin_rows, 32 * v)
        for i, part in enumerate(split3(pins)):
            rows[pl.ds(2 * i + v, 32, stride=height), :] = part
        if first:
            for i, part in enumerate(split3(pins * pins)):
                rows[pl.ds(8 + 2 * i + v, 32, stride=height), :] = part
    acc = None
    for j in range(0, 32, 2):
        left = jnp.concatenate(
            [rows[height * i : height * i + height, :] for i in (j, j + 1)], axis=1
        ).astype(BF16)
        if first:
            hot = jnp.concatenate([one_hot(nets[i : i + 1], LANES) for i in (j, j + 1)], axis=1)
            part = dot_nt(left, hot)
        else:
            part = dot_nn(left, net_hot[LANES * j : LANES * (j + 2), :])
        acc = part if acc is None else acc + part
    weight = net_weight[0:1, :]
    totals = [acc[v : v + 1] + acc[v + 2 : v + 3] + acc[v + 4 : v + 5] for v in range(2)]
    centres = [weight * (1.0 / FANOUT) * t for t in totals]
    tail = jnp.zeros((1, LANES), F32)
    for v in range(2):
        line = share_ref[v : v + 1, :] - centres[v] * totals[v]
        if first:
            squares = acc[8 + v : 9 + v] + acc[10 + v : 11 + v] + acc[12 + v : 13 + v]
            line = line + weight * squares
        cut = cut_weight[...] * (kept[128 * v : 128 * v + 128, :] * got[pl.ds(v, 128, stride=3), :])
        line = line - jnp.sum(cut, axis=0, keepdims=True)
        tail = jnp.where(
            iota((1, LANES), 1) == SUM_LANE + v, jnp.sum(line, axis=1, keepdims=True), tail
        )
    lane = iota((8, LANES), 1)
    tables = [jnp.broadcast_to(c, (8, LANES)) for c in centres]
    for g in range(16):
        row = got[pl.ds(24 * g + 2, 8, stride=3), :]
        index = jnp.where(lane < 32, roll(row, -64), roll(row, -32)).astype(I32) & (LANES - 1)
        gx, gy = (
            jnp.take_along_axis(t, index, axis=1, mode="promise_in_bounds") for t in tables
        )
        out_ref[pl.ds(8 * g, 8), :] = jnp.where(
            lane < 32, gx, jnp.where(lane < 64, gy, jnp.where(lane < 96, 0.0, tail))
        )


def put_hots(hot_ref, numbers):
    columns = jnp.concatenate([numbers, numbers, numbers, numbers], axis=0).astype(F32).T
    for j in range(32):
        wide = jnp.broadcast_to(columns[:, j : j + 1], (LANES, LANES)).astype(I32)
        hot = jnp.where(iota((LANES, LANES), 1) == wide, 1.0, 0.0)
        hot_ref[LANES * j : LANES * (j + 1), :] = hot.astype(BF16)


def net_kernel(nets, share_ref, hot_ref):
    del share_ref
    put_hots(hot_ref, nets[...].astype(I32))


def cut_kernel(first, cut_cells, cut_weight, got, local_ref, sums_ref, pin_cell, *refs):
    del sums_ref

    def values(j):
        weight = cut_weight[j : j + 1, :]
        parts = [split2(weight * got[3 * j + v : 3 * j + v + 1, :]) for v in range(2)]
        moved = [parts[0][0], parts[1][0], parts[0][1], parts[1][1]]
        return moved + split3(weight) if first else moved

    acc = add_rows(128, lambda j: cut_cells[j : j + 1, :], values)
    if not first:
        out_ref, cell_hot = refs
        put_hots(cell_hot, pin_cell[...] & (LANES - 1))
        out_ref[...] = fold(acc, 2, 2) + local_ref[...]
        return
    pin_net, star, anchor, out_ref, cell_hot, degree_ref, rows_ref, pins_ref = refs
    put_hots(cell_hot, pin_cell[...] & (LANES - 1))
    out_ref[...] = fold(acc[:64], 2, 2) + local_ref[0:32, :]
    net = pin_net[...] & (LANES - 1)
    for q in range(4):
        rows_ref[pl.ds(32 * q, 32), :] = jnp.take_along_axis(
            star[pl.ds(q, 32, stride=4), :], roll(net, -32 * q), axis=1, mode="promise_in_bounds"
        )
    weight = dense([rows_ref[pl.ds(32 * q, 32), :] for q in range(4)], 0)
    for i, part in enumerate(split3(weight)):
        pins_ref[pl.ds(32 * i, 32), :] = part
    pinned = add_rows(
        32,
        lambda j: pin_cell[j : j + 1, :],
        lambda j: [pins_ref[32 * i + j : 32 * i + j + 1, :] for i in range(3)],
    )
    degree_ref[...] = (
        anchor[...] + fold(acc[64:], 1, 3) + fold(pinned, 1, 3) + local_ref[32:48, :]
    )


def step_kernel(first, last, pin_cell, cell_hot, got, degree_in, others, back_ref, sums_ref, start_ref, *refs):
    refs = list(refs)
    state, old = (None, None) if first else (refs.pop(0), refs.pop(0))
    if last:
        positions_ref, residual_ref, pins = refs
    elif first:
        cut_cells, pin_net, send_ref, residual_ref, state_ref, old_ref, kept_ref, degree_ref, pins = refs
    else:
        cut_cells, pin_net, send_ref, residual_ref, state_ref, old_ref, kept_ref, pins = refs
    pin_rows = [got[pl.ds(q, 32, stride=4), :] for q in range(4)]
    energy = sum(jnp.sum(row, axis=0, keepdims=True) for row in pin_rows)
    for v in range(2):
        for i, part in enumerate(split2(dense(pin_rows, 32 * v))):
            pins[pl.ds(32 * (2 * i + v), 32), :] = part
    acc = None
    for j in range(0, 32, 2):
        masked = []
        for k in (j, j + 1):
            here = iota((TILES, LANES), 0) == (pin_cell[k : k + 1, :] >> 7)
            values = [pins[32 * i + k : 32 * i + k + 1, :] for i in range(4)]
            masked.append(jnp.concatenate([jnp.where(here, v, 0.0) for v in values], axis=0).astype(BF16))
        part = dot_nn(jnp.concatenate(masked, axis=1), cell_hot[LANES * j : LANES * (j + 2), :])
        acc = part if acc is None else acc + part
    removed = fold(acc, 2, 2) + others[...] + back_ref[0:32, :]
    degree = degree_in[...]
    if first:
        degree = degree + back_ref[32:48, :]
        degree_ref[...] = degree
    news, line = [], jnp.zeros((1, LANES), F32)
    lanes = iota((1, LANES), 1)
    sent_sums = [None] * 4
    for v in range(2):
        part = slice(16 * v, 16 * v + 16)
        r = start_ref[part, :]
        z = degree * r - removed[part]
        norm = lane_value(sums_ref[0:1, :], SUM_LANE + v)
        product = lane_value(energy, SUM_LANE + v)
        if first:
            p, q = r, z
        else:
            cross = lane_value(sums_ref[0:1, :], SUM_LANE + 2 + v)
            beta = norm / lane_value(old[0:1, :], v)
            product = product + beta * (2.0 * cross + beta * lane_value(old[0:1, :], 2 + v))
            p = r + beta * state[part, :]
            q = z + beta * state[32 + 16 * v : 48 + 16 * v, :]
        step = norm / product
        x = step * p
        if not first:
            x = x + state[64 + 16 * v : 80 + 16 * v, :]
        r = r - step * q
        if last:
            for t in range(TILES):
                positions_ref[v : v + 1, LANES * t : LANES * (t + 1)] = x[t : t + 1]
                residual_ref[v : v + 1, LANES * t : LANES * (t + 1)] = r[t : t + 1]
            continue
        residual_ref[part, :] = r
        for i, new in enumerate((p, q, x)):
            state_ref[32 * i + 16 * v : 32 * i + 16 * v + 16, :] = new
        news.append([r[t : t + 1] for t in range(TILES)])
        sent_sums[v], sent_sums[2 + v] = total(r * r), total(r * q)
        line = jnp.where(lanes == v, norm, jnp.where(lanes == 2 + v, product, line))
    if last:
        return
    old_ref[...] = jnp.broadcast_to(line, (8, LANES))
    put_gathered(news, sent_sums, cut_cells, pin_cell, pin_net, send_ref, kept_ref)


VMEM, SMEM, HBM = (pl.BlockSpec(memory_space=m) for m in (pltpu.VMEM, pltpu.SMEM, pltpu.HBM))


def call(kernel, shapes, scratch, cost, args, spaces=()):
    return pl.pallas_call(
        kernel,
        out_shape=[jax.ShapeDtypeStruct(s, F32) if isinstance(s, tuple) else s for s in shapes],
        in_specs=list(spaces) + [VMEM] * (len(args) - len(spaces)),
        out_specs=[VMEM] * len(shapes),
        scratch_shapes=[pltpu.VMEM(s, F32) if isinstance(s, tuple) else s for s in scratch],
        compiler_params=pltpu.CompilerParams(vmem_limit_bytes=32 << 20),
        cost_estimate=pl.CostEstimate(flops=cost, bytes_accessed=1 << 20, transcendentals=0),
    )(*args)


def stay(x):
    return pltpu.with_memory_space_constraint(x, pltpu.HBM)


def exchange(rows, height):
    return lax.all_to_all(
        rows.reshape(LANES, 1, height * LANES), AXES, split_axis=0, concat_axis=0, tiled=True
    ).reshape(LANES * height, LANES)


def swap(x):
    return lax.ppermute(x, "coord", [(0, 1), (1, 0)])


def per_device(
    right_side, anchor, blocks, tile_nbr, cut_cells, cut_weight, pin_cell, pin_net, star_weight
):
    cut_cells, cut_weight = cut_cells[0], cut_weight[0]
    pin_cell, pin_net = pin_cell.reshape(32, LANES), pin_net.reshape(32, LANES)
    star, anchor = star_weight.reshape(LANES, LANES), anchor.reshape(TILES, LANES)
    coord = lax.axis_index("coord")
    place = jnp.stack([coord, lax.axis_index("region") * 2 + coord]).astype(I32)
    side = jnp.full((8, LANES), coord).astype(F32)
    nbr = tile_nbr.T
    send, residual, kept, cut_weight, anchor, star, nbr = call(
        first_kernel,
        [(384, LANES), (32, LANES), (256, LANES), (LANES, LANES), (TILES, LANES), (LANES, LANES),
         jax.ShapeDtypeStruct(nbr.shape, I32)],
        [
            (2, TILES * LANES),
            pltpu.VMEM((128, LANES), I32),
            pltpu.VMEM((32, LANES), I32),
            pltpu.VMEM((32, LANES), I32),
            pltpu.SemaphoreType.DMA((8,)),
        ],
        1 << 24,
        tuple(stay(x) for x in (right_side, cut_cells, pin_cell, pin_net, cut_weight, anchor, star, nbr)),
        [HBM] * 8,
    )
    hots = jax.ShapeDtypeStruct((32 * LANES, LANES), BF16)
    for iteration in range(ITERS):
        first, last = iteration == 0, iteration == ITERS - 1
        got = exchange(send, 3)
        peer = swap(residual)
        rows = 48 if first else 32
        scratch = [(256, LANES), (128, LANES), pltpu.VMEM((8, LANES), I32)]
        local_sum, back, *more = call(
            functools.partial(backward_kernel, first),
            [(rows, LANES), (rows, LANES)] + [(32, LANES), (8, LANES)] * first,
            [(128, LANES), (256, LANES), pltpu.VMEM((8, LANES), I32)],
            BACKWARD_COST,
            (residual, side, nbr, blocks) + ((place, star) if first else ()),
            [VMEM] * 4 + [SMEM] * first,
        )
        if first:
            ones, net_weight = more
        local_sum, share = call(
            functools.partial(forward_kernel, first),
            [(rows, LANES), (8, LANES)],
            scratch,
            FORWARD_COST,
            (residual, peer, side, nbr, blocks, local_sum)
            + ((ones, anchor, cut_weight, kept) if first else (degree,)),
        )
        if not first:
            net_hot = call(net_kernel, [hots], [], 1 << 28, (nets, share))[0]
        out, sums, *more = call(
            functools.partial(owner_kernel, first),
            [(128, LANES), (8, LANES)] + [(32, LANES)] * first,
            [(512 if first else 256, LANES)],
            1 << 26,
            (got, kept, cut_weight, net_weight, share) + (() if first else (net_hot,)),
        )
        if first:
            nets = more[0]
        returned = exchange(out, 1)
        back, sums = lax.optimization_barrier((back, sums))
        back = swap(back)
        args = (cut_cells, cut_weight, got, local_sum, sums, pin_cell)
        if first:
            others, cell_hot, degree = call(
                functools.partial(cut_kernel, True),
                [(32, LANES), hots, (16, LANES)],
                [(128, LANES), (96, LANES)],
                1 << 31,
                args + (pin_net, star, anchor),
            )
        else:
            others, cell_hot = call(
                functools.partial(cut_kernel, False), [(32, LANES), hots], [], 1 << 31, args
            )
        args = (pin_cell, cell_hot, returned, degree, others, back, sums, residual)
        if not first:
            args = args + (state, old)
        if last:
            shapes = [(2, TILES * LANES), (2, TILES * LANES)]
        else:
            args = args + (cut_cells, pin_net)
            shapes = [(384, LANES), (32, LANES), (96, LANES), (8, LANES), (256, LANES)]
            shapes = shapes + [(16, LANES)] * first
        results = call(
            functools.partial(step_kernel, first, last), shapes, [(128, LANES)], 1 << 26, args
        )
        if last:
            return tuple(results)
        send, residual, state, old, kept, *more = results
        if first:
            degree = more[0]


def solution(mesh):
    return jax.shard_map(
        per_device,
        mesh=mesh,
        in_specs=(
            P(None, AXES),
            P(AXES),
            P(AXES, None, None, None),
            P(AXES, None),
            P(AXES, None, None),
            P(AXES, None, None),
            P(AXES),
            P(AXES),
            P(),
        ),
        out_specs=(P(None, AXES), P(None, AXES)),
        check_vma=False,
    )
```

```python
import functools

import jax
import jax.numpy as jnp
from jax import lax
from jax.experimental import pallas as pl
from jax.experimental.pallas import tpu as pltpu
from jax.sharding import PartitionSpec as P

FANOUT = 32
BACKWARD_COST = 1 << 30
FORWARD_COST = 1 << 30
ITERS = 3
AXES = ("region", "coord")
LANES = 128
TILES = 16
F32 = jnp.float32
BF16 = jnp.bfloat16
I32 = jnp.int32
SUM_LANE = 96


def iota(shape, axis):
    return lax.broadcasted_iota(I32, shape, axis)


def split2(x):
    high = x.astype(BF16).astype(F32)
    return [high, (x - high).astype(BF16).astype(F32)]


def split3(x):
    high = x.astype(BF16).astype(F32)
    return [high] + split2(x - high)


def dot_nt(a, b):
    return lax.dot_general(a, b, (((1,), (1,)), ((), ())), preferred_element_type=F32)


def dot_nn(a, b):
    return lax.dot_general(a, b, (((1,), (0,)), ((), ())), preferred_element_type=F32)


def roll(x, shift):
    shift = shift % LANES
    return x if shift == 0 else pltpu.roll(x, shift, 1)


def total(x):
    return jnp.sum(jnp.sum(x, axis=0, keepdims=True), axis=1, keepdims=True)


def lane_value(row, lane):
    return jnp.sum(jnp.where(iota(row.shape, 1) == lane, row, 0.0), axis=1, keepdims=True)


def pick(tables, cells):
    low = cells & (LANES - 1)
    high = cells >> 7
    rows = [jnp.zeros(cells.shape, F32) for _ in tables]
    for tile in range(TILES):
        here = high == tile
        for v, table in enumerate(tables):
            wide = jnp.broadcast_to(table[tile], cells.shape)
            got = jnp.take_along_axis(wide, low, axis=1, mode="promise_in_bounds")
            rows[v] = jnp.where(here, got, rows[v])
    return rows


def one_hot(row, count):
    return jnp.where(iota((count, LANES), 0) == row, 1.0, 0.0).astype(BF16)


def add_rows(row_count, cell_row, value_rows):
    acc = None
    for j in range(0, row_count, 2):
        hots, masked = [], []
        for i in (j, j + 1):
            cells = cell_row(i)
            hots.append(one_hot(cells & (LANES - 1), LANES))
            here = iota((TILES, LANES), 0) == (cells >> 7)
            masked.append(
                jnp.concatenate([jnp.where(here, v, 0.0) for v in value_rows(i)], axis=0).astype(BF16)
            )
        part = dot_nt(jnp.concatenate(masked, axis=1), jnp.concatenate(hots, axis=1))
        acc = part if acc is None else acc + part
    return acc


def fold(acc, vectors, parts):
    size = vectors * TILES
    return sum(acc[i * size : (i + 1) * size] for i in range(parts))


def put_gathered(vectors, sums, cut_cells, pin_cell, pin_net, out_ref, kept_ref):
    lane = iota((32, LANES), 1)
    tail = jnp.zeros((1, LANES), F32)
    for i, s in enumerate(sums):
        tail = jnp.where(iota((1, LANES), 1) == SUM_LANE + i, s, tail)
    groups = [pick(vectors, pin_cell[8 * h : 8 * h + 8, :]) for h in range(4)]
    gx, gy = (jnp.concatenate([g[v] for g in groups], axis=0) for v in range(2))
    net = (pin_net[...] & (LANES - 1)).astype(F32)
    for q in range(4):
        row = jnp.where(
            lane < 32,
            roll(gx, -32 * q),
            jnp.where(
                lane < 64,
                roll(gy, 32 - 32 * q),
                jnp.where(lane < 96, roll(net, 64 - 32 * q), tail),
            ),
        )
        out_ref[pl.ds(3 * q + 2, 32, stride=12), :] = row
    for g in range(16):
        gx, gy = pick(vectors, cut_cells[pl.ds(8 * g, 8), :])
        out_ref[pl.ds(24 * g, 8, stride=3), :] = gx
        out_ref[pl.ds(24 * g + 1, 8, stride=3), :] = gy
        kept_ref[pl.ds(8 * g, 8), :] = gx
        kept_ref[pl.ds(128 + 8 * g, 8), :] = gy


def dense(rows, offset):
    lane = iota((32, LANES), 1)
    out = roll(rows[0], -offset)
    for q in range(1, 4):
        out = jnp.where(lane >= 32 * q, roll(rows[q], 32 * q - offset), out)
    return out


def first_kernel(right_hbm, cells_hbm, pin_cell_hbm, pin_net_hbm, weight_hbm, anchor_hbm, star_hbm, nbr_hbm,
                 send_ref, start_ref, kept_ref, weight_ref, anchor_ref, star_ref, nbr_ref,
                 right_ref, cut_cells, pin_cell, pin_net, sems):
    copies = [
        pltpu.make_async_copy(source, target, sems.at[i])
        for i, (source, target) in enumerate(
            (
                (right_hbm, right_ref),
                (pin_cell_hbm, pin_cell),
                (pin_net_hbm, pin_net),
                (cells_hbm, cut_cells),
                (weight_hbm, weight_ref),
                (anchor_hbm, anchor_ref),
                (star_hbm, star_ref),
                (nbr_hbm, nbr_ref),
            )
        )
    ]
    for copy in copies:
        copy.start()
    for copy in copies[:4]:
        copy.wait()
    tables = [
        [right_ref[v : v + 1, LANES * t : LANES * (t + 1)] for t in range(TILES)] for v in range(2)
    ]
    for v in range(2):
        for t in range(TILES):
            start_ref[TILES * v + t : TILES * v + t + 1, :] = tables[v][t]
    r = start_ref[...]
    sums = [total(r[16 * v : 16 * v + 16] * r[16 * v : 16 * v + 16]) for v in range(2)]
    put_gathered(tables, sums, cut_cells, pin_cell, pin_net, send_ref, kept_ref)
    for copy in copies[4:]:
        copy.wait()


def tile_names(nbr, names):
    names[...] = jnp.zeros(names.shape, I32)
    for k in range(2):
        names[k : k + 1, 0:TILES] = nbr[k : k + 1, :]
    return [jnp.where(iota((LANES, LANES), 0) == names[k : k + 1, :], 1.0, 0.0) for k in range(2)]


def block_parts(blocks, t):
    pair = jnp.concatenate([blocks[t, 0], blocks[t, 1]], axis=1)
    high = pair.astype(BF16)
    return high, (pair - high.astype(F32)).astype(BF16)


def tile_rows(ref, at, v):
    if v == 2:
        return ref[pl.ds(at + 4, 16, stride=8), :]
    return ref[pl.ds(at + v, 16, stride=8), :] + ref[pl.ds(at + v + 2, 16, stride=8), :]


def backward_kernel(first, own_ref, side, nbr, blocks, *refs):
    if first:
        star, local_ref, back_ref, ones_ref, net_weight_ref, near, got, names = refs
        mine = iota((LANES, LANES), 0) == side[0:1, :]
        weight = jnp.sum(jnp.where(mine, star[...], 0.0), axis=0, keepdims=True)
        net_weight_ref[...] = jnp.broadcast_to(weight, (8, LANES))
    else:
        local_ref, back_ref, near, got, names = refs
    spread_rows = [h[:32].astype(BF16) for h in tile_names(nbr, names)]
    near[...] = jnp.ones(near.shape, F32)
    for v in range(2):
        for i, part in enumerate(split2(own_ref[16 * v : 16 * v + 16, :])):
            near[pl.ds(2 * i + v, 16, stride=8), :] = part
    for t in range(TILES):
        a = near[8 * t : 8 * t + 8, :].astype(BF16)
        high, low = block_parts(blocks, t)
        back = dot_nn(a, high) + dot_nn(a, low)
        for k in range(2):
            got[128 * k + 8 * t : 128 * k + 8 * t + 8, :] = back[:, LANES * k : LANES * (k + 1)]
    filler = jnp.zeros((112, LANES), F32)
    upper = (side[0:1, :] & 1) == 1
    for v in range(3 if first else 2):
        spread = sum(
            dot_nn(spread_rows[k], jnp.concatenate([part, filler], axis=0).astype(BF16))
            for k in range(2)
            for part in split3(tile_rows(got, 128 * k, v))
        )
        lower, higher = spread[:16], spread[16:]
        local_ref[16 * v : 16 * v + 16, :] = jnp.where(upper, higher, lower)
        back_ref[16 * v : 16 * v + 16, :] = jnp.where(upper, lower, higher)
        if v == 2:
            ones_ref[...] = spread


def forward_kernel(first, own_ref, peer_ref, side, nbr, blocks, before_ref, *refs):
    if first:
        ones_ref, anchor, cut_weight, kept, local_ref, share_ref, far, got, names = refs
    else:
        degree, local_ref, share_ref, far, got, names = refs
    upper = (side[0:1, :] & 1) == 1
    pick_rows = jnp.concatenate([h.T[:16] for h in tile_names(nbr, names)], axis=0).astype(BF16)
    far[...] = jnp.ones(far.shape, F32)
    zeros = jnp.zeros((96, LANES), F32)
    wholes = []
    for v in range(2):
        o, p = own_ref[16 * v : 16 * v + 16, :], peer_ref[16 * v : 16 * v + 16, :]
        whole = jnp.concatenate([jnp.where(upper, p, o), jnp.where(upper, o, p)], axis=0)
        wholes.append(whole)
        for i, part in enumerate(split2(whole)):
            picked = dot_nn(pick_rows, jnp.concatenate([part, zeros], axis=0).astype(BF16))
            for k in range(2):
                far[pl.ds(128 * k + 2 * i + v, 16, stride=8), :] = picked[16 * k : 16 * k + 16]
    for t in range(TILES):
        b = jnp.concatenate(
            [far[128 * k + 8 * t : 128 * k + 8 * t + 8, :] for k in range(2)], axis=1
        ).astype(BF16)
        high, low = block_parts(blocks, t)
        got[8 * t : 8 * t + 8, :] = dot_nt(b, high) + dot_nt(b, low)
    ahead = [tile_rows(got, 0, v) for v in range(3 if first else 2)]
    for v, forward in enumerate(ahead):
        local_ref[16 * v : 16 * v + 16, :] = before_ref[16 * v : 16 * v + 16, :] + forward
    for v in range(2):
        r = own_ref[16 * v : 16 * v + 16, :]
        if first:
            square = r * (r * (anchor[...] + ahead[2]) - 2.0 * ahead[v])
            line = jnp.sum(square, axis=0, keepdims=True)
            line = line + jnp.sum(wholes[v] * wholes[v] * ones_ref[...], axis=0, keepdims=True)
            cut = kept[128 * v : 128 * v + 128, :]
            line = line + jnp.sum(cut_weight[...] * cut * cut, axis=0, keepdims=True)
        else:
            line = jnp.sum(r * (r * degree[...] - 2.0 * ahead[v]), axis=0, keepdims=True)
        share_ref[v : v + 1, :] = line
    share_ref[2:8, :] = jnp.zeros((6, LANES), F32)


def owner_kernel(first, got, kept, cut_weight, net_weight, share_ref, out_ref, sums_ref, rows):
    height = 16 if first else 8
    pin_rows = [got[pl.ds(3 * q + 2, 32, stride=12), :] for q in range(4)]
    sums = sum(jnp.sum(row, axis=0, keepdims=True) for row in pin_rows)
    sums_ref[...] = jnp.broadcast_to(sums, (8, LANES))
    nets = dense(pin_rows, 64).astype(I32)
    rows[...] = jnp.zeros(rows.shape, F32)
    for v in range(2):
        pins = dense(pin_rows, 32 * v)
        for i, part in enumerate(split3(pins)):
            rows[pl.ds(2 * i + v, 32, stride=height), :] = part
        if first:
            for i, part in enumerate(split3(pins * pins)):
                rows[pl.ds(8 + 2 * i + v, 32, stride=height), :] = part
    acc = None
    for j in range(0, 32, 2):
        hot = jnp.concatenate([one_hot(nets[i : i + 1], LANES) for i in (j, j + 1)], axis=1)
        left = jnp.concatenate(
            [rows[height * i : height * i + height, :] for i in (j, j + 1)], axis=1
        )
        part = dot_nt(left.astype(BF16), hot)
        acc = part if acc is None else acc + part
    weight = net_weight[0:1, :]
    totals = [acc[v : v + 1] + acc[v + 2 : v + 3] + acc[v + 4 : v + 5] for v in range(2)]
    centres = [weight * (1.0 / FANOUT) * t for t in totals]
    tail = jnp.zeros((1, LANES), F32)
    for v in range(2):
        line = share_ref[v : v + 1, :] - centres[v] * totals[v]
        if first:
            squares = acc[8 + v : 9 + v] + acc[10 + v : 11 + v] + acc[12 + v : 13 + v]
            line = line + weight * squares
        cut = cut_weight[...] * (kept[128 * v : 128 * v + 128, :] * got[pl.ds(v, 128, stride=3), :])
        line = line - jnp.sum(cut, axis=0, keepdims=True)
        tail = jnp.where(
            iota((1, LANES), 1) == SUM_LANE + v, jnp.sum(line, axis=1, keepdims=True), tail
        )
    lane = iota((8, LANES), 1)
    tables = [jnp.broadcast_to(c, (8, LANES)) for c in centres]
    for g in range(16):
        row = got[pl.ds(24 * g + 2, 8, stride=3), :]
        index = jnp.where(lane < 32, roll(row, -64), roll(row, -32)).astype(I32) & (LANES - 1)
        gx, gy = (
            jnp.take_along_axis(t, index, axis=1, mode="promise_in_bounds") for t in tables
        )
        out_ref[pl.ds(8 * g, 8), :] = jnp.where(
            lane < 32, gx, jnp.where(lane < 64, gy, jnp.where(lane < 96, 0.0, tail))
        )


def put_hots(hot_ref, numbers):
    columns = jnp.concatenate([numbers, numbers, numbers, numbers], axis=0).astype(F32).T
    for j in range(32):
        wide = jnp.broadcast_to(columns[:, j : j + 1], (LANES, LANES)).astype(I32)
        hot = jnp.where(iota((LANES, LANES), 1) == wide, 1.0, 0.0)
        hot_ref[LANES * j : LANES * (j + 1), :] = hot.astype(BF16)


def cut_kernel(first, cut_cells, cut_weight, got, local_ref, sums_ref, pin_cell, *refs):
    del sums_ref

    def values(j):
        weight = cut_weight[j : j + 1, :]
        parts = [split2(weight * got[3 * j + v : 3 * j + v + 1, :]) for v in range(2)]
        moved = [parts[0][0], parts[1][0], parts[0][1], parts[1][1]]
        return moved + split3(weight) if first else moved

    acc = add_rows(128, lambda j: cut_cells[j : j + 1, :], values)
    if not first:
        out_ref, cell_hot = refs
        put_hots(cell_hot, pin_cell[...] & (LANES - 1))
        out_ref[...] = fold(acc, 2, 2) + local_ref[...]
        return
    pin_net, star, anchor, out_ref, cell_hot, degree_ref, rows_ref, pins_ref = refs
    put_hots(cell_hot, pin_cell[...] & (LANES - 1))
    out_ref[...] = fold(acc[:64], 2, 2) + local_ref[0:32, :]
    net = pin_net[...] & (LANES - 1)
    for q in range(4):
        rows_ref[pl.ds(32 * q, 32), :] = jnp.take_along_axis(
            star[pl.ds(q, 32, stride=4), :], roll(net, -32 * q), axis=1, mode="promise_in_bounds"
        )
    weight = dense([rows_ref[pl.ds(32 * q, 32), :] for q in range(4)], 0)
    for i, part in enumerate(split3(weight)):
        pins_ref[pl.ds(32 * i, 32), :] = part
    pinned = add_rows(
        32,
        lambda j: pin_cell[j : j + 1, :],
        lambda j: [pins_ref[32 * i + j : 32 * i + j + 1, :] for i in range(3)],
    )
    degree_ref[...] = (
        anchor[...] + fold(acc[64:], 1, 3) + fold(pinned, 1, 3) + local_ref[32:48, :]
    )


def step_kernel(first, last, pin_cell, cell_hot, got, degree_in, others, back_ref, sums_ref, start_ref, *refs):
    refs = list(refs)
    state, old = (None, None) if first else (refs.pop(0), refs.pop(0))
    if last:
        positions_ref, residual_ref, pins = refs
    elif first:
        cut_cells, pin_net, send_ref, residual_ref, state_ref, old_ref, kept_ref, degree_ref, pins = refs
    else:
        cut_cells, pin_net, send_ref, residual_ref, state_ref, old_ref, kept_ref, pins = refs
    pin_rows = [got[pl.ds(q, 32, stride=4), :] for q in range(4)]
    energy = sum(jnp.sum(row, axis=0, keepdims=True) for row in pin_rows)
    for v in range(2):
        for i, part in enumerate(split2(dense(pin_rows, 32 * v))):
            pins[pl.ds(32 * (2 * i + v), 32), :] = part
    acc = None
    for j in range(0, 32, 2):
        masked = []
        for k in (j, j + 1):
            here = iota((TILES, LANES), 0) == (pin_cell[k : k + 1, :] >> 7)
            values = [pins[32 * i + k : 32 * i + k + 1, :] for i in range(4)]
            masked.append(jnp.concatenate([jnp.where(here, v, 0.0) for v in values], axis=0).astype(BF16))
        part = dot_nn(jnp.concatenate(masked, axis=1), cell_hot[LANES * j : LANES * (j + 2), :])
        acc = part if acc is None else acc + part
    removed = fold(acc, 2, 2) + others[...] + back_ref[0:32, :]
    degree = degree_in[...]
    if first:
        degree = degree + back_ref[32:48, :]
        degree_ref[...] = degree
    news, line = [], jnp.zeros((1, LANES), F32)
    lanes = iota((1, LANES), 1)
    sent_sums = [None] * 4
    for v in range(2):
        part = slice(16 * v, 16 * v + 16)
        r = start_ref[part, :]
        z = degree * r - removed[part]
        norm = lane_value(sums_ref[0:1, :], SUM_LANE + v)
        product = lane_value(energy, SUM_LANE + v)
        if first:
            p, q = r, z
        else:
            cross = lane_value(sums_ref[0:1, :], SUM_LANE + 2 + v)
            beta = norm / lane_value(old[0:1, :], v)
            product = product + beta * (2.0 * cross + beta * lane_value(old[0:1, :], 2 + v))
            p = r + beta * state[part, :]
            q = z + beta * state[32 + 16 * v : 48 + 16 * v, :]
        step = norm / product
        x = step * p
        if not first:
            x = x + state[64 + 16 * v : 80 + 16 * v, :]
        r = r - step * q
        if last:
            for t in range(TILES):
                positions_ref[v : v + 1, LANES * t : LANES * (t + 1)] = x[t : t + 1]
                residual_ref[v : v + 1, LANES * t : LANES * (t + 1)] = r[t : t + 1]
            continue
        residual_ref[part, :] = r
        for i, new in enumerate((p, q, x)):
            state_ref[32 * i + 16 * v : 32 * i + 16 * v + 16, :] = new
        news.append([r[t : t + 1] for t in range(TILES)])
        sent_sums[v], sent_sums[2 + v] = total(r * r), total(r * q)
        line = jnp.where(lanes == v, norm, jnp.where(lanes == 2 + v, product, line))
    if last:
        return
    old_ref[...] = jnp.broadcast_to(line, (8, LANES))
    put_gathered(news, sent_sums, cut_cells, pin_cell, pin_net, send_ref, kept_ref)


VMEM, HBM = (pl.BlockSpec(memory_space=m) for m in (pltpu.VMEM, pltpu.HBM))


def call(kernel, shapes, scratch, cost, args, spaces=()):
    return pl.pallas_call(
        kernel,
        out_shape=[jax.ShapeDtypeStruct(s, F32) if isinstance(s, tuple) else s for s in shapes],
        in_specs=list(spaces) + [VMEM] * (len(args) - len(spaces)),
        out_specs=[VMEM] * len(shapes),
        scratch_shapes=[pltpu.VMEM(s, F32) if isinstance(s, tuple) else s for s in scratch],
        compiler_params=pltpu.CompilerParams(vmem_limit_bytes=32 << 20),
        cost_estimate=pl.CostEstimate(flops=cost, bytes_accessed=1 << 20, transcendentals=0),
    )(*args)


def stay(x):
    return pltpu.with_memory_space_constraint(x, pltpu.HBM)


def exchange(rows, height):
    return lax.all_to_all(
        rows.reshape(LANES, 1, height * LANES), AXES, split_axis=0, concat_axis=0, tiled=True
    ).reshape(LANES * height, LANES)


def swap(x):
    return lax.ppermute(x, "coord", [(0, 1), (1, 0)])


def per_device(
    right_side, anchor, blocks, tile_nbr, cut_cells, cut_weight, pin_cell, pin_net, star_weight
):
    cut_cells, cut_weight = cut_cells[0], cut_weight[0]
    pin_cell, pin_net = pin_cell.reshape(32, LANES), pin_net.reshape(32, LANES)
    star, anchor = star_weight.reshape(LANES, LANES), anchor.reshape(TILES, LANES)
    number = lax.axis_index("region") * 2 + lax.axis_index("coord")
    side = jnp.full((8, LANES), number, I32)
    nbr = tile_nbr.T
    send, residual, kept, cut_weight, anchor, star, nbr = call(
        first_kernel,
        [(384, LANES), (32, LANES), (256, LANES), (LANES, LANES), (TILES, LANES), (LANES, LANES),
         jax.ShapeDtypeStruct(nbr.shape, I32)],
        [
            (2, TILES * LANES),
            pltpu.VMEM((128, LANES), I32),
            pltpu.VMEM((32, LANES), I32),
            pltpu.VMEM((32, LANES), I32),
            pltpu.SemaphoreType.DMA((8,)),
        ],
        1 << 24,
        tuple(stay(x) for x in (right_side, cut_cells, pin_cell, pin_net, cut_weight, anchor, star, nbr)),
        [HBM] * 8,
    )
    hots = jax.ShapeDtypeStruct((32 * LANES, LANES), BF16)
    for iteration in range(ITERS):
        first, last = iteration == 0, iteration == ITERS - 1
        got = exchange(send, 3)
        peer = swap(residual)
        rows = 48 if first else 32
        scratch = [(256, LANES), (128, LANES), pltpu.VMEM((8, LANES), I32)]
        local_sum, back, *more = call(
            functools.partial(backward_kernel, first),
            [(rows, LANES), (rows, LANES)] + [(32, LANES), (8, LANES)] * first,
            [(128, LANES), (256, LANES), pltpu.VMEM((8, LANES), I32)],
            BACKWARD_COST,
            (residual, side, nbr, blocks) + ((star,) if first else ()),
        )
        if first:
            ones, net_weight = more
        local_sum, share = call(
            functools.partial(forward_kernel, first),
            [(rows, LANES), (8, LANES)],
            scratch,
            FORWARD_COST,
            (residual, peer, side, nbr, blocks, local_sum)
            + ((ones, anchor, cut_weight, kept) if first else (degree,)),
        )
        out, sums = call(
            functools.partial(owner_kernel, first),
            [(128, LANES), (8, LANES)],
            [(512 if first else 256, LANES)],
            1 << 26,
            (got, kept, cut_weight, net_weight, share),
        )
        returned = exchange(out, 1)
        back, sums = lax.optimization_barrier((back, sums))
        back = swap(back)
        args = (cut_cells, cut_weight, got, local_sum, sums, pin_cell)
        if first:
            others, cell_hot, degree = call(
                functools.partial(cut_kernel, True),
                [(32, LANES), hots, (16, LANES)],
                [(128, LANES), (96, LANES)],
                1 << 31,
                args + (pin_net, star, anchor),
            )
        else:
            others, cell_hot = call(
                functools.partial(cut_kernel, False), [(32, LANES), hots], [], 1 << 31, args
            )
        args = (pin_cell, cell_hot, returned, degree, others, back, sums, residual)
        if not first:
            args = args + (state, old)
        if last:
            shapes = [(2, TILES * LANES), (2, TILES * LANES)]
        else:
            args = args + (cut_cells, pin_net)
            shapes = [(384, LANES), (32, LANES), (96, LANES), (8, LANES), (256, LANES)]
            shapes = shapes + [(16, LANES)] * first
        results = call(
            functools.partial(step_kernel, first, last), shapes, [(128, LANES)], 1 << 26, args
        )
        if last:
            return tuple(results)
        send, residual, state, old, kept, *more = results
        if first:
            degree = more[0]


def solution(mesh):
    return jax.shard_map(
        per_device,
        mesh=mesh,
        in_specs=(
            P(None, AXES),
            P(AXES),
            P(AXES, None, None, None),
            P(AXES, None),
            P(AXES, None, None),
            P(AXES, None, None),
            P(AXES),
            P(AXES),
            P(),
        ),
        out_specs=(P(None, AXES), P(None, AXES)),
        check_vma=False,
    )
```

```python
import functools

import jax
import jax.numpy as jnp
from jax import lax
from jax.experimental import pallas as pl
from jax.experimental.pallas import tpu as pltpu
from jax.sharding import PartitionSpec as P

FANOUT = 32
BACKWARD_COST = 1 << 30
FORWARD_COST = 1 << 30
ITERS = 3
AXES = ("region", "coord")
LANES = 128
TILES = 16
F32 = jnp.float32
BF16 = jnp.bfloat16
I32 = jnp.int32
SUM_LANE = 96


def iota(shape, axis):
    return lax.broadcasted_iota(I32, shape, axis)


def split2(x):
    high = x.astype(BF16).astype(F32)
    return [high, (x - high).astype(BF16).astype(F32)]


def split3(x):
    high = x.astype(BF16).astype(F32)
    return [high] + split2(x - high)


def dot_nt(a, b):
    return lax.dot_general(a, b, (((1,), (1,)), ((), ())), preferred_element_type=F32)


def dot_nn(a, b):
    return lax.dot_general(a, b, (((1,), (0,)), ((), ())), preferred_element_type=F32)


def roll(x, shift):
    shift = shift % LANES
    return x if shift == 0 else pltpu.roll(x, shift, 1)


def total(x):
    return jnp.sum(jnp.sum(x, axis=0, keepdims=True), axis=1, keepdims=True)


def lane_value(row, lane):
    return jnp.sum(jnp.where(iota(row.shape, 1) == lane, row, 0.0), axis=1, keepdims=True)


def pick(tables, cells):
    low = cells & (LANES - 1)
    high = cells >> 7
    rows = [jnp.zeros(cells.shape, F32) for _ in tables]
    for tile in range(TILES):
        here = high == tile
        for v, table in enumerate(tables):
            wide = jnp.broadcast_to(table[tile], cells.shape)
            got = jnp.take_along_axis(wide, low, axis=1, mode="promise_in_bounds")
            rows[v] = jnp.where(here, got, rows[v])
    return rows


def one_hot(row, count):
    return jnp.where(iota((count, LANES), 0) == row, 1.0, 0.0).astype(BF16)


def add_rows(row_count, cell_row, value_rows):
    acc = None
    for j in range(0, row_count, 2):
        hots, masked = [], []
        for i in (j, j + 1):
            cells = cell_row(i)
            hots.append(one_hot(cells & (LANES - 1), LANES))
            here = iota((TILES, LANES), 0) == (cells >> 7)
            masked.append(
                jnp.concatenate([jnp.where(here, v, 0.0) for v in value_rows(i)], axis=0).astype(BF16)
            )
        part = dot_nt(jnp.concatenate(masked, axis=1), jnp.concatenate(hots, axis=1))
        acc = part if acc is None else acc + part
    return acc


def fold(acc, vectors, parts):
    size = vectors * TILES
    return sum(acc[i * size : (i + 1) * size] for i in range(parts))


def put_gathered(vectors, sums, cut_cells, pin_cell, pin_net, out_ref, kept_ref):
    lane = iota((32, LANES), 1)
    tail = jnp.zeros((1, LANES), F32)
    for i, s in enumerate(sums):
        tail = jnp.where(iota((1, LANES), 1) == SUM_LANE + i, s, tail)
    groups = [pick(vectors, pin_cell[8 * h : 8 * h + 8, :]) for h in range(4)]
    gx, gy = (jnp.concatenate([g[v] for g in groups], axis=0) for v in range(2))
    if pin_net is not None:
        net = (pin_net[...] & (LANES - 1)).astype(F32)
    for q in range(4):
        more = 0.0 if pin_net is None else roll(net, 64 - 32 * q)
        row = jnp.where(
            lane < 32,
            roll(gx, -32 * q),
            jnp.where(
                lane < 64,
                roll(gy, 32 - 32 * q),
                jnp.where(lane < 96, more, tail),
            ),
        )
        out_ref[pl.ds(3 * q + 2, 32, stride=12), :] = row
    for g in range(16):
        gx, gy = pick(vectors, cut_cells[pl.ds(8 * g, 8), :])
        out_ref[pl.ds(24 * g, 8, stride=3), :] = gx
        out_ref[pl.ds(24 * g + 1, 8, stride=3), :] = gy
        kept_ref[pl.ds(8 * g, 8), :] = gx
        kept_ref[pl.ds(128 + 8 * g, 8), :] = gy


def dense(rows, offset):
    lane = iota((32, LANES), 1)
    out = roll(rows[0], -offset)
    for q in range(1, 4):
        out = jnp.where(lane >= 32 * q, roll(rows[q], 32 * q - offset), out)
    return out


def first_kernel(right_hbm, cells_hbm, pin_cell_hbm, pin_net_hbm, weight_hbm, anchor_hbm, star_hbm, nbr_hbm,
                 send_ref, start_ref, kept_ref, weight_ref, anchor_ref, star_ref, nbr_ref,
                 right_ref, cut_cells, pin_cell, pin_net, sems):
    copies = [
        pltpu.make_async_copy(source, target, sems.at[i])
        for i, (source, target) in enumerate(
            (
                (right_hbm, right_ref),
                (pin_cell_hbm, pin_cell),
                (pin_net_hbm, pin_net),
                (cells_hbm, cut_cells),
                (weight_hbm, weight_ref),
                (anchor_hbm, anchor_ref),
                (star_hbm, star_ref),
                (nbr_hbm, nbr_ref),
            )
        )
    ]
    for copy in copies:
        copy.start()
    for copy in copies[:4]:
        copy.wait()
    tables = [
        [right_ref[v : v + 1, LANES * t : LANES * (t + 1)] for t in range(TILES)] for v in range(2)
    ]
    for v in range(2):
        for t in range(TILES):
            start_ref[TILES * v + t : TILES * v + t + 1, :] = tables[v][t]
    r = start_ref[...]
    sums = [total(r[16 * v : 16 * v + 16] * r[16 * v : 16 * v + 16]) for v in range(2)]
    put_gathered(tables, sums, cut_cells, pin_cell, pin_net, send_ref, kept_ref)
    for copy in copies[4:]:
        copy.wait()


def tile_names(nbr, names):
    names[...] = jnp.zeros(names.shape, I32)
    for k in range(2):
        names[k : k + 1, 0:TILES] = nbr[k : k + 1, :]
    return [jnp.where(iota((LANES, LANES), 0) == names[k : k + 1, :], 1.0, 0.0) for k in range(2)]


def block_parts(blocks, t):
    pair = jnp.concatenate([blocks[t, 0], blocks[t, 1]], axis=1)
    high = pair.astype(BF16)
    return high, (pair - high.astype(F32)).astype(BF16)


def tile_rows(ref, at, v):
    if v == 2:
        return ref[pl.ds(at + 4, 16, stride=8), :]
    return ref[pl.ds(at + v, 16, stride=8), :] + ref[pl.ds(at + v + 2, 16, stride=8), :]


def backward_kernel(first, own_ref, side, nbr, blocks, *refs):
    if first:
        star, local_ref, back_ref, ones_ref, net_weight_ref, near, got, names = refs
        mine = iota((LANES, LANES), 0) == side[0:1, :]
        weight = jnp.sum(jnp.where(mine, star[...], 0.0), axis=0, keepdims=True)
        net_weight_ref[...] = jnp.broadcast_to(weight, (8, LANES))
    else:
        local_ref, back_ref, near, got, names = refs
    spread_rows = [h[:32].astype(BF16) for h in tile_names(nbr, names)]
    near[...] = jnp.ones(near.shape, F32)
    for v in range(2):
        for i, part in enumerate(split2(own_ref[16 * v : 16 * v + 16, :])):
            near[pl.ds(2 * i + v, 16, stride=8), :] = part
    for t in range(TILES):
        a = near[8 * t : 8 * t + 8, :].astype(BF16)
        high, low = block_parts(blocks, t)
        back = dot_nn(a, high) + dot_nn(a, low)
        for k in range(2):
            got[128 * k + 8 * t : 128 * k + 8 * t + 8, :] = back[:, LANES * k : LANES * (k + 1)]
    filler = jnp.zeros((112, LANES), F32)
    upper = (side[0:1, :] & 1) == 1
    for v in range(3 if first else 2):
        spread = sum(
            dot_nn(spread_rows[k], jnp.concatenate([part, filler], axis=0).astype(BF16))
            for k in range(2)
            for part in split3(tile_rows(got, 128 * k, v))
        )
        lower, higher = spread[:16], spread[16:]
        local_ref[16 * v : 16 * v + 16, :] = jnp.where(upper, higher, lower)
        back_ref[16 * v : 16 * v + 16, :] = jnp.where(upper, lower, higher)
        if v == 2:
            ones_ref[...] = spread


def forward_kernel(first, own_ref, peer_ref, side, nbr, blocks, before_ref, *refs):
    if first:
        ones_ref, anchor, cut_weight, kept, local_ref, share_ref, far, got, names = refs
    else:
        degree, local_ref, share_ref, far, got, names = refs
    upper = (side[0:1, :] & 1) == 1
    pick_rows = jnp.concatenate([h.T[:16] for h in tile_names(nbr, names)], axis=0).astype(BF16)
    far[...] = jnp.ones(far.shape, F32)
    zeros = jnp.zeros((96, LANES), F32)
    wholes = []
    for v in range(2):
        o, p = own_ref[16 * v : 16 * v + 16, :], peer_ref[16 * v : 16 * v + 16, :]
        whole = jnp.concatenate([jnp.where(upper, p, o), jnp.where(upper, o, p)], axis=0)
        wholes.append(whole)
        for i, part in enumerate(split2(whole)):
            picked = dot_nn(pick_rows, jnp.concatenate([part, zeros], axis=0).astype(BF16))
            for k in range(2):
                far[pl.ds(128 * k + 2 * i + v, 16, stride=8), :] = picked[16 * k : 16 * k + 16]
    for t in range(TILES):
        b = jnp.concatenate(
            [far[128 * k + 8 * t : 128 * k + 8 * t + 8, :] for k in range(2)], axis=1
        ).astype(BF16)
        high, low = block_parts(blocks, t)
        got[8 * t : 8 * t + 8, :] = dot_nt(b, high) + dot_nt(b, low)
    ahead = [tile_rows(got, 0, v) for v in range(3 if first else 2)]
    for v, forward in enumerate(ahead):
        local_ref[16 * v : 16 * v + 16, :] = before_ref[16 * v : 16 * v + 16, :] + forward
    for v in range(2):
        r = own_ref[16 * v : 16 * v + 16, :]
        if first:
            square = r * (r * (anchor[...] + ahead[2]) - 2.0 * ahead[v])
            line = jnp.sum(square, axis=0, keepdims=True)
            line = line + jnp.sum(wholes[v] * wholes[v] * ones_ref[...], axis=0, keepdims=True)
            cut = kept[128 * v : 128 * v + 128, :]
            line = line + jnp.sum(cut_weight[...] * cut * cut, axis=0, keepdims=True)
        else:
            line = jnp.sum(r * (r * degree[...] - 2.0 * ahead[v]), axis=0, keepdims=True)
        share_ref[v : v + 1, :] = line
    share_ref[2:8, :] = jnp.zeros((6, LANES), F32)


def owner_kernel(first, got, kept, cut_weight, net_weight, share_ref, *refs):
    if first:
        out_ref, sums_ref, nets_ref, index_ref, rows = refs
    else:
        nets_ref, index_ref, out_ref, sums_ref, rows = refs
    height = 16 if first else 8
    pin_rows = [got[pl.ds(3 * q + 2, 32, stride=12), :] for q in range(4)]
    sums = sum(jnp.sum(row, axis=0, keepdims=True) for row in pin_rows)
    sums_ref[...] = jnp.broadcast_to(sums, (8, LANES))
    if first:
        nets_ref[...] = dense(pin_rows, 64).astype(I32)
    nets = nets_ref[...]
    rows[...] = jnp.zeros(rows.shape, F32)
    for v in range(2):
        pins = dense(pin_rows, 32 * v)
        for i, part in enumerate(split3(pins)):
            rows[pl.ds(2 * i + v, 32, stride=height), :] = part
        if first:
            for i, part in enumerate(split3(pins * pins)):
                rows[pl.ds(8 + 2 * i + v, 32, stride=height), :] = part
    acc = None
    for j in range(0, 32, 2):
        hot = jnp.concatenate([one_hot(nets[i : i + 1], LANES) for i in (j, j + 1)], axis=1)
        left = jnp.concatenate(
            [rows[height * i : height * i + height, :] for i in (j, j + 1)], axis=1
        )
        part = dot_nt(left.astype(BF16), hot)
        acc = part if acc is None else acc + part
    weight = net_weight[0:1, :]
    totals = [acc[v : v + 1] + acc[v + 2 : v + 3] + acc[v + 4 : v + 5] for v in range(2)]
    centres = [weight * (1.0 / FANOUT) * t for t in totals]
    tail = jnp.zeros((1, LANES), F32)
    for v in range(2):
        line = share_ref[v : v + 1, :] - centres[v] * totals[v]
        if first:
            squares = acc[8 + v : 9 + v] + acc[10 + v : 11 + v] + acc[12 + v : 13 + v]
            line = line + weight * squares
        cut = cut_weight[...] * (kept[128 * v : 128 * v + 128, :] * got[pl.ds(v, 128, stride=3), :])
        line = line - jnp.sum(cut, axis=0, keepdims=True)
        tail = jnp.where(
            iota((1, LANES), 1) == SUM_LANE + v, jnp.sum(line, axis=1, keepdims=True), tail
        )
    lane = iota((8, LANES), 1)
    tables = [jnp.broadcast_to(c, (8, LANES)) for c in centres]
    for g in range(16):
        if first:
            row = got[pl.ds(24 * g + 2, 8, stride=3), :]
            index = jnp.where(lane < 32, roll(row, -64), roll(row, -32)).astype(I32) & (LANES - 1)
            index_ref[pl.ds(8 * g, 8), :] = index
        else:
            index = index_ref[pl.ds(8 * g, 8), :]
        gx, gy = (
            jnp.take_along_axis(t, index, axis=1, mode="promise_in_bounds") for t in tables
        )
        out_ref[pl.ds(8 * g, 8), :] = jnp.where(
            lane < 32, gx, jnp.where(lane < 64, gy, jnp.where(lane < 96, 0.0, tail))
        )


def put_hots(hot_ref, numbers):
    columns = jnp.concatenate([numbers, numbers, numbers, numbers], axis=0).astype(F32).T
    for j in range(32):
        wide = jnp.broadcast_to(columns[:, j : j + 1], (LANES, LANES)).astype(I32)
        hot = jnp.where(iota((LANES, LANES), 1) == wide, 1.0, 0.0)
        hot_ref[LANES * j : LANES * (j + 1), :] = hot.astype(BF16)


def cut_kernel(first, cut_cells, cut_weight, got, local_ref, sums_ref, pin_cell, *refs):
    del sums_ref

    def values(j):
        weight = cut_weight[j : j + 1, :]
        parts = [split2(weight * got[3 * j + v : 3 * j + v + 1, :]) for v in range(2)]
        moved = [parts[0][0], parts[1][0], parts[0][1], parts[1][1]]
        return moved + split3(weight) if first else moved

    acc = add_rows(128, lambda j: cut_cells[j : j + 1, :], values)
    if not first:
        out_ref, cell_hot = refs
        put_hots(cell_hot, pin_cell[...] & (LANES - 1))
        out_ref[...] = fold(acc, 2, 2) + local_ref[...]
        return
    pin_net, star, anchor, out_ref, cell_hot, degree_ref, rows_ref, pins_ref = refs
    put_hots(cell_hot, pin_cell[...] & (LANES - 1))
    out_ref[...] = fold(acc[:64], 2, 2) + local_ref[0:32, :]
    net = pin_net[...] & (LANES - 1)
    for q in range(4):
        rows_ref[pl.ds(32 * q, 32), :] = jnp.take_along_axis(
            star[pl.ds(q, 32, stride=4), :], roll(net, -32 * q), axis=1, mode="promise_in_bounds"
        )
    weight = dense([rows_ref[pl.ds(32 * q, 32), :] for q in range(4)], 0)
    for i, part in enumerate(split3(weight)):
        pins_ref[pl.ds(32 * i, 32), :] = part
    pinned = add_rows(
        32,
        lambda j: pin_cell[j : j + 1, :],
        lambda j: [pins_ref[32 * i + j : 32 * i + j + 1, :] for i in range(3)],
    )
    degree_ref[...] = (
        anchor[...] + fold(acc[64:], 1, 3) + fold(pinned, 1, 3) + local_ref[32:48, :]
    )


def step_kernel(first, last, pin_cell, cell_hot, got, degree_in, others, back_ref, sums_ref, start_ref, *refs):
    refs = list(refs)
    state, old = (None, None) if first else (refs.pop(0), refs.pop(0))
    if last:
        positions_ref, residual_ref, pins = refs
    elif first:
        cut_cells, send_ref, residual_ref, state_ref, old_ref, kept_ref, degree_ref, pins = refs
    else:
        cut_cells, send_ref, residual_ref, state_ref, old_ref, kept_ref, pins = refs
    pin_rows = [got[pl.ds(q, 32, stride=4), :] for q in range(4)]
    energy = sum(jnp.sum(row, axis=0, keepdims=True) for row in pin_rows)
    for v in range(2):
        for i, part in enumerate(split2(dense(pin_rows, 32 * v))):
            pins[pl.ds(32 * (2 * i + v), 32), :] = part
    acc = None
    for j in range(0, 32, 2):
        masked = []
        for k in (j, j + 1):
            here = iota((TILES, LANES), 0) == (pin_cell[k : k + 1, :] >> 7)
            values = [pins[32 * i + k : 32 * i + k + 1, :] for i in range(4)]
            masked.append(jnp.concatenate([jnp.where(here, v, 0.0) for v in values], axis=0).astype(BF16))
        part = dot_nn(jnp.concatenate(masked, axis=1), cell_hot[LANES * j : LANES * (j + 2), :])
        acc = part if acc is None else acc + part
    removed = fold(acc, 2, 2) + others[...] + back_ref[0:32, :]
    degree = degree_in[...]
    if first:
        degree = degree + back_ref[32:48, :]
        degree_ref[...] = degree
    news, line = [], jnp.zeros((1, LANES), F32)
    lanes = iota((1, LANES), 1)
    sent_sums = [None] * 4
    for v in range(2):
        part = slice(16 * v, 16 * v + 16)
        r = start_ref[part, :]
        z = degree * r - removed[part]
        norm = lane_value(sums_ref[0:1, :], SUM_LANE + v)
        product = lane_value(energy, SUM_LANE + v)
        if first:
            p, q = r, z
        else:
            cross = lane_value(sums_ref[0:1, :], SUM_LANE + 2 + v)
            beta = norm / lane_value(old[0:1, :], v)
            product = product + beta * (2.0 * cross + beta * lane_value(old[0:1, :], 2 + v))
            p = r + beta * state[part, :]
            q = z + beta * state[32 + 16 * v : 48 + 16 * v, :]
        step = norm / product
        x = step * p
        if not first:
            x = x + state[64 + 16 * v : 80 + 16 * v, :]
        r = r - step * q
        if last:
            for t in range(TILES):
                positions_ref[v : v + 1, LANES * t : LANES * (t + 1)] = x[t : t + 1]
                residual_ref[v : v + 1, LANES * t : LANES * (t + 1)] = r[t : t + 1]
            continue
        residual_ref[part, :] = r
        for i, new in enumerate((p, q, x)):
            state_ref[32 * i + 16 * v : 32 * i + 16 * v + 16, :] = new
        news.append([r[t : t + 1] for t in range(TILES)])
        sent_sums[v], sent_sums[2 + v] = total(r * r), total(r * q)
        line = jnp.where(lanes == v, norm, jnp.where(lanes == 2 + v, product, line))
    if last:
        return
    old_ref[...] = jnp.broadcast_to(line, (8, LANES))
    put_gathered(news, sent_sums, cut_cells, pin_cell, None, send_ref, kept_ref)


VMEM, HBM = (pl.BlockSpec(memory_space=m) for m in (pltpu.VMEM, pltpu.HBM))


def call(kernel, shapes, scratch, cost, args, spaces=()):
    return pl.pallas_call(
        kernel,
        out_shape=[jax.ShapeDtypeStruct(s, F32) if isinstance(s, tuple) else s for s in shapes],
        in_specs=list(spaces) + [VMEM] * (len(args) - len(spaces)),
        out_specs=[VMEM] * len(shapes),
        scratch_shapes=[pltpu.VMEM(s, F32) if isinstance(s, tuple) else s for s in scratch],
        compiler_params=pltpu.CompilerParams(vmem_limit_bytes=32 << 20),
        cost_estimate=pl.CostEstimate(flops=cost, bytes_accessed=1 << 20, transcendentals=0),
    )(*args)


def stay(x):
    return pltpu.with_memory_space_constraint(x, pltpu.HBM)


def exchange(rows, height):
    return lax.all_to_all(
        rows.reshape(LANES, 1, height * LANES), AXES, split_axis=0, concat_axis=0, tiled=True
    ).reshape(LANES * height, LANES)


def swap(x):
    return lax.ppermute(x, "coord", [(0, 1), (1, 0)])


def per_device(
    right_side, anchor, blocks, tile_nbr, cut_cells, cut_weight, pin_cell, pin_net, star_weight
):
    cut_cells, cut_weight = cut_cells[0], cut_weight[0]
    pin_cell, pin_net = pin_cell.reshape(32, LANES), pin_net.reshape(32, LANES)
    star, anchor = star_weight.reshape(LANES, LANES), anchor.reshape(TILES, LANES)
    number = lax.axis_index("region") * 2 + lax.axis_index("coord")
    side = jnp.full((8, LANES), number, I32)
    nbr = tile_nbr.T
    send, residual, kept, cut_weight, anchor, star, nbr = call(
        first_kernel,
        [(384, LANES), (32, LANES), (256, LANES), (LANES, LANES), (TILES, LANES), (LANES, LANES),
         jax.ShapeDtypeStruct(nbr.shape, I32)],
        [
            (2, TILES * LANES),
            pltpu.VMEM((128, LANES), I32),
            pltpu.VMEM((32, LANES), I32),
            pltpu.VMEM((32, LANES), I32),
            pltpu.SemaphoreType.DMA((8,)),
        ],
        1 << 24,
        tuple(stay(x) for x in (right_side, cut_cells, pin_cell, pin_net, cut_weight, anchor, star, nbr)),
        [HBM] * 8,
    )
    hots = jax.ShapeDtypeStruct((32 * LANES, LANES), BF16)
    numbers = [jax.ShapeDtypeStruct((n, LANES), I32) for n in (32, LANES)]
    for iteration in range(ITERS):
        first, last = iteration == 0, iteration == ITERS - 1
        got = exchange(send, 3)
        peer = swap(residual)
        rows = 48 if first else 32
        scratch = [(256, LANES), (128, LANES), pltpu.VMEM((8, LANES), I32)]
        local_sum, back, *more = call(
            functools.partial(backward_kernel, first),
            [(rows, LANES), (rows, LANES)] + [(32, LANES), (8, LANES)] * first,
            [(128, LANES), (256, LANES), pltpu.VMEM((8, LANES), I32)],
            BACKWARD_COST,
            (residual, side, nbr, blocks) + ((star,) if first else ()),
        )
        if first:
            ones, net_weight = more
        local_sum, share = call(
            functools.partial(forward_kernel, first),
            [(rows, LANES), (8, LANES)],
            scratch,
            FORWARD_COST,
            (residual, peer, side, nbr, blocks, local_sum)
            + ((ones, anchor, cut_weight, kept) if first else (degree,)),
        )
        out, sums, *more = call(
            functools.partial(owner_kernel, first),
            [(128, LANES), (8, LANES)] + numbers * first,
            [(512 if first else 256, LANES)],
            1 << 26,
            (got, kept, cut_weight, net_weight, share) + (() if first else (nets, index)),
        )
        if first:
            nets, index = more
        returned = exchange(out, 1)
        back, sums = lax.optimization_barrier((back, sums))
        back = swap(back)
        args = (cut_cells, cut_weight, got, local_sum, sums, pin_cell)
        if first:
            others, cell_hot, degree = call(
                functools.partial(cut_kernel, True),
                [(32, LANES), hots, (16, LANES)],
                [(128, LANES), (96, LANES)],
                1 << 31,
                args + (pin_net, star, anchor),
            )
        else:
            others, cell_hot = call(
                functools.partial(cut_kernel, False), [(32, LANES), hots], [], 1 << 31, args
            )
        args = (pin_cell, cell_hot, returned, degree, others, back, sums, residual)
        if not first:
            args = args + (state, old)
        if last:
            shapes = [(2, TILES * LANES), (2, TILES * LANES)]
        else:
            args = args + (cut_cells,)
            shapes = [(384, LANES), (32, LANES), (96, LANES), (8, LANES), (256, LANES)]
            shapes = shapes + [(16, LANES)] * first
        results = call(
            functools.partial(step_kernel, first, last), shapes, [(128, LANES)], 1 << 26, args
        )
        if last:
            return tuple(results)
        send, residual, state, old, kept, *more = results
        if first:
            degree = more[0]


def solution(mesh):
    return jax.shard_map(
        per_device,
        mesh=mesh,
        in_specs=(
            P(None, AXES),
            P(AXES),
            P(AXES, None, None, None),
            P(AXES, None),
            P(AXES, None, None),
            P(AXES, None, None),
            P(AXES),
            P(AXES),
            P(),
        ),
        out_specs=(P(None, AXES), P(None, AXES)),
        check_vma=False,
    )
```
